128 devices in a mesh: rep: 4 (over z_lo, core), shard: 32 (over x, y, z_hi).
Axes of the slice: x: 4, y: 4, z: 4 (z_hi: 2, z_lo: 2; z = z_hi * 2 + z_lo), core: 2. Of those that a mesh axis runs over, the one named last changes fastest.
Arguments:
- tokens: bfloat16 [4, 4096, 2048], P('rep', 'shard'), may hold values from -6 to 6
- span_order: int32 [4, 32], P('rep'), may hold values from 0 to 31, each once within a row
- ln_gain: bfloat16 [2048], P('shard'), may hold values from 0.5 to 1.5
- ln_bias: bfloat16 [2048], P('shard'), may hold values from -3 to 3
- qkv_weight: bfloat16 [2048, 6144], P('shard'), may hold values from -0.125 to 0.125
- qkv_bias: bfloat16 [6144], P('shard'), may hold values from -3 to 3
- out_weight: bfloat16 [2048, 2048], P('shard'), may hold values from -2 to 2
- out_bias: bfloat16 [2048], P('shard'), may hold values from -2 to 2
- fc1_weight: bfloat16 [2048, 8192], P('shard'), may hold values from -0.125 to 0.125
- fc1_bias: bfloat16 [8192], P('shard'), may hold values from -3 to 3
- fc2_weight: bfloat16 [8192, 2048], P('shard'), may hold values from -0.0625 to 0.0625
- fc2_bias: bfloat16 [2048], P('shard'), may hold values from -2 to 2
- cotangent: bfloat16 [4, 4096, 2048], P('rep', 'shard'), may hold values from -6 to 6
Outputs:
- block_out: bfloat16 [4, 4096, 2048], P('rep', 'shard')
- d_tokens: bfloat16 [4, 4096, 2048], P('rep', 'shard')
- g_ln_gain: float32 [2048], P('shard')
- g_ln_bias: float32 [2048], P('shard')
- g_qkv_weight: float32 [2048, 6144], P('shard')
- g_qkv_bias: float32 [6144], P('shard')
- g_out_weight: float32 [2048, 2048], P('shard')
- g_out_bias: float32 [2048], P('shard')
- g_fc1_weight: float32 [2048, 8192], P('shard')
- g_fc1_bias: float32 [8192], P('shard')
- g_fc2_weight: float32 [8192, 2048], P('shard')
- g_fc2_bias: float32 [2048], P('shard')
The draws below stay inside these ranges and needn't reach their ends.
Inputs may be any that keep to these rules, and one draw needn't show every extreme that they name: Each row of span_order holds every number from 0 to 31 once.
All inputs are finite; a program needn't handle non-finite values.
Results may differ from the reference program's by a relative error of at most 0.03.
Values may be sent and summed in bfloat16 or wider, within the bound.
A program may use at most 768 MiB of HBM per device.

```python
import jax
import jax.numpy as jnp
from jax import lax

D = 2048
HEADS = 32
HEAD_DIM = 64
ROT = 32
FF = 8192
SPAN = 128
SEQUENCES = 4
LENGTH = 4096
N_SHARD = 32


def block_levels(stream_key, shape, pieces, low, largest):
    loudness = 1.0
    for dim, blocks in pieces:
        draws = jax.random.uniform(jax.random.fold_in(jax.random.fold_in(stream_key, 6), dim), (blocks,), jnp.float32, low / len(pieces), largest / len(pieces))
        loudness = loudness * jnp.repeat(jnp.exp(draws), shape[dim] // blocks).reshape((-1,) + (1,) * (len(shape) - 1 - dim))
    return loudness


def normal_values(own_key, shape, spread, limit, pieces=(), kind=jnp.bfloat16):
    entries = spread * jax.random.normal(own_key, shape, jnp.float32)
    if pieces:
        entries = entries * block_levels(own_key, shape, pieces, -0.22, 0.18)
    return jnp.clip(entries, -limit, limit).astype(kind)


def setup_inputs(seed: int = 0) -> dict:
    arg_keys = jax.random.split(jax.random.key(seed), 14)
    return {
        "tokens": normal_values(arg_keys[0], (SEQUENCES, LENGTH, D), 1.0, 6.0, ((0, 4), (1, 32))),
        "span_order": jax.vmap(lambda own: jax.random.permutation(own, N_SHARD))(jax.random.split(arg_keys[1], SEQUENCES)).reshape((SEQUENCES, N_SHARD)).astype(jnp.int32),
        "ln_gain": jnp.clip(1.0 + 0.1 * jax.random.normal(arg_keys[2], (D,), jnp.float32), 0.5, 1.5).astype(jnp.bfloat16),
        "ln_bias": normal_values(arg_keys[3], (D,), 0.5, 3.0, ((0, 32),)),
        "qkv_weight": normal_values(arg_keys[4], (D, 3 * D), D ** -0.5, 0.125, ((0, 32),)),
        "qkv_bias": normal_values(arg_keys[5], (3 * D,), 0.5, 3.0, ((0, 32),)),
        "out_weight": normal_values(arg_keys[6], (D, D), (D * 16 // LENGTH) ** -0.5, 2.0, ((0, 32),)),
        "out_bias": normal_values(arg_keys[7], (D,), 0.3, 2.0, ((0, 32),)),
        "fc1_weight": normal_values(arg_keys[8], (D, FF), D ** -0.5, 0.125, ((0, 32),)),
        "fc1_bias": normal_values(arg_keys[9], (FF,), 0.5, 3.0, ((0, 32),)),
        "fc2_weight": normal_values(arg_keys[10], (FF, D), FF ** -0.5, 0.0625, ((0, 32),)),
        "fc2_bias": normal_values(arg_keys[11], (D,), 0.3, 2.0, ((0, 32),)),
        "cotangent": normal_values(arg_keys[12], (SEQUENCES, LENGTH, D), 1.0, 6.0, ((0, 4), (1, 32))),
    }


@jax.custom_vjp
def low(v):
    return lax.optimization_barrier(v.astype(jnp.bfloat16)).astype(jnp.float32)

@jax.custom_vjp
def low_back(v):
    return v

def low_keep(v):
    return (low(v), None)

def low_pass(kept, grad):
    return (grad,)

def back_keep(v):
    return (v, None)

def back_low(kept, grad):
    return (low(grad),)
low.defvjp(low_keep, low_pass)
low_back.defvjp(back_keep, back_low)
HIGH = lax.Precision.HIGHEST
eps_norm = 1e-05
rope_base = 10000.0
negative = -1e+30

def rotate(field, positions):
    half = ROT // 2
    freq = rope_base ** (-(jnp.arange(half, dtype=jnp.float32) * 2.0 / ROT))
    angle = positions.astype(jnp.float32)[:, None] * freq[None, :]
    cosine = jnp.cos(angle)[:, None, :]
    sine = jnp.sin(angle)[:, None, :]
    first = field[..., :half]
    second = field[..., half:ROT]
    rest = field[..., ROT:]
    return jnp.concatenate([first * cosine - second * sine, second * cosine + first * sine, rest], axis=-1)

def attend(queries, keys, values, positions):
    length = queries.shape[0]
    block = 512 if length % 512 == 0 else length
    q_blocks = queries.reshape(length // block, block, HEADS, HEAD_DIM)
    p_blocks = positions.reshape(length // block, block)

    def one_block(item):
        q_rows, q_pos = item
        scores = low_back(jnp.einsum('qhd,khd->hqk', q_rows, keys, precision=HIGH))
        allowed = positions[None, None, :] <= q_pos[None, :, None]
        scores = jnp.where(allowed, scores, negative)
        top = lax.optimization_barrier(jnp.max(scores, axis=-1, keepdims=True))
        expo = jnp.exp(scores - top)
        probs = low(expo / lax.optimization_barrier(jnp.sum(expo, axis=-1, keepdims=True)))
        return jnp.einsum('hqk,khd->qhd', probs, values, precision=HIGH)
    result = lax.map(jax.checkpoint(one_block), (q_blocks, p_blocks))
    return result.reshape(length, HEADS, HEAD_DIM)

def forward(tokens, params, positions):
    gain, shift, w_qkv, b_qkv, w_out, b_out, w_in, b_in, w_back, b_back = params
    length = tokens.shape[0]
    mean = lax.optimization_barrier(jnp.mean(tokens, axis=-1, keepdims=True))
    centred = tokens - mean
    var = lax.optimization_barrier(jnp.mean(centred * centred, axis=-1, keepdims=True))
    normed = low(centred * lax.rsqrt(var + eps_norm) * gain + shift)
    mixed = low_back(jnp.dot(normed, w_qkv, precision=HIGH) + b_qkv).reshape(length, 3, HEADS, HEAD_DIM)
    queries = low(rotate(mixed[:, 0], positions) * HEAD_DIM ** (-0.5))
    keys = low(rotate(mixed[:, 1], positions))
    values = low(mixed[:, 2])
    attended = low(low_back(attend(queries, keys, values, positions).reshape(length, D)))
    branch_attn = jnp.dot(attended, w_out, precision=HIGH) + b_out
    hidden = low_back(jnp.dot(normed, w_in, precision=HIGH) + b_in)
    active = low(jax.nn.gelu(hidden, approximate=True))
    branch_mlp = jnp.dot(active, w_back, precision=HIGH) + b_back
    return tokens + branch_attn + branch_mlp

def reference(tokens, span_order, ln_gain, ln_bias, qkv_weight, qkv_bias, out_weight, out_bias, fc1_weight, fc1_bias, fc2_weight, fc2_bias, cotangent):
    params = tuple((p.astype(jnp.float32) for p in (ln_gain, ln_bias, qkv_weight, qkv_bias, out_weight, out_bias, fc1_weight, fc1_bias, fc2_weight, fc2_bias)))

    def one(totals, item):
        sequence, order, grad_out = item
        positions = (order[:, None] * SPAN + jnp.arange(SPAN, dtype=jnp.int32)[None, :]).reshape(-1).astype(jnp.int32)

        def run(inputs, weights):
            return forward(inputs, weights, positions)
        result, pull = jax.vjp(run, sequence.astype(jnp.float32), params)
        d_input, d_params = pull(grad_out.astype(jnp.float32))
        totals = jax.tree.map(lambda a, b: a + b, totals, d_params)
        return (totals, (result.astype(jnp.bfloat16), d_input.astype(jnp.bfloat16)))
    zeros = tuple((jnp.zeros(p.shape, jnp.float32) for p in params))
    totals, (outputs, d_inputs) = lax.scan(one, zeros, (tokens, span_order, cotangent))
    return (outputs, d_inputs, totals[0], totals[1], totals[2], totals[3], totals[4], totals[5], totals[6], totals[7], totals[8], totals[9])
```

```python
import jax
import jax.numpy as jnp
from jax import lax
from jax.experimental import pallas as pl
from jax.experimental.pallas import tpu as pltpu
from jax.sharding import PartitionSpec as P

F32 = jnp.float32
BF = jnp.bfloat16
MESH = pl.DeviceIdType.MESH
HEADS = 32
WIDTH = 2048
LENGTH = 4096
TILE = 512
eps_norm = 1e-05
rope_base = 10000.0
negative = -1e30
VM = pl.BlockSpec(memory_space=pltpu.VMEM)
ANY = pl.BlockSpec(memory_space=pl.ANY)


def place():
    rep = lax.axis_index("rep")
    sh = lax.axis_index("shard")
    return sh // 8, (sh // 2) % 4, sh % 2, rep // 2, rep % 2


def spot(x, y, zh, zl, c):
    return (zl * 2 + c, (x * 4 + y) * 2 + zh)


def remote(src, dst, send, recv, to):
    return pltpu.make_async_remote_copy(
        src_ref=src, dst_ref=dst, send_sem=send, recv_sem=recv, device_id=to, device_id_type=MESH
    )


def greet(peers):
    barrier = pltpu.get_barrier_semaphore()
    for d in peers:
        pl.semaphore_signal(barrier, inc=1, device_id=d, device_id_type=MESH)
    pl.semaphore_wait(barrier, len(peers))


OFFS = [(p, q) for p in (0, -1, 1, 2) for q in (0, -1, 1, 2)]
GROUP = {0: 0, -1: 1, 1: 2, 2: 3}


def gather_kernel(n_arr, *refs):
    ins = refs[:n_arr]
    outs = refs[n_arr : 2 * n_arr]
    send, recv, psend, precv, loc = refs[2 * n_arr :]
    x, y, zh, zl, c = place()
    other = spot(x, y, zh, zl, 1 - c)

    def dev(half, da, db):
        dx, dy = (da, db) if half == 0 else (db, da)
        return spot((x + dx + 4) % 4, (y + dy + 4) % 4, zh, zl, c)

    def slot(half, da, db, core):
        dx, dy = (da, db) if half == 0 else (db, da)
        return (((x + dx + 4) % 4) * 4 + (y + dy + 4) % 4) * 2 + core

    def rows(half, part):
        return pl.ds(half * 64 + (32 if part == 2 else 0), 64 if part == 0 else 32)

    greet([dev(0, 1, 0), dev(0, -1, 0), dev(0, 0, 1), dev(0, 0, -1), other])
    started = []
    shared = []

    def go(cp):
        cp.start()
        started.append(cp)

    def pass_on(a, h, role, off, part, to, own=False):
        s, r = slot(h, *off, c), rows(h, part)
        src = ins[a].at[r] if own else outs[a].at[s, r]
        go(remote(src, outs[a].at[s, r], send.at[a, h, role], recv.at[a, h, role], dev(h, *to)))

    def arrived(a, h, role, off, part):
        ref = outs[a].at[slot(h, *off, c), rows(h, part)]
        remote(ref, ref, send.at[a, h, role], recv.at[a, h, role], other).wait_recv()

    def share(a, h, off, own=False):
        i = OFFS.index(off)
        s, r = slot(h, *off, c), rows(h, 0)
        src = ins[a].at[r] if own else outs[a].at[s, r]
        go(remote(src, outs[a].at[s, r], psend.at[a, h, i], precv.at[a, h, i], other))
        shared.append((a, h, off, i))

    def second(a, h, ao, own=False):
        k = GROUP[ao]
        pass_on(a, h, 4 + 2 * k, (ao, 0), 0, (0, 1), own)
        pass_on(a, h, 5 + 2 * k, (ao, 0), 0, (0, -1), own)

    def near(a, h, ao):
        k = GROUP[ao]
        arrived(a, h, 4 + 2 * k, (ao, -1), 0)
        pass_on(a, h, 12 + 2 * k, (ao, -1), 1, (0, 1))
        share(a, h, (ao, -1))
        arrived(a, h, 5 + 2 * k, (ao, 1), 0)
        pass_on(a, h, 13 + 2 * k, (ao, 1), 2, (0, -1))
        share(a, h, (ao, 1))

    def far(a, h, ao):
        k = GROUP[ao]
        arrived(a, h, 12 + 2 * k, (ao, 2), 1)
        arrived(a, h, 13 + 2 * k, (ao, 2), 2)
        share(a, h, (ao, 2))

    local = []
    for a in range(n_arr):
        cp = pltpu.make_async_copy(ins[a], outs[a].at[slot(0, 0, 0, c)], loc.at[a])
        cp.start()
        local.append(cp)
    both = [(a, h) for a in range(n_arr) for h in (0, 1)]
    for a, h in both:
        pass_on(a, h, 0, (0, 0), 0, (1, 0), True)
        pass_on(a, h, 1, (0, 0), 0, (-1, 0), True)
    for a, h in both:
        second(a, h, 0, True)
        share(a, h, (0, 0), True)
    for a in range(n_arr):
        for h in (0, 1):
            arrived(a, h, 0, (-1, 0), 0)
            pass_on(a, h, 2, (-1, 0), 1, (1, 0))
            second(a, h, -1)
            share(a, h, (-1, 0))
            arrived(a, h, 1, (1, 0), 0)
            pass_on(a, h, 3, (1, 0), 2, (-1, 0))
            second(a, h, 1)
            share(a, h, (1, 0))
        for h in (0, 1):
            near(a, h, 0)
        for h in (0, 1):
            arrived(a, h, 2, (2, 0), 1)
            arrived(a, h, 3, (2, 0), 2)
            second(a, h, 2)
            share(a, h, (2, 0))
        for h in (0, 1):
            near(a, h, -1)
        for h in (0, 1):
            far(a, h, 0)
        for h in (0, 1):
            near(a, h, 1)
        for h in (0, 1):
            far(a, h, -1)
        for h in (0, 1):
            near(a, h, 2)
        for ao in (1, 2):
            for h in (0, 1):
                far(a, h, ao)
    for a, h, off, i in shared:
        ref = outs[a].at[slot(h, *off, 1 - c), rows(h, 0)]
        remote(ref, ref, psend.at[a, h, i], precv.at[a, h, i], other).wait_recv()
    for cp in started:
        cp.wait_send()
    for cp in local:
        cp.wait()


def gather(*arrs):
    n = len(arrs)
    dma = pltpu.SemaphoreType.DMA
    return pl.pallas_call(
        lambda *refs: gather_kernel(n, *refs),
        out_shape=[jax.ShapeDtypeStruct((32,) + a.shape, a.dtype) for a in arrs],
        in_specs=[ANY] * n,
        out_specs=[ANY] * n,
        scratch_shapes=[dma((n, 2, 20)), dma((n, 2, 20)), dma((n, 2, 16)), dma((n, 2, 16)), dma((n,))],
        compiler_params=pltpu.CompilerParams(collective_id=1, has_side_effects=True),
    )(*arrs)


def dot(a, b):
    return jnp.dot(a, b, preferred_element_type=F32)


def spin(v, cos, sin):
    a, b = v[0:16], v[16:32]
    return jnp.concatenate([a * cos - b * sin, b * cos + a * sin, v[32:]], axis=0)


def attend_kernel(
    order, x_ref, cos_ref, sin_ref, out_ref, q_n, k_n, v_n, q_t, k_t, v_t, do_t, s_buf, p_buf, dk, dv, fin
):
    def load(b, _):
        here = pl.ds(pl.multiple_of(order[b] * 128, 128), 128)
        t = x_ref[b].astype(F32).T
        cos, sin = cos_ref[:, here], sin_ref[:, here]
        q = spin(t[0:64], cos, sin) * 0.125
        k = spin(t[64:128], cos, sin)
        q_t[:, here] = q.astype(BF)
        k_t[:, here] = k.astype(BF)
        v_t[:, here] = t[128:192].astype(BF)
        do_t[:, here] = t[192:256].astype(BF)
        q_n[here, :] = q.T.astype(BF)
        k_n[here, :] = k.T.astype(BF)
        v_n[here, :] = x_ref[b][:, 128:192]
        return 0

    lax.fori_loop(0, 32, load, 0)
    dk[...] = jnp.zeros_like(dk)
    dv[...] = jnp.zeros_like(dv)
    square = (TILE, TILE)
    allowed = lax.broadcasted_iota(jnp.int32, square, 0) <= lax.broadcasted_iota(jnp.int32, square, 1)
    for i in range(LENGTH // TILE):
        qs = pl.ds(i * TILE, TILE)
        qt, qn, do = q_t[:, qs], q_n[qs, :], do_t[:, qs].astype(F32)

        def first(j, top):
            ks = pl.ds(pl.multiple_of(j * TILE, TILE), TILE)
            s = dot(k_n[ks, :], qt)
            s_buf[ks, :] = s
            return jnp.maximum(top, jnp.max(s, axis=0, keepdims=True))

        top = jnp.full((1, TILE), negative, F32)
        if i:
            top = lax.fori_loop(0, i, first, top)
        s = jnp.where(allowed, dot(k_n[qs, :], qt), negative)
        s_buf[qs, :] = s
        top = jnp.maximum(top, jnp.max(s, axis=0, keepdims=True))

        def second(j, carry):
            total, o = carry
            ks = pl.ds(pl.multiple_of(j * TILE, TILE), TILE)
            p = jnp.exp(s_buf[ks, :] - top)
            pb = p.astype(BF)
            p_buf[ks, :] = pb
            return total + jnp.sum(p, axis=0, keepdims=True), o + dot(v_t[:, ks], pb)

        total, o = lax.fori_loop(
            0, i + 1, second, (jnp.zeros((1, TILE), F32), jnp.zeros((64, TILE), F32))
        )
        inv = 1.0 / total
        o = o * inv
        do = do * inv
        delta = jnp.sum(do * o, axis=0, keepdims=True)
        dt = do.astype(BF)
        dn = do.T.astype(BF)

        def third(j, dq):
            ks = pl.ds(pl.multiple_of(j * TILE, TILE), TILE)
            dp = dot(v_n[ks, :], dt)
            pb = p_buf[ks, :]
            ds = (pb.astype(F32) * (dp - delta)).astype(BF)
            dk[ks, :] += dot(ds, qn)
            dv[ks, :] += dot(pb, dn)
            return dq + dot(k_t[:, ks], ds)

        dq = lax.fori_loop(0, i + 1, third, jnp.zeros((64, TILE), F32))
        fin[0:64, qs] = o
        fin[64:128, qs] = spin(dq, cos_ref[:, qs], -sin_ref[:, qs]) * 0.125

    def store(b, _):
        here = pl.ds(pl.multiple_of(order[b] * 128, 128), 128)
        k = spin(dk[here, :].T, cos_ref[:, here], -sin_ref[:, here])
        t = jnp.concatenate([fin[:, here], k, dv[here, :].T], axis=0)
        out_ref[b] = t.T.astype(BF)
        return 0

    lax.fori_loop(0, 32, store, 0)


def attend(order, x):
    freq = rope_base ** (-(jnp.arange(16, dtype=F32) * 2.0 / 32))
    angle = jnp.arange(LENGTH, dtype=F32)[None, :] * freq[:, None]
    natural, turned = pltpu.VMEM((LENGTH, 64), BF), pltpu.VMEM((64, LENGTH), BF)
    return pl.pallas_call(
        attend_kernel,
        out_shape=jax.ShapeDtypeStruct((32, 128, 256), BF),
        in_specs=[pl.BlockSpec(memory_space=pltpu.SMEM), VM, VM, VM],
        out_specs=VM,
        scratch_shapes=[natural] * 3
        + [turned] * 4
        + [pltpu.VMEM((LENGTH, TILE), F32), pltpu.VMEM((LENGTH, TILE), BF)]
        + [pltpu.VMEM((LENGTH, 64), F32)] * 2
        + [pltpu.VMEM((128, LENGTH), F32)],
        compiler_params=pltpu.CompilerParams(vmem_limit_bytes=60 * 2**20),
    )(order, x, jnp.cos(angle), jnp.sin(angle))


TURN = [(2, 2), (1, 2), (3, 2), (0, 2), (2, 1), (2, 3), (2, 0), (1, 1)]
TURN += [(1, 3), (3, 1), (3, 3), (0, 1), (0, 3), (1, 0), (3, 0), (0, 0)]


def sum_kernel(lhs, w, out, psend, precv, acc, far, near, ps, pr, send, recv):
    x, y, zh, zl, c = place()
    other = spot(x, y, zh, zl, 1 - c)

    def dev(half, da, db):
        dx, dy = (da, db) if half == 0 else (db, da)
        return spot((x + dx + 4) % 4, (y + dy + 4) % 4, zh, zl, c)

    def rows(half, part):
        return pl.ds(half * 64 + (32 if part == 2 else 0), 64 if part == 0 else 32)

    greet([dev(0, 1, 0), dev(0, -1, 0), dev(0, 0, 1), dev(0, 0, -1), other])
    started = []

    def go(cp):
        cp.start()
        started.append(cp)

    def step_to(h, g, s):
        return dev(h, 0, s) if g < 4 else dev(h, s, 0)

    def block(h, g, o):
        da, db = (g, o) if g < 4 else (o, 0)
        dx, dy = (da, db) if h == 0 else (db, da)
        return (dx % 4) * 4 + dy % 4

    def send_far(h, g):
        k = block(h, g, 2)
        for role, s in ((0, 1), (1, -1)):
            src, dst = acc.at[k, rows(h, role + 1)], far.at[h, g, role]
            go(remote(src, dst, send.at[h, g, role], recv.at[h, g, role], step_to(h, g, s)))

    def relay(h, g):
        for role, s in ((0, 1), (1, -1)):
            ref = far.at[h, g, role]
            remote(ref, ref, send.at[h, g, role], recv.at[h, g, role], other).wait_recv()
            k, r = block(h, g, s), rows(h, role + 1)
            acc[k, r] = (acc[k, r].astype(F32) + ref[...].astype(F32)).astype(BF)
            src, dst = acc.at[k, rows(h, 0)], near.at[h, g, role]
            go(remote(src, dst, send.at[h, g, 2 + role], recv.at[h, g, 2 + role], step_to(h, g, s)))

    def land(h, g):
        k, r = block(h, g, 0), rows(h, 0)
        for role in (0, 1):
            ref = near.at[h, g, role]
            remote(ref, ref, send.at[h, g, 2 + role], recv.at[h, g, 2 + role], other).wait_recv()
        tot = acc[k, r].astype(F32) + near[h, g, 0].astype(F32) + near[h, g, 1].astype(F32)
        if g < 4:
            acc[k, r] = tot.astype(BF)
        else:
            out[r] = tot

    def slot(dx, dy, core):
        return (((x + dx) % 4) * 4 + (y + dy) % 4) * 2 + core

    def for_partner(n):
        dx, dy = TURN[n]
        k, b = dx * 4 + dy, slot(dx, dy, 1 - c)

        def tile(t, _):
            cs = pl.ds(pl.multiple_of(t * TILE, TILE), TILE)
            psend[k, :, cs] = dot(lhs[b], w[:, cs]).astype(BF)
            return 0

        lax.fori_loop(0, WIDTH // TILE, tile, 0)
        go(remote(psend.at[k], precv.at[k], ps.at[k], pr.at[k], other))

    def for_own(n):
        dx, dy = TURN[n]
        k, b = dx * 4 + dy, slot(dx, dy, c)
        remote(psend.at[k], precv.at[k], ps.at[k], pr.at[k], other).wait_recv()

        def tile(t, _):
            cs = pl.ds(pl.multiple_of(t * TILE, TILE), TILE)
            acc[k, :, cs] = (dot(lhs[b], w[:, cs]) + precv[k, :, cs].astype(F32)).astype(BF)
            return 0

        lax.fori_loop(0, WIDTH // TILE, tile, 0)
        if dy == 2:
            send_far(0, dx)
        if dx == 2:
            send_far(1, dy)

    for_partner(0)
    for n in range(1, 16):
        for_partner(n)
        for_own(n - 1)
    for_own(15)
    for g in (2, 1, 3, 0):
        for h in (0, 1):
            relay(h, g)
    for g in (2, 1, 3, 0):
        for h in (0, 1):
            land(h, g)
            if g == 2:
                send_far(h, 4)
    for h in (0, 1):
        relay(h, 4)
    for h in (0, 1):
        land(h, 4)
    for cp in started:
        cp.wait_send()


def summed(lhs, w, which):
    dma = pltpu.SemaphoreType.DMA
    return pl.pallas_call(
        sum_kernel,
        out_shape=jax.ShapeDtypeStruct((128, WIDTH), F32),
        in_specs=[VM, VM],
        out_specs=VM,
        scratch_shapes=[pltpu.VMEM((16, 128, WIDTH), BF)] * 3
        + [pltpu.VMEM((2, 5, 2, 32, WIDTH), BF), pltpu.VMEM((2, 5, 2, 64, WIDTH), BF)]
        + [dma((16,)), dma((16,)), dma((2, 5, 4)), dma((2, 5, 4))],
        compiler_params=pltpu.CompilerParams(
            collective_id=which, has_side_effects=True, vmem_limit_bytes=60 * 2**20
        ),
    )(lhs, w)


def layer_norm(tokens, gain, shift):
    mean = jnp.mean(tokens, axis=-1, keepdims=True)
    centred = tokens - mean
    var = jnp.mean(centred * centred, axis=-1, keepdims=True)
    return centred * lax.rsqrt(var + eps_norm) * gain + shift


def swap_planes(v):
    return lax.ppermute(v, "shard", [(j, j ^ 1) for j in range(32)])


def body(
    tokens,
    span_order,
    ln_gain,
    ln_bias,
    qkv_weight,
    qkv_bias,
    out_weight,
    out_bias,
    fc1_weight,
    fc1_bias,
    fc2_weight,
    fc2_bias,
    cotangent,
):
    x, y, zh, zl, c = place()
    me = (x * 4 + y) * 2 + c
    shard = lax.axis_index("shard")

    small = lax.all_gather(
        jnp.concatenate([ln_gain, ln_bias, out_bias, fc2_bias, qkv_bias, fc1_bias]), "shard", axis=0
    ).astype(F32)
    gain, shift, b_out, b_back = (small[:, 64 * i : 64 * i + 64].reshape(WIDTH) for i in range(4))
    b_qkv = lax.dynamic_index_in_dim(
        small[:, 256:448].reshape(3, HEADS, 64), me, 1, keepdims=False
    ).reshape(192)
    b_in = lax.dynamic_index_in_dim(small[:, 448:704], me, 0, keepdims=False)
    orders = lax.all_gather(span_order, "rep", axis=0, tiled=True)
    order = lax.dynamic_index_in_dim(orders, 2 * zl + zh, 0, keepdims=False)

    cols = jnp.concatenate(
        [
            jnp.transpose(qkv_weight.reshape(64, 3, HEADS, 64), (2, 0, 1, 3)).reshape(HEADS, 64, 192),
            jnp.transpose(fc1_weight.reshape(64, HEADS, 256), (1, 0, 2)),
        ],
        axis=-1,
    ).reshape(16, 2, 64, 448)
    cols = lax.dynamic_index_in_dim(cols, c, 1, keepdims=True)
    cols = jnp.broadcast_to(cols, (16, 2, 64, 448)).reshape(32, 64, 448)
    w_cols = lax.all_to_all(cols, "shard", 0, 0, tiled=True).reshape(WIDTH, 448)
    own_rows = jnp.concatenate([out_weight, fc2_weight], axis=0)
    w_rows = jnp.where(c == zh, own_rows, swap_planes(own_rows))

    flat = tokens.reshape(128, WIDTH).astype(F32)
    normed = layer_norm(flat, gain, shift).astype(BF)
    g_own = cotangent.reshape(128, WIDTH)
    normed_all, g_all = gather(normed, g_own)
    normed_all = normed_all.reshape(LENGTH, WIDTH)
    g_all = g_all.reshape(LENGTH, WIDTH)

    contract = (((1,), (1,)), ((), ()))
    mixed = dot(normed_all, w_cols[:, :192]) + b_qkv
    hidden = dot(normed_all, w_cols[:, 192:]) + b_in
    d_att = lax.dot_general(g_all, w_rows[:64], contract, preferred_element_type=F32)
    d_active = lax.dot_general(g_all, w_rows[64:], contract, preferred_element_type=F32)
    active, pull = jax.vjp(lambda u: jax.nn.gelu(u, approximate=True), hidden)
    active = active.astype(BF)
    d_hidden = pull(d_active)[0].astype(BF)

    fields = jnp.concatenate([mixed.astype(BF), d_att.astype(BF)], axis=-1).reshape(16, 2, 128, 256)

    def exchange(v):
        keep = lax.dynamic_index_in_dim(v, zh, 1, keepdims=False)
        came = swap_planes(lax.dynamic_index_in_dim(v, 1 - zh, 1, keepdims=False))
        pair = (jnp.where(zh == 0, keep, came), jnp.where(zh == 0, came, keep))
        return jnp.stack(pair, axis=1).reshape(32, 128, 256)

    done = exchange(attend(order, exchange(fields)).reshape(16, 2, 128, 256)).reshape(LENGTH, 256)
    left = jnp.concatenate([done[:, :64], active], axis=-1)
    right = jnp.concatenate([done[:, 64:], d_hidden], axis=-1)
    branch = summed(left.reshape(32, 128, 320), w_rows, 2)
    d_normed = summed(right.reshape(32, 128, 448), w_cols.T, 3)
    block_out = (flat + branch + b_out + b_back).astype(BF).reshape(1, 128, WIDTH)
    _, norm_pull = jax.vjp(layer_norm, flat, gain, shift)
    d_flat, d_gain, d_shift = norm_pull(d_normed)
    d_tokens = (g_own.astype(F32) + d_flat).astype(BF).reshape(1, 128, WIDTH)

    outer = (((0,), (0,)), ((), ()))
    g_cols = lax.dot_general(normed_all, right, outer, preferred_element_type=F32)
    g_rows = lax.dot_general(left, g_all, outer, preferred_element_type=F32)
    moved = lax.all_to_all(g_cols.reshape(32, 64, 448), "shard", 0, 0, tiled=True)
    moved = jnp.sum(moved.reshape(16, 2, 64, 448), axis=1)
    full = jnp.zeros((16, 2, 64, 448), F32)
    full = lax.dynamic_update_slice_in_dim(full, moved[:, None], c, 1)
    g_rows = g_rows + swap_planes(g_rows)
    g_rows = jnp.where(c == zh, g_rows, 0.0)
    full, g_rows = lax.psum((full, g_rows), "rep")
    full = full.reshape(32, 64, 448)
    g_qkv = jnp.transpose(full[..., :192].reshape(32, 64, 3, 64), (1, 2, 0, 3)).reshape(64, 6144)
    g_in = jnp.transpose(full[..., 192:], (1, 0, 2)).reshape(64, 8192)

    sums = jnp.sum(right.astype(F32), axis=0)
    bq = jnp.zeros((3, HEADS, 64), F32)
    bq = lax.dynamic_update_slice_in_dim(bq, sums[:192].reshape(3, 1, 64), me, 1).reshape(6144)
    bi = jnp.zeros((HEADS, 256), F32)
    bi = lax.dynamic_update_slice_in_dim(bi, sums[None, 192:], me, 0).reshape(8192)
    bo = jnp.sum(g_own.astype(F32), axis=0)
    vec = jnp.concatenate([v.reshape(32, -1) for v in (d_gain, d_shift, bo, bq, bi)], axis=1)
    vec = lax.dynamic_index_in_dim(lax.psum(vec, ("rep", "shard")), shard, 0, keepdims=False)
    return (
        block_out,
        d_tokens,
        vec[:64],
        vec[64:128],
        g_qkv,
        vec[192:384],
        g_rows[:64],
        vec[128:192],
        g_in,
        vec[384:],
        g_rows[64:],
        vec[128:192],
    )


def solution(mesh):
    act, rows, vec = P("rep", "shard", None), P("shard", None), P("shard")
    return jax.shard_map(
        body,
        mesh=mesh,
        in_specs=(act, P("rep", None), vec, vec, rows, vec, rows, vec, rows, vec, rows, vec, act),
        out_specs=(act, act, vec, vec, rows, vec, rows, vec, rows, vec, rows, vec),
        check_vma=False,
    )
```

```python
import jax
import jax.numpy as jnp
from jax import lax
from jax.experimental import pallas as pl
from jax.experimental.pallas import tpu as pltpu
from jax.sharding import PartitionSpec as P

F32 = jnp.float32
BF = jnp.bfloat16
MESH = pl.DeviceIdType.MESH
HEADS = 32
WIDTH = 2048
LENGTH = 4096
TILE = 512
eps_norm = 1e-05
rope_base = 10000.0
negative = -1e30
VM = pl.BlockSpec(memory_space=pltpu.VMEM)
ANY = pl.BlockSpec(memory_space=pl.ANY)


def place():
    rep = lax.axis_index("rep")
    sh = lax.axis_index("shard")
    return sh // 8, (sh // 2) % 4, sh % 2, rep // 2, rep % 2


def spot(x, y, zh, zl, c):
    return (zl * 2 + c, (x * 4 + y) * 2 + zh)


def remote(src, dst, send, recv, to):
    return pltpu.make_async_remote_copy(
        src_ref=src, dst_ref=dst, send_sem=send, recv_sem=recv, device_id=to, device_id_type=MESH
    )


def greet(peers):
    barrier = pltpu.get_barrier_semaphore()
    for d in peers:
        pl.semaphore_signal(barrier, inc=1, device_id=d, device_id_type=MESH)
    pl.semaphore_wait(barrier, len(peers))


OFFS = [(p, q) for p in (0, -1, 1, 2) for q in (0, -1, 1, 2)]
GROUP = {0: 0, -1: 1, 1: 2, 2: 3}


LEVELS = (
    ((0, 0),),
    ((-1, 0), (1, 0), (0, -1), (0, 1)),
    ((2, 0), (0, 2), (-1, -1), (-1, 1), (1, -1), (1, 1)),
    ((-1, 2), (1, 2), (2, -1), (2, 1)),
    ((2, 2),),
)
N_LINK = 20
N_MORE = 110


def gelu_both(u):
    k0, k1 = 0.7978845608028654, 0.044715
    sq = u * u
    t = jnp.tanh(k0 * u * (1.0 + k1 * sq))
    half = 0.5 * (1.0 + t)
    return u * half, half + 0.5 * u * (1.0 - t * t) * k0 * (1.0 + 3.0 * k1 * sq)


def front_kernel(
    tok, g_own, small, w_qkv, w_in, w_out, w_back,
    n_all, g_all, fields, active, d_hidden, cols_t, rows_w, small_all, small_other,
    n_own, buf, d_act, d_att, f_send, w_f, w_m, w_ot, w_bt, wf1, wq1, wf2, wq2, table, bq,
    send, recv, psend, precv, msend, mrecv, fsem_s, fsem_r, loc, lsem,
):
    x, y, zh, zl, c = place()
    z = zh * 2 + zl
    other = spot(x, y, zh, zl, 1 - c)

    def at(dx, dy):
        return spot((x + dx + 4) % 4, (y + dy + 4) % 4, zh, zl, c)

    def at_z(dz):
        w = (z + dz + 4) % 4
        return spot(x, y, w // 2, w % 2, c)

    def dev(half, da, db):
        return at(da, db) if half == 0 else at(db, da)

    def slot(half, da, db, core):
        dx, dy = (da, db) if half == 0 else (db, da)
        return (((x + dx + 4) % 4) * 4 + (y + dy + 4) % 4) * 2 + core

    def rows(half, part):
        return pl.ds(half * 64 + (32 if part == 2 else 0), 64 if part == 0 else 32)

    greet([at(1, 0), at(-1, 0), at(2, 0), at(0, 1), at(0, -1), at(0, 2), at_z(1), at_z(-1), at_z(2), other])
    started = []
    ins = (g_own, n_own)
    outs = (g_all, n_all)
    counter = [0]

    def go(cp):
        cp.start()
        started.append(cp)

    def new():
        counter[0] += 1
        return counter[0] - 1

    def push(src, dst, to, land):
        i = new()
        go(remote(src, dst, msend.at[i], mrecv.at[i], to))
        return lambda: remote(land, land, msend.at[i], mrecv.at[i], to).wait_recv()

    def wrap(v):
        return (v + 4) % 4

    small_all[x, y, zh] = small[...]
    got = [push(small, small_other, other, small_other)]
    waits = []
    for d in (1, -1, 2):
        waits.append(
            push(small, small_all.at[x, y, zh], at(d, 0), small_all.at[wrap(x - d), y, zh])
        )

    def pass_on(a, h, role, off, part, to, own=False):
        s, r = slot(h, *off, c), rows(h, part)
        src = ins[a].at[r] if own else outs[a].at[s, r]
        go(remote(src, outs[a].at[s, r], send.at[a, h, role], recv.at[a, h, role], dev(h, *to)))

    def arrived(a, h, role, off, part):
        ref = outs[a].at[slot(h, *off, c), rows(h, part)]
        remote(ref, ref, send.at[a, h, role], recv.at[a, h, role], other).wait_recv()

    def share(a, h, off, own=False):
        i = OFFS.index(off)
        s, r = slot(h, *off, c), rows(h, 0)
        src = ins[a].at[r] if own else outs[a].at[s, r]
        go(remote(src, outs[a].at[s, r], psend.at[a, h, i], precv.at[a, h, i], other))

    def second(a, h, ao, own=False):
        k = GROUP[ao]
        pass_on(a, h, 4 + 2 * k, (ao, 0), 0, (0, 1), own)
        pass_on(a, h, 5 + 2 * k, (ao, 0), 0, (0, -1), own)

    def near(a, h, ao):
        k = GROUP[ao]
        arrived(a, h, 4 + 2 * k, (ao, -1), 0)
        pass_on(a, h, 12 + 2 * k, (ao, -1), 1, (0, 1))
        share(a, h, (ao, -1))
        arrived(a, h, 5 + 2 * k, (ao, 1), 0)
        pass_on(a, h, 13 + 2 * k, (ao, 1), 2, (0, -1))
        share(a, h, (ao, 1))

    def far(a, h, ao):
        k = GROUP[ao]
        arrived(a, h, 12 + 2 * k, (ao, 2), 1)
        arrived(a, h, 13 + 2 * k, (ao, 2), 2)
        share(a, h, (ao, 2))

    def begin(a):
        cp = pltpu.make_async_copy(ins[a], outs[a].at[slot(0, 0, 0, c)], loc.at[a])
        cp.start()
        for h in (0, 1):
            pass_on(a, h, 0, (0, 0), 0, (1, 0), True)
            pass_on(a, h, 1, (0, 0), 0, (-1, 0), True)
        for h in (0, 1):
            second(a, h, 0, True)
            share(a, h, (0, 0), True)
        return cp

    def level(a, n):
        for h in (0, 1):
            if n == 1:
                arrived(a, h, 0, (-1, 0), 0)
                pass_on(a, h, 2, (-1, 0), 1, (1, 0))
                second(a, h, -1)
                share(a, h, (-1, 0))
                arrived(a, h, 1, (1, 0), 0)
                pass_on(a, h, 3, (1, 0), 2, (-1, 0))
                second(a, h, 1)
                share(a, h, (1, 0))
                near(a, h, 0)
            if n == 2:
                arrived(a, h, 2, (2, 0), 1)
                arrived(a, h, 3, (2, 0), 2)
                second(a, h, 2)
                share(a, h, (2, 0))
                near(a, h, -1)
                near(a, h, 1)
                far(a, h, 0)
            if n == 3:
                near(a, h, 2)
                far(a, h, -1)
                far(a, h, 1)
            if n == 4:
                far(a, h, 2)

    held = [begin(0)]

    mine = pl.ds(pl.multiple_of(zl * 32, 32), 32)

    def col_copies(dx):
        xx = wrap(x + dx)
        for yy in range(4):
            t = (xx * 4 + yy) * 2 + c
            yield (
                w_in.at[mine, pl.ds(pl.multiple_of(t * 256, 256), 256)], wf1.at[yy, x], wf1.at[yy, wrap(x - dx)],
            )
            for m in range(3):
                lanes = pl.ds(pl.multiple_of(m * WIDTH + (xx * 4 + yy) * 128, 128), 128)
                yield w_qkv.at[mine, lanes], wq1.at[yy, x, m], wq1.at[yy, wrap(x - dx), m]

    mates = []
    for i, (src, dst, _) in enumerate(col_copies(0)):
        cp = pltpu.make_async_copy(src, dst, lsem.at[i])
        cp.start()
        mates.append(cp)
    for d in (1, -1, 2):
        for src, dst, land in col_copies(d):
            waits.append(push(src, dst, at(d, 0), land))

    ri = new(), new()
    to_row = spot(x, y, 1 - zh, 1 - zl, c)

    def row_copies():
        for i, src, part in ((0, w_back, pl.ds(0, 256)), (1, w_out, pl.ds(256, 64))):
            yield remote(src, rows_w.at[part], msend.at[ri[i]], mrecv.at[ri[i]], to_row), pltpu.make_async_copy(
                src, rows_w.at[part], lsem.at[16 + i]
            )

    @pl.when(c == zh)
    def _():
        for far_copy, near_copy in row_copies():
            far_copy.start()
            near_copy.start()

    for w in waits[:3]:
        w()
    waits = waits[3:]
    more = []
    for d in (1, -1, 2):
        more.append(
            push(small_all.at[:, y, zh], small_all.at[:, y, zh], at(0, d), small_all.at[:, wrap(y - d), zh])
        )
    for w in more:
        w()
    push(small_all.at[:, :, zh], small_all.at[:, :, zh], at_z(2), small_all.at[:, :, 1 - zh])()
    got[0]()
    for j in range(32):
        piece = small_all[j // 8, (j // 2) % 4, j % 2]
        for i in (0, 1):
            table[pl.ds(i, 1), pl.ds(64 * j, 64)] = piece[0:1, 64 * i : 64 * i + 64]
        for i in range(3):
            bq[pl.ds(3 * j + i, 1), 0:64] = piece[2 + i // 2 : 3 + i // 2, 64 * (i % 2) : 64 * (i % 2) + 64]

    def norm(i, _):
        r = pl.ds(pl.multiple_of(i * 32, 32), 32)
        v = tok[r, :].astype(F32)
        v = v - jnp.mean(v, axis=-1, keepdims=True)
        v = v * lax.rsqrt(jnp.mean(v * v, axis=-1, keepdims=True) + eps_norm)
        n_own[r, :] = (v * table[0:1, :] + table[1:2, :]).astype(BF)
        return 0

    lax.fori_loop(0, 4, norm, 0)
    held.append(begin(1))

    for w in waits:
        w()
    for cp in mates:
        cp.wait()
    waits = []
    for d in (1, -1, 2):
        yy = wrap(y + d)
        waits.append(push(wf1.at[yy], wf2.at[:, y, z], at(0, d), wf2.at[:, wrap(y - d), z]))
        waits.append(push(wq1.at[yy], wq2.at[:, :, y, z], at(0, d), wq2.at[:, :, wrap(y - d), z]))
    wf2[:, y, z] = wf1[y]
    wq2[:, :, y, z] = wq1[y]
    level(0, 1)
    for w in waits:
        w()
    waits = []
    for s in (1, -1):
        waits.append(push(wf2.at[:, :, z], wf2.at[:, :, z], at_z(s), wf2.at[:, :, wrap(z - s)]))
        waits.append(push(wq2.at[:, :, :, z], wq2.at[:, :, :, z], at_z(s), wq2.at[:, :, :, wrap(z - s)]))

    @pl.when(c == zh)
    def _():
        for _, near_copy in row_copies():
            near_copy.wait()

    @pl.when(c != zh)
    def _():
        for far_copy, _ in row_copies():
            far_copy.wait_recv()

    def turn_rows(i, _):
        r = pl.ds(pl.multiple_of(i * 256, 256), 256)
        w_bt[r, :] = rows_w[0:256, r].astype(F32).T.astype(BF)
        w_ot[r, :] = rows_w[256:320, r].astype(F32).T.astype(BF)
        return 0

    lax.fori_loop(0, 8, turn_rows, 0)

    def pass_columns():
        for w in waits:
            w()
        waits.clear()
        for s, k in ((1, 0), (-1, 2)):
            zz, part, far_z = wrap(z - s), pl.ds(k, 2), wrap(z + 2)
            waits.append(push(wf2.at[part, :, zz], wf2.at[part, :, zz], at_z(s), wf2.at[part, :, far_z]))
            waits.append(
                push(wq2.at[part, :, :, zz], wq2.at[part, :, :, zz], at_z(s), wq2.at[part, :, :, far_z])
            )

    def take_columns():
        for w in waits:
            w()
        waits.clear()
        for xx in range(4):
            r = pl.ds(xx * 512, 512)
            w_f[r, :] = wf2[xx].reshape(512, 256)
            for m in range(3):
                v = wq2[xx, m].reshape(512, 128)
                w_m[r, 64 * m : 64 * m + 64] = jnp.where(c == 0, v[:, 0:64], v[:, 64:128])

        def turn_cols(i, _):
            r = pl.ds(pl.multiple_of(i * 256, 256), 256)
            cols_t[0:256, r] = w_f[r, :].astype(F32).T.astype(BF)
            cols_t[256:448, r] = w_m[r, :].astype(F32).T.astype(BF)
            return 0

        lax.fori_loop(0, 8, turn_cols, 0)

    t = (x * 4 + y) * 2 + c
    here = small_all[x, y, c]
    b_in = jnp.concatenate([here[4:5, :], here[5:6, :]], axis=1)
    b_m = jnp.concatenate([bq[pl.ds(t + 32 * m, 1), 0:64] for m in range(3)], axis=1)

    queue = []
    step = [0]

    def pair(off):
        return ((x + off[0] + 4) % 4) * 4 + (y + off[1] + 4) % 4

    def fetch(a, off):
        p = pair(off)
        for h in (0, 1):
            i = OFFS.index(off if h == 0 else (off[1], off[0]))
            ref = outs[a].at[p * 2 + 1 - c, rows(h, 0)]
            remote(ref, ref, psend.at[a, h, i], precv.at[a, h, i], other).wait_recv()
        if off == (0, 0):
            held[a].wait()
        k = step[0] % 2
        step[0] += 1
        cp = pltpu.make_async_copy(outs[a].at[pl.ds(p * 2, 2)], buf.at[k], loc.at[2 + k])
        cp.start()
        return a, p, k, cp

    def run(job):
        a, p, k, cp = job
        cp.wait()
        two = pl.ds(p * 2, 2)

        def over(wa, wb, na, nb):
            def inner(i, carry):
                va, vb = carry
                cs = pl.ds(pl.multiple_of(i * 512, 512), 512)
                v = buf[k, :, :, cs].reshape(256, 512)
                return va + dot(v, wa[cs, :]), vb + dot(v, wb[cs, :])

            return lax.fori_loop(0, 4, inner, (jnp.zeros((256, na), F32), jnp.zeros((256, nb), F32)))

        if a == 0:
            da, do = over(w_bt, w_ot, 256, 64)
            d_act[two] = da.reshape(2, 128, 256)
            d_att[two] = do.astype(BF).reshape(2, 128, 64)
            return
        hidden, mixed = over(w_f, w_m, 256, 192)
        act, slope = gelu_both(hidden + b_in)
        active[two] = act.astype(BF).reshape(2, 128, 256)
        d_hidden[two] = (d_act[two].reshape(256, 256) * slope).astype(BF).reshape(2, 128, 256)
        mixed = (mixed + b_m).astype(BF).reshape(2, 128, 192)
        f_send[p, :, :, 0:192] = mixed
        f_send[p, :, :, 192:256] = d_att[two]
        fields[p, zh] = f_send[p, zh]
        go(remote(f_send.at[p, 1 - zh], fields.at[p, zh], fsem_s.at[p], fsem_r.at[p], at_z(2)))

    def compute(a, offs):
        for off in offs:
            queue.append(fetch(a, off))
            while len(queue) > 1:
                run(queue.pop(0))

    compute(0, LEVELS[0])
    pass_columns()
    level(0, 2)
    compute(0, LEVELS[1])
    level(1, 1)
    take_columns()
    level(0, 3)
    compute(0, LEVELS[2])
    level(1, 2)
    compute(1, LEVELS[0])
    level(0, 4)
    compute(0, LEVELS[3])
    compute(1, LEVELS[1])
    level(1, 3)
    compute(0, LEVELS[4])
    compute(1, LEVELS[2])
    level(1, 4)
    compute(1, LEVELS[3])
    compute(1, LEVELS[4])
    while queue:
        run(queue.pop(0))

    def came(p, _):
        ref = fields.at[p, 1 - zh]
        remote(ref, ref, fsem_s.at[p], fsem_r.at[p], other).wait_recv()
        return 0

    lax.fori_loop(0, 16, came, 0)
    for cp in started:
        cp.wait_send()

    @pl.when(c == zh)
    def _():
        for far_copy, _ in row_copies():
            far_copy.wait_send()


def front(tok, g_own, small, w_qkv, w_in, w_out, w_back):
    dma = pltpu.SemaphoreType.DMA

    def vmem(*shape, t=BF):
        return pltpu.VMEM(shape, t)

    def arr(*shape, t=BF):
        return jax.ShapeDtypeStruct(shape, t)

    return pl.pallas_call(
        front_kernel,
        out_shape=[
            arr(32, 128, WIDTH), arr(32, 128, WIDTH), arr(16, 2, 128, 256), arr(32, 128, 256), arr(32, 128, 256),
            arr(448, WIDTH), arr(320, WIDTH), arr(4, 4, 2, 8, 128, t=F32), arr(8, 128, t=F32),
        ],
        in_specs=[VM, ANY, VM, ANY, ANY, ANY, ANY],
        out_specs=[ANY, ANY, VM, VM, VM, VM, VM, VM, VM],
        scratch_shapes=[
            vmem(128, WIDTH), vmem(2, 2, 128, WIDTH), vmem(32, 128, 256, t=F32), vmem(32, 128, 64),
            vmem(16, 2, 128, 256), vmem(WIDTH, 256), vmem(WIDTH, 192), vmem(WIDTH, 64), vmem(WIDTH, 256),
            vmem(4, 4, 32, 256), vmem(4, 4, 3, 32, 128), vmem(4, 4, 4, 32, 256), vmem(4, 3, 4, 4, 32, 128),
            vmem(8, WIDTH, t=F32), vmem(96, 128, t=F32),
            dma((2, 2, 20)), dma((2, 2, 20)), dma((2, 2, 16)), dma((2, 2, 16)), dma((N_MORE,)), dma((N_MORE,)),
            dma((16,)), dma((16,)), dma((4,)), dma((18,)),
        ],
        compiler_params=pltpu.CompilerParams(
            collective_id=1, has_side_effects=True, vmem_limit_bytes=60 * 2**20
        ),
    )(tok, g_own, small, w_qkv, w_in, w_out, w_back)


def dot(a, b):
    return jnp.dot(a, b, preferred_element_type=F32)


def spin(v, cos, sin):
    a, b = v[0:16], v[16:32]
    return jnp.concatenate([a * cos - b * sin, b * cos + a * sin, v[32:]], axis=0)


def attend_kernel(
    order, x_ref, cos_ref, sin_ref, out_ref, q_n, k_n, v_n, q_t, k_t, v_t, do_t, s_buf, p_buf, dk, dv, fin
):
    def load(b, _):
        here = pl.ds(pl.multiple_of(order[b] * 128, 128), 128)
        t = x_ref[b].astype(F32).T
        cos, sin = cos_ref[:, here], sin_ref[:, here]
        q = spin(t[0:64], cos, sin) * 0.125
        k = spin(t[64:128], cos, sin)
        q_t[:, here] = q.astype(BF)
        k_t[:, here] = k.astype(BF)
        v_t[:, here] = t[128:192].astype(BF)
        do_t[:, here] = t[192:256].astype(BF)
        q_n[here, :] = q.T.astype(BF)
        k_n[here, :] = k.T.astype(BF)
        v_n[here, :] = x_ref[b][:, 128:192]
        return 0

    lax.fori_loop(0, 32, load, 0)
    dk[...] = jnp.zeros_like(dk)
    dv[...] = jnp.zeros_like(dv)
    square = (TILE, TILE)
    allowed = lax.broadcasted_iota(jnp.int32, square, 0) <= lax.broadcasted_iota(jnp.int32, square, 1)
    for i in range(LENGTH // TILE):
        qs = pl.ds(i * TILE, TILE)
        qt, qn, do = q_t[:, qs], q_n[qs, :], do_t[:, qs].astype(F32)

        def first(j, top):
            ks = pl.ds(pl.multiple_of(j * TILE, TILE), TILE)
            s = dot(k_n[ks, :], qt)
            s_buf[ks, :] = s
            return jnp.maximum(top, jnp.max(s, axis=0, keepdims=True))

        top = jnp.full((1, TILE), negative, F32)
        if i:
            top = lax.fori_loop(0, i, first, top)
        s = jnp.where(allowed, dot(k_n[qs, :], qt), negative)
        s_buf[qs, :] = s
        top = jnp.maximum(top, jnp.max(s, axis=0, keepdims=True))

        def second(j, carry):
            total, o = carry
            ks = pl.ds(pl.multiple_of(j * TILE, TILE), TILE)
            p = jnp.exp(s_buf[ks, :] - top)
            pb = p.astype(BF)
            p_buf[ks, :] = pb
            return total + jnp.sum(p, axis=0, keepdims=True), o + dot(v_t[:, ks], pb)

        total, o = lax.fori_loop(
            0, i + 1, second, (jnp.zeros((1, TILE), F32), jnp.zeros((64, TILE), F32))
        )
        inv = 1.0 / total
        o = o * inv
        do = do * inv
        delta = jnp.sum(do * o, axis=0, keepdims=True)
        dt = do.astype(BF)
        dn = do.T.astype(BF)

        def third(j, dq):
            ks = pl.ds(pl.multiple_of(j * TILE, TILE), TILE)
            dp = dot(v_n[ks, :], dt)
            pb = p_buf[ks, :]
            ds = (pb.astype(F32) * (dp - delta)).astype(BF)
            dk[ks, :] += dot(ds, qn)
            dv[ks, :] += dot(pb, dn)
            return dq + dot(k_t[:, ks], ds)

        dq = lax.fori_loop(0, i + 1, third, jnp.zeros((64, TILE), F32))
        fin[0:64, qs] = o
        fin[64:128, qs] = spin(dq, cos_ref[:, qs], -sin_ref[:, qs]) * 0.125

    def store(b, _):
        here = pl.ds(pl.multiple_of(order[b] * 128, 128), 128)
        k = spin(dk[here, :].T, cos_ref[:, here], -sin_ref[:, here])
        t = jnp.concatenate([fin[:, here], k, dv[here, :].T], axis=0)
        out_ref[b] = t.T.astype(BF)
        return 0

    lax.fori_loop(0, 32, store, 0)


def attend(order, x):
    freq = rope_base ** (-(jnp.arange(16, dtype=F32) * 2.0 / 32))
    angle = jnp.arange(LENGTH, dtype=F32)[None, :] * freq[:, None]
    natural, turned = pltpu.VMEM((LENGTH, 64), BF), pltpu.VMEM((64, LENGTH), BF)
    return pl.pallas_call(
        attend_kernel,
        out_shape=jax.ShapeDtypeStruct((32, 128, 256), BF),
        in_specs=[pl.BlockSpec(memory_space=pltpu.SMEM), VM, VM, VM],
        out_specs=VM,
        scratch_shapes=[natural] * 3
        + [turned] * 4
        + [pltpu.VMEM((LENGTH, TILE), F32), pltpu.VMEM((LENGTH, TILE), BF)]
        + [pltpu.VMEM((LENGTH, 64), F32)] * 2
        + [pltpu.VMEM((128, LENGTH), F32)],
        compiler_params=pltpu.CompilerParams(vmem_limit_bytes=60 * 2**20),
    )(order, x, jnp.cos(angle), jnp.sin(angle))


TURN = [(2, 2), (1, 2), (3, 2), (0, 2), (2, 1), (2, 3), (2, 0), (1, 1)]
TURN += [(1, 3), (3, 1), (3, 3), (0, 1), (0, 3), (1, 0), (3, 0), (0, 0)]


def sum_kernel(lhs, w, out, psend, precv, acc, far, near, ps, pr, send, recv):
    x, y, zh, zl, c = place()
    other = spot(x, y, zh, zl, 1 - c)

    def dev(half, da, db):
        dx, dy = (da, db) if half == 0 else (db, da)
        return spot((x + dx + 4) % 4, (y + dy + 4) % 4, zh, zl, c)

    def rows(half, part):
        return pl.ds(half * 64 + (32 if part == 2 else 0), 64 if part == 0 else 32)

    greet([dev(0, 1, 0), dev(0, -1, 0), dev(0, 0, 1), dev(0, 0, -1), other])
    started = []

    def go(cp):
        cp.start()
        started.append(cp)

    def step_to(h, g, s):
        return dev(h, 0, s) if g < 4 else dev(h, s, 0)

    def block(h, g, o):
        da, db = (g, o) if g < 4 else (o, 0)
        dx, dy = (da, db) if h == 0 else (db, da)
        return (dx % 4) * 4 + dy % 4

    def send_far(h, g):
        k = block(h, g, 2)
        for role, s in ((0, 1), (1, -1)):
            src, dst = acc.at[k, rows(h, role + 1)], far.at[h, g, role]
            go(remote(src, dst, send.at[h, g, role], recv.at[h, g, role], step_to(h, g, s)))

    def relay(h, g):
        for role, s in ((0, 1), (1, -1)):
            ref = far.at[h, g, role]
            remote(ref, ref, send.at[h, g, role], recv.at[h, g, role], other).wait_recv()
            k, r = block(h, g, s), rows(h, role + 1)
            acc[k, r] = (acc[k, r].astype(F32) + ref[...].astype(F32)).astype(BF)
            src, dst = acc.at[k, rows(h, 0)], near.at[h, g, role]
            go(remote(src, dst, send.at[h, g, 2 + role], recv.at[h, g, 2 + role], step_to(h, g, s)))

    def land(h, g):
        k, r = block(h, g, 0), rows(h, 0)
        for role in (0, 1):
            ref = near.at[h, g, role]
            remote(ref, ref, send.at[h, g, 2 + role], recv.at[h, g, 2 + role], other).wait_recv()
        tot = acc[k, r].astype(F32) + near[h, g, 0].astype(F32) + near[h, g, 1].astype(F32)
        if g < 4:
            acc[k, r] = tot.astype(BF)
        else:
            out[r] = tot

    def slot(dx, dy, core):
        return (((x + dx) % 4) * 4 + (y + dy) % 4) * 2 + core

    def for_partner(n):
        dx, dy = TURN[n]
        k, b = dx * 4 + dy, slot(dx, dy, 1 - c)

        def tile(t, _):
            cs = pl.ds(pl.multiple_of(t * TILE, TILE), TILE)
            psend[k, :, cs] = dot(lhs[b], w[:, cs]).astype(BF)
            return 0

        lax.fori_loop(0, WIDTH // TILE, tile, 0)
        go(remote(psend.at[k], precv.at[k], ps.at[k], pr.at[k], other))

    def for_own(n):
        dx, dy = TURN[n]
        k, b = dx * 4 + dy, slot(dx, dy, c)
        remote(psend.at[k], precv.at[k], ps.at[k], pr.at[k], other).wait_recv()

        def tile(t, _):
            cs = pl.ds(pl.multiple_of(t * TILE, TILE), TILE)
            acc[k, :, cs] = (dot(lhs[b], w[:, cs]) + precv[k, :, cs].astype(F32)).astype(BF)
            return 0

        lax.fori_loop(0, WIDTH // TILE, tile, 0)
        if dy == 2:
            send_far(0, dx)
        if dx == 2:
            send_far(1, dy)

    for_partner(0)
    for n in range(1, 16):
        for_partner(n)
        for_own(n - 1)
    for_own(15)
    for g in (2, 1, 3, 0):
        for h in (0, 1):
            relay(h, g)
    for g in (2, 1, 3, 0):
        for h in (0, 1):
            land(h, g)
            if g == 2:
                send_far(h, 4)
    for h in (0, 1):
        relay(h, 4)
    for h in (0, 1):
        land(h, 4)
    for cp in started:
        cp.wait_send()


def summed(lhs, w, which):
    dma = pltpu.SemaphoreType.DMA
    return pl.pallas_call(
        sum_kernel,
        out_shape=jax.ShapeDtypeStruct((128, WIDTH), F32),
        in_specs=[VM, VM],
        out_specs=VM,
        scratch_shapes=[pltpu.VMEM((16, 128, WIDTH), BF)] * 3
        + [pltpu.VMEM((2, 5, 2, 32, WIDTH), BF), pltpu.VMEM((2, 5, 2, 64, WIDTH), BF)]
        + [dma((16,)), dma((16,)), dma((2, 5, 4)), dma((2, 5, 4))],
        compiler_params=pltpu.CompilerParams(
            collective_id=which, has_side_effects=True, vmem_limit_bytes=60 * 2**20
        ),
    )(lhs, w)


def grads_kernel(
    cols, rws, vec, cols_out, rows_out, vec_out,
    far, near, mine, total, a1, rfar, rbuf, vp, vs, vx, vy, vq, vz, vr, send, recv,
):
    x, y, zh, zl, c = place()
    z = zh * 2 + zl
    other = spot(x, y, zh, zl, 1 - c)
    started = []
    counter = [0]

    def wrap(v):
        return (v + 4) % 4

    def at(dx, dy):
        return spot(wrap(x + dx), wrap(y + dy), zh, zl, c)

    def at_z(dz):
        w = wrap(z + dz)
        return spot(x, y, w // 2, w % 2, c)

    twin = spot(x, y, zh, 1 - zl, c)
    greet([at(1, 0), at(-1, 0), at(2, 0), at(0, 1), at(0, -1), at(0, 2), at_z(1), at_z(-1), at_z(2), other])

    def new():
        counter[0] += 1
        return counter[0] - 1

    def copy(src, dst, i, to):
        return remote(src, dst, send.at[i], recv.at[i], to)

    def push(src, dst, to, land):
        i = new()
        cp = copy(src, dst, i, to)
        cp.start()
        started.append(cp)
        return lambda: copy(land, land, i, to).wait_recv()

    def only(test):
        return pl.when(test)

    zf = wrap(z + 2)
    parts = ((1, pl.ds(0, 8)), (-1, pl.ds(8, 8)))
    got_far = [push(cols.at[p, zf], far.at[r], at_z(s), far.at[r]) for r, (s, p) in enumerate(parts)]

    halves = (pl.ds(0, 160), pl.ds(160, 160))
    r_far, r_mid, r_twin, r_core = (new(), new()), new(), new(), (new(), new())
    down, up = at_z(-1), at_z(1)
    receiver = c == zh

    def early(to):
        return [copy(rws.at[halves[k]], rfar.at[k], r_far[k], to) for k in (0, 1)]

    for flag, to in ((0, down), (1, up)):

        @only((c != zh) & (zl == flag))
        def _():
            for cp in early(to):
                cp.start()

    got_v = push(vec, vp, other, vp)

    got_near = []
    for r, (s, p) in enumerate(parts):
        got_far[r]()
        mine[r] = cols[:, wrap(z + s)]
        mine[r, p] = (mine[r, p].astype(F32) + far[r].astype(F32)).astype(BF)
        got_near.append(push(mine.at[r], near.at[r], at_z(s), near.at[r]))

    got_v()
    vs[...] = vp[...] + vec[...]
    waits = [push(vs.at[wrap(x + d)], vx.at[k], at(d, 0), vx.at[k]) for k, d in enumerate((1, -1, 2))]

    for flag, to in ((0, up), (1, down)):

        @only(receiver & (zl == flag))
        def _():
            for cp in early(to):
                cp.wait_recv()
            theirs = 1 - flag
            rbuf[0] = (rws[halves[theirs]].astype(F32) + rfar[theirs].astype(F32)).astype(BF)
            copy(rbuf.at[0], rbuf.at[1], r_mid, to).start()

    for w in waits:
        w()
    vy[...] = vs[x] + vx[0] + vx[1] + vx[2]
    waits = [push(vy.at[wrap(y + d)], vq.at[k], at(0, d), vq.at[k]) for k, d in enumerate((1, -1, 2))]

    for w in got_near:
        w()
    v = cols[:, z].astype(F32) + near[0].astype(F32) + near[1].astype(F32)
    total[...] = v.astype(BF).reshape(4, 4, 32, 448)
    a1[x] = total[x]
    got_x = [push(total.at[wrap(x + d)], a1.at[x], at(d, 0), a1.at[wrap(x - d)]) for d in (1, -1, 2)]

    for w in waits:
        w()
    vz[...] = vy[y] + vq[0] + vq[1] + vq[2]
    waits = [push(vz, vr.at[k], at_z(d), vr.at[k]) for k, d in enumerate((1, -1, 2))]

    for flag, to in ((0, up), (1, down)):

        @only(receiver & (zl == flag))
        def _():
            h = halves[flag]
            copy(rbuf.at[0], rbuf.at[1], r_mid, to).wait()
            v = rws[h].astype(F32) + rfar[flag].astype(F32) + rbuf[1].astype(F32)
            rows_out[h] = v.astype(BF)
            copy(rows_out.at[h], rows_out.at[h], r_twin, to).start()
            copy(rows_out.at[h], rows_out.at[h], r_core[0], other).start()

    for w in got_x:
        w()
    cols_out[c, zl, :, y] = a1[:, y]
    got_y = [
        push(a1.at[:, wrap(y + d)], cols_out.at[c, zl, :, y], at(0, d), cols_out.at[c, zl, :, wrap(y - d)])
        for d in (1, -1, 2)
    ]
    for w in waits:
        w()
    vec_out[...] = vz[...] + vr[0] + vr[1] + vr[2]
    for w in got_y:
        w()
    block = cols_out.at[c, zl]
    got_core = [push(block, block, other, cols_out.at[1 - c, zl])]
    push(block, block, twin, cols_out.at[c, 1 - zl])()
    block = cols_out.at[c, 1 - zl]
    got_core.append(push(block, block, other, cols_out.at[1 - c, 1 - zl]))

    for flag, to in ((0, up), (1, down)):
        h, g = halves[flag], halves[1 - flag]

        @only(receiver & (zl == flag))
        def _():
            copy(rows_out.at[g], rows_out.at[g], r_twin, to).wait_recv()
            copy(rows_out.at[g], rows_out.at[g], r_core[1], other).start()
            copy(rows_out.at[h], rows_out.at[h], r_twin, to).wait_send()
            copy(rows_out.at[h], rows_out.at[h], r_core[0], other).wait_send()
            copy(rows_out.at[g], rows_out.at[g], r_core[1], other).wait_send()

        @only((c != zh) & (zl == flag))
        def _():
            for cp in early(to):
                cp.wait_send()
            copy(rows_out.at[h], rows_out.at[h], r_core[0], other).wait_recv()
            copy(rows_out.at[g], rows_out.at[g], r_core[1], other).wait_recv()

    for w in got_core:
        w()
    for cp in started:
        cp.wait_send()


def grads(cols, rws, vec):
    dma = pltpu.SemaphoreType.DMA

    def vmem(*shape, t=BF):
        return pltpu.VMEM(shape, t)

    return pl.pallas_call(
        grads_kernel,
        out_shape=[
            jax.ShapeDtypeStruct((2, 2, 4, 4, 32, 448), BF),
            jax.ShapeDtypeStruct((320, WIDTH), BF),
            jax.ShapeDtypeStruct((16, 128), F32),
        ],
        in_specs=[VM] * 3,
        out_specs=[VM] * 3,
        scratch_shapes=[
            vmem(2, 8, 32, 448), vmem(2, 16, 32, 448), vmem(2, 16, 32, 448), vmem(4, 4, 32, 448),
            vmem(4, 4, 32, 448), vmem(2, 160, WIDTH), vmem(2, 160, WIDTH), vmem(4, 4, 16, 128, t=F32),
            vmem(4, 4, 16, 128, t=F32), vmem(3, 4, 16, 128, t=F32), vmem(4, 16, 128, t=F32),
            vmem(3, 16, 128, t=F32), vmem(16, 128, t=F32), vmem(3, 16, 128, t=F32), dma((40,)), dma((40,)),
        ],
        compiler_params=pltpu.CompilerParams(
            collective_id=4, has_side_effects=True, vmem_limit_bytes=60 * 2**20
        ),
    )(cols, rws, vec)


def finish_kernel(cols, rws, g_qkv, g_in, g_out, g_back):
    g_back[...] = rws[0:256].astype(F32)
    g_out[...] = rws[256:320].astype(F32)

    def one(p, _):
        for h in (0, 1):
            r = pl.ds(32 * h, 32)
            a, b = cols[0, h, p].astype(F32), cols[1, h, p].astype(F32)
            g_in[r, pl.ds(pl.multiple_of(p * 512, 512), 256)] = a[:, 0:256]
            g_in[r, pl.ds(pl.multiple_of(p * 512 + 256, 256), 256)] = b[:, 0:256]
            for m in range(3):
                k = 256 + 64 * m
                both = jnp.concatenate([a[:, k : k + 64], b[:, k : k + 64]], axis=1)
                g_qkv[r, pl.ds(pl.multiple_of(m * WIDTH + p * 128, 128), 128)] = both
        return 0

    lax.fori_loop(0, 16, one, 0)


def finish(cols, rws):
    def arr(*shape):
        return jax.ShapeDtypeStruct(shape, F32)

    return pl.pallas_call(
        finish_kernel,
        out_shape=[arr(64, 6144), arr(64, 8192), arr(64, WIDTH), arr(256, WIDTH)],
        in_specs=[VM] * 2,
        out_specs=[VM] * 4,
        compiler_params=pltpu.CompilerParams(vmem_limit_bytes=60 * 2**20),
    )(cols, rws)


def layer_norm(tokens, gain, shift):
    mean = jnp.mean(tokens, axis=-1, keepdims=True)
    centred = tokens - mean
    var = jnp.mean(centred * centred, axis=-1, keepdims=True)
    return centred * lax.rsqrt(var + eps_norm) * gain + shift


def swap_planes(v):
    return lax.ppermute(v, "shard", [(j, j ^ 1) for j in range(32)])


def body(
    tokens,
    span_order,
    ln_gain,
    ln_bias,
    qkv_weight,
    qkv_bias,
    out_weight,
    out_bias,
    fc1_weight,
    fc1_bias,
    fc2_weight,
    fc2_bias,
    cotangent,
):
    x, y, zh, zl, c = place()
    me = (x * 4 + y) * 2 + c

    tok = tokens.reshape(128, WIDTH)
    g_own = cotangent.reshape(128, WIDTH)
    own = [ln_gain, ln_bias, out_bias, fc2_bias, qkv_bias, jnp.zeros((64,), BF), fc1_bias]
    own = [v.astype(F32) for v in own] + [span_order.reshape(32).astype(F32), jnp.zeros((224,), F32)]
    small = jnp.concatenate(own).reshape(8, 128)
    n_all, g_all, fields, active, d_hidden, cols_t, rows_w, small_all, small_other = front(
        tok, g_own, small, qkv_weight, fc1_weight, out_weight, fc2_weight
    )
    small_all = small_all.reshape(32, 8, 128)
    gain, shift = small_all[:, 0, :64].reshape(WIDTH), small_all[:, 0, 64:].reshape(WIDTH)
    b_sum = (small_all[:, 1, :64] + small_all[:, 1, 64:]).reshape(WIDTH)
    order = jnp.where(c == zh, span_order.reshape(32), small_other[6, :32].astype(jnp.int32))

    done = attend(order, fields.reshape(32, 128, 256)).reshape(16, 2, 128, 256)
    keep = lax.dynamic_index_in_dim(done, zh, 1, keepdims=False)
    came = swap_planes(lax.dynamic_index_in_dim(done, 1 - zh, 1, keepdims=False))
    pair = (jnp.where(zh == 0, keep, came), jnp.where(zh == 0, came, keep))
    done = jnp.stack(pair, axis=1).reshape(32, 128, 256)

    left = jnp.concatenate([active, done[..., :64]], axis=-1)
    right = jnp.concatenate([d_hidden, done[..., 64:]], axis=-1)
    branch = summed(left, rows_w, 2)
    d_normed = summed(right, cols_t, 3)
    flat = tok.astype(F32)
    block_out = (flat + branch + b_sum).astype(BF).reshape(1, 128, WIDTH)
    _, norm_pull = jax.vjp(layer_norm, flat, gain, shift)
    d_flat, d_gain, d_shift = norm_pull(d_normed)
    d_tokens = (g_own.astype(F32) + d_flat).astype(BF).reshape(1, 128, WIDTH)

    outer = (((0,), (0,)), ((), ()))
    left, right = left.reshape(LENGTH, 320), right.reshape(LENGTH, 448)
    g_cols = lax.dot_general(n_all.reshape(LENGTH, WIDTH), right, outer, preferred_element_type=F32)
    g_rows = lax.dot_general(left, g_all.reshape(LENGTH, WIDTH), outer, preferred_element_type=F32)
    sums = jnp.sum(right.astype(F32), axis=0)
    bq = jnp.zeros((3, HEADS, 64), F32)
    bq = lax.dynamic_update_slice_in_dim(bq, sums[256:].reshape(3, 1, 64), me, 1).reshape(32, 192)
    bi = jnp.zeros((HEADS, 256), F32)
    bi = lax.dynamic_update_slice_in_dim(bi, sums[None, :256], me, 0)
    bo = jnp.sum(g_own.astype(F32), axis=0)
    vec = [v.reshape(32, 64) for v in (d_gain, d_shift, bo)] + [bq, bi, jnp.zeros((32, 384), F32)]
    vec = jnp.concatenate(vec, axis=1).reshape(4, 4, 16, 128)
    cols, rws, vec = grads(g_cols.astype(BF).reshape(16, 4, 32, 448), g_rows.astype(BF), vec)
    g_qkv, g_in, g_out, g_back = finish(cols.reshape(2, 2, 16, 32, 448), rws)
    vec = lax.dynamic_index_in_dim(vec.reshape(2, 1024), zh, 0, keepdims=False)
    return (
        block_out,
        d_tokens,
        vec[:64],
        vec[64:128],
        g_qkv,
        vec[192:384],
        g_out,
        vec[128:192],
        g_in,
        vec[384:640],
        g_back,
        vec[128:192],
    )


def solution(mesh):
    act, rows, vec = P("rep", "shard", None), P("shard", None), P("shard")
    return jax.shard_map(
        body,
        mesh=mesh,
        in_specs=(act, P("rep", None), vec, vec, rows, vec, rows, vec, rows, vec, rows, vec, act),
        out_specs=(act, act, vec, vec, rows, vec, rows, vec, rows, vec, rows, vec),
        check_vma=False,
    )
```

```python
import jax
import jax.numpy as jnp
from jax import lax
from jax.experimental import pallas as pl
from jax.experimental.pallas import tpu as pltpu
from jax.sharding import PartitionSpec as P

F32 = jnp.float32
BF = jnp.bfloat16
MESH = pl.DeviceIdType.MESH
HEADS = 32
WIDTH = 2048
LENGTH = 4096
TILE = 512
eps_norm = 1e-05
rope_base = 10000.0
negative = -1e30
VM = pl.BlockSpec(memory_space=pltpu.VMEM)
ANY = pl.BlockSpec(memory_space=pl.ANY)


def place():
    rep = lax.axis_index("rep")
    sh = lax.axis_index("shard")
    return sh // 8, (sh // 2) % 4, sh % 2, rep // 2, rep % 2


def spot(x, y, zh, zl, c):
    return (zl * 2 + c, (x * 4 + y) * 2 + zh)


def remote(src, dst, send, recv, to):
    return pltpu.make_async_remote_copy(
        src_ref=src, dst_ref=dst, send_sem=send, recv_sem=recv, device_id=to, device_id_type=MESH
    )


def greet(peers):
    barrier = pltpu.get_barrier_semaphore()
    for d in peers:
        pl.semaphore_signal(barrier, inc=1, device_id=d, device_id_type=MESH)
    pl.semaphore_wait(barrier, len(peers))


OFFS = [(p, q) for p in (0, -1, 1, 2) for q in (0, -1, 1, 2)]
GROUP = {0: 0, -1: 1, 1: 2, 2: 3}


LEVELS = (
    ((0, 0),),
    ((-1, 0), (1, 0), (0, -1), (0, 1)),
    ((2, 0), (0, 2), (-1, -1), (-1, 1), (1, -1), (1, 1)),
    ((-1, 2), (1, 2), (2, -1), (2, 1)),
    ((2, 2),),
)
N_LINK = 20
N_MORE = 110


def gelu_both(u):
    k0, k1 = 0.7978845608028654, 0.044715
    sq = u * u
    t = jnp.tanh(k0 * u * (1.0 + k1 * sq))
    half = 0.5 * (1.0 + t)
    return u * half, half + 0.5 * u * (1.0 - t * t) * k0 * (1.0 + 3.0 * k1 * sq)


def front_kernel(
    tok, g_own, small, w_qkv, w_in, w_out, w_back,
    n_all, g_all, fields, active, d_hidden, cols_t, rows_w, small_all, small_other,
    n_own, buf, d_act, d_att, f_send, w_f, w_m, w_ot, w_bt, wf1, wq1, wf2, wq2, table, bq,
    send, recv, psend, precv, msend, mrecv, fsem_s, fsem_r, loc, lsem,
):
    x, y, zh, zl, c = place()
    z = zh * 2 + zl
    other = spot(x, y, zh, zl, 1 - c)

    def at(dx, dy):
        return spot((x + dx + 4) % 4, (y + dy + 4) % 4, zh, zl, c)

    def at_z(dz):
        w = (z + dz + 4) % 4
        return spot(x, y, w // 2, w % 2, c)

    def dev(half, da, db):
        return at(da, db) if half == 0 else at(db, da)

    def slot(half, da, db, core):
        dx, dy = (da, db) if half == 0 else (db, da)
        return (((x + dx + 4) % 4) * 4 + (y + dy + 4) % 4) * 2 + core

    def rows(half, part):
        return pl.ds(half * 64 + (32 if part == 2 else 0), 64 if part == 0 else 32)

    greet([at(1, 0), at(-1, 0), at(2, 0), at(0, 1), at(0, -1), at(0, 2), at_z(1), at_z(-1), at_z(2), other])
    started = []
    ins = (g_own, n_own)
    outs = (g_all, n_all)
    counter = [0]

    def go(cp):
        cp.start()
        started.append(cp)

    def new():
        counter[0] += 1
        return counter[0] - 1

    def push(src, dst, to, land):
        i = new()
        go(remote(src, dst, msend.at[i], mrecv.at[i], to))
        return lambda: remote(land, land, msend.at[i], mrecv.at[i], to).wait_recv()

    def wrap(v):
        return (v + 4) % 4

    small_all[x, y, zh] = small[...]
    got = [push(small, small_other, other, small_other)]
    waits = []
    for d in (1, -1, 2):
        waits.append(
            push(small, small_all.at[x, y, zh], at(d, 0), small_all.at[wrap(x - d), y, zh])
        )

    def pass_on(a, h, role, off, part, to, own=False):
        s, r = slot(h, *off, c), rows(h, part)
        src = ins[a].at[r] if own else outs[a].at[s, r]
        go(remote(src, outs[a].at[s, r], send.at[a, h, role], recv.at[a, h, role], dev(h, *to)))

    def arrived(a, h, role, off, part):
        ref = outs[a].at[slot(h, *off, c), rows(h, part)]
        remote(ref, ref, send.at[a, h, role], recv.at[a, h, role], other).wait_recv()

    def share(a, h, off, own=False):
        i = OFFS.index(off)
        s, r = slot(h, *off, c), rows(h, 0)
        src = ins[a].at[r] if own else outs[a].at[s, r]
        go(remote(src, outs[a].at[s, r], psend.at[a, h, i], precv.at[a, h, i], other))

    def second(a, h, ao, own=False):
        k = GROUP[ao]
        pass_on(a, h, 4 + 2 * k, (ao, 0), 0, (0, 1), own)
        pass_on(a, h, 5 + 2 * k, (ao, 0), 0, (0, -1), own)

    def near(a, h, ao):
        k = GROUP[ao]
        arrived(a, h, 4 + 2 * k, (ao, -1), 0)
        pass_on(a, h, 12 + 2 * k, (ao, -1), 1, (0, 1))
        share(a, h, (ao, -1))
        arrived(a, h, 5 + 2 * k, (ao, 1), 0)
        pass_on(a, h, 13 + 2 * k, (ao, 1), 2, (0, -1))
        share(a, h, (ao, 1))

    def far(a, h, ao):
        k = GROUP[ao]
        arrived(a, h, 12 + 2 * k, (ao, 2), 1)
        arrived(a, h, 13 + 2 * k, (ao, 2), 2)
        share(a, h, (ao, 2))

    def begin(a):
        cp = pltpu.make_async_copy(ins[a], outs[a].at[slot(0, 0, 0, c)], loc.at[a])
        cp.start()
        for h in (0, 1):
            pass_on(a, h, 0, (0, 0), 0, (1, 0), True)
            pass_on(a, h, 1, (0, 0), 0, (-1, 0), True)
        for h in (0, 1):
            second(a, h, 0, True)
            share(a, h, (0, 0), True)
        return cp

    def level(a, n):
        for h in (0, 1):
            if n == 1:
                arrived(a, h, 0, (-1, 0), 0)
                pass_on(a, h, 2, (-1, 0), 1, (1, 0))
                second(a, h, -1)
                share(a, h, (-1, 0))
                arrived(a, h, 1, (1, 0), 0)
                pass_on(a, h, 3, (1, 0), 2, (-1, 0))
                second(a, h, 1)
                share(a, h, (1, 0))
                near(a, h, 0)
            if n == 2:
                arrived(a, h, 2, (2, 0), 1)
                arrived(a, h, 3, (2, 0), 2)
                second(a, h, 2)
                share(a, h, (2, 0))
                near(a, h, -1)
                near(a, h, 1)
                far(a, h, 0)
            if n == 3:
                near(a, h, 2)
                far(a, h, -1)
                far(a, h, 1)
            if n == 4:
                far(a, h, 2)

    held = [begin(0)]

    mine = pl.ds(pl.multiple_of(zl * 32, 32), 32)

    def col_copies(dx):
        xx = wrap(x + dx)
        for yy in range(4):
            t = (xx * 4 + yy) * 2 + c
            yield (
                w_in.at[mine, pl.ds(pl.multiple_of(t * 256, 256), 256)], wf1.at[yy, x], wf1.at[yy, wrap(x - dx)],
            )
            for m in range(3):
                lanes = pl.ds(pl.multiple_of(m * WIDTH + (xx * 4 + yy) * 128, 128), 128)
                yield w_qkv.at[mine, lanes], wq1.at[yy, x, m], wq1.at[yy, wrap(x - dx), m]

    mates = []
    for i, (src, dst, _) in enumerate(col_copies(0)):
        cp = pltpu.make_async_copy(src, dst, lsem.at[i])
        cp.start()
        mates.append(cp)
    for d in (1, -1, 2):
        for src, dst, land in col_copies(d):
            waits.append(push(src, dst, at(d, 0), land))

    ri = new(), new()
    to_row = spot(x, y, 1 - zh, 1 - zl, c)

    def row_copies():
        for i, src, part in ((0, w_back, pl.ds(0, 256)), (1, w_out, pl.ds(256, 64))):
            yield remote(src, rows_w.at[part], msend.at[ri[i]], mrecv.at[ri[i]], to_row), pltpu.make_async_copy(
                src, rows_w.at[part], lsem.at[16 + i]
            )

    @pl.when(c == zh)
    def _():
        for far_copy, near_copy in row_copies():
            far_copy.start()
            near_copy.start()

    for w in waits[:3]:
        w()
    waits = waits[3:]
    more = []
    for d in (1, -1, 2):
        more.append(
            push(small_all.at[:, y, zh], small_all.at[:, y, zh], at(0, d), small_all.at[:, wrap(y - d), zh])
        )
    for w in more:
        w()
    push(small_all.at[:, :, zh], small_all.at[:, :, zh], at_z(2), small_all.at[:, :, 1 - zh])()
    got[0]()
    for j in range(32):
        piece = small_all[j // 8, (j // 2) % 4, j % 2]
        for i in (0, 1):
            table[pl.ds(i, 1), pl.ds(64 * j, 64)] = piece[0:1, 64 * i : 64 * i + 64]
        for i in range(3):
            bq[pl.ds(3 * j + i, 1), 0:64] = piece[2 + i // 2 : 3 + i // 2, 64 * (i % 2) : 64 * (i % 2) + 64]

    def norm(i, _):
        r = pl.ds(pl.multiple_of(i * 32, 32), 32)
        v = tok[r, :].astype(F32)
        v = v - jnp.mean(v, axis=-1, keepdims=True)
        v = v * lax.rsqrt(jnp.mean(v * v, axis=-1, keepdims=True) + eps_norm)
        n_own[r, :] = (v * table[0:1, :] + table[1:2, :]).astype(BF)
        return 0

    lax.fori_loop(0, 4, norm, 0)
    held.append(begin(1))

    for w in waits:
        w()
    for cp in mates:
        cp.wait()
    waits = []
    for d in (1, -1, 2):
        yy = wrap(y + d)
        waits.append(push(wf1.at[yy], wf2.at[:, y, z], at(0, d), wf2.at[:, wrap(y - d), z]))
        waits.append(push(wq1.at[yy], wq2.at[:, :, y, z], at(0, d), wq2.at[:, :, wrap(y - d), z]))
    wf2[:, y, z] = wf1[y]
    wq2[:, :, y, z] = wq1[y]
    level(0, 1)
    for w in waits:
        w()
    waits = []
    for s in (1, -1):
        waits.append(push(wf2.at[:, :, z], wf2.at[:, :, z], at_z(s), wf2.at[:, :, wrap(z - s)]))
        waits.append(push(wq2.at[:, :, :, z], wq2.at[:, :, :, z], at_z(s), wq2.at[:, :, :, wrap(z - s)]))

    @pl.when(c == zh)
    def _():
        for _, near_copy in row_copies():
            near_copy.wait()

    @pl.when(c != zh)
    def _():
        for far_copy, _ in row_copies():
            far_copy.wait_recv()

    def turn_rows(i, _):
        r = pl.ds(pl.multiple_of(i * 256, 256), 256)
        w_bt[r, :] = rows_w[0:256, r].astype(F32).T.astype(BF)
        w_ot[r, :] = rows_w[256:320, r].astype(F32).T.astype(BF)
        return 0

    lax.fori_loop(0, 8, turn_rows, 0)

    def pass_columns():
        for w in waits:
            w()
        waits.clear()
        for s, k in ((1, 0), (-1, 2)):
            zz, part, far_z = wrap(z - s), pl.ds(k, 2), wrap(z + 2)
            waits.append(push(wf2.at[part, :, zz], wf2.at[part, :, zz], at_z(s), wf2.at[part, :, far_z]))
            waits.append(
                push(wq2.at[part, :, :, zz], wq2.at[part, :, :, zz], at_z(s), wq2.at[part, :, :, far_z])
            )

    def take_columns():
        for w in waits:
            w()
        waits.clear()
        for xx in range(4):
            r = pl.ds(xx * 512, 512)
            w_f[r, :] = wf2[xx].reshape(512, 256)
            for m in range(3):
                v = wq2[xx, m].reshape(512, 128)
                w_m[r, 64 * m : 64 * m + 64] = jnp.where(c == 0, v[:, 0:64], v[:, 64:128])

        def turn_cols(i, _):
            r = pl.ds(pl.multiple_of(i * 256, 256), 256)
            cols_t[0:256, r] = w_f[r, :].astype(F32).T.astype(BF)
            cols_t[256:448, r] = w_m[r, :].astype(F32).T.astype(BF)
            return 0

        lax.fori_loop(0, 8, turn_cols, 0)

    t = (x * 4 + y) * 2 + c
    here = small_all[x, y, c]
    b_in = jnp.concatenate([here[4:5, :], here[5:6, :]], axis=1)
    b_m = jnp.concatenate([bq[pl.ds(t + 32 * m, 1), 0:64] for m in range(3)], axis=1)

    queue = []
    step = [0]

    def pair(off):
        return ((x + off[0] + 4) % 4) * 4 + (y + off[1] + 4) % 4

    def fetch(a, off):
        p = pair(off)
        for h in (0, 1):
            i = OFFS.index(off if h == 0 else (off[1], off[0]))
            ref = outs[a].at[p * 2 + 1 - c, rows(h, 0)]
            remote(ref, ref, psend.at[a, h, i], precv.at[a, h, i], other).wait_recv()
        if off == (0, 0):
            held[a].wait()
        k = step[0] % 2
        step[0] += 1
        cp = pltpu.make_async_copy(outs[a].at[pl.ds(p * 2, 2)], buf.at[k], loc.at[2 + k])
        cp.start()
        return a, p, k, cp

    def run(job):
        a, p, k, cp = job
        cp.wait()
        two = pl.ds(p * 2, 2)

        def over(wa, wb, na, nb):
            def inner(i, carry):
                va, vb = carry
                cs = pl.ds(pl.multiple_of(i * 512, 512), 512)
                v = buf[k, :, :, cs].reshape(256, 512)
                return va + dot(v, wa[cs, :]), vb + dot(v, wb[cs, :])

            return lax.fori_loop(0, 4, inner, (jnp.zeros((256, na), F32), jnp.zeros((256, nb), F32)))

        if a == 0:
            da, do = over(w_bt, w_ot, 256, 64)
            d_act[two] = da.reshape(2, 128, 256)
            d_att[two] = do.astype(BF).reshape(2, 128, 64)
            return
        hidden, mixed = over(w_f, w_m, 256, 192)
        act, slope = gelu_both(hidden + b_in)
        active[two] = act.astype(BF).reshape(2, 128, 256)
        d_hidden[two] = (d_act[two].reshape(256, 256) * slope).astype(BF).reshape(2, 128, 256)
        mixed = (mixed + b_m).astype(BF).reshape(2, 128, 192)
        f_send[p, :, :, 0:192] = mixed
        f_send[p, :, :, 192:256] = d_att[two]
        fields[p, zh] = f_send[p, zh]
        go(remote(f_send.at[p, 1 - zh], fields.at[p, zh], fsem_s.at[p], fsem_r.at[p], at_z(2)))

    def compute(a, offs):
        for off in offs:
            queue.append(fetch(a, off))
            while len(queue) > 1:
                run(queue.pop(0))

    compute(0, LEVELS[0])
    pass_columns()
    level(0, 2)
    compute(0, LEVELS[1])
    level(1, 1)
    take_columns()
    level(0, 3)
    compute(0, LEVELS[2])
    level(1, 2)
    compute(1, LEVELS[0])
    level(0, 4)
    compute(0, LEVELS[3])
    compute(1, LEVELS[1])
    level(1, 3)
    compute(0, LEVELS[4])
    compute(1, LEVELS[2])
    level(1, 4)
    compute(1, LEVELS[3])
    compute(1, LEVELS[4])
    while queue:
        run(queue.pop(0))

    def came(p, _):
        ref = fields.at[p, 1 - zh]
        remote(ref, ref, fsem_s.at[p], fsem_r.at[p], other).wait_recv()
        return 0

    lax.fori_loop(0, 16, came, 0)
    for cp in started:
        cp.wait_send()

    @pl.when(c == zh)
    def _():
        for far_copy, _ in row_copies():
            far_copy.wait_send()


def front(tok, g_own, small, w_qkv, w_in, w_out, w_back):
    dma = pltpu.SemaphoreType.DMA

    def vmem(*shape, t=BF):
        return pltpu.VMEM(shape, t)

    def arr(*shape, t=BF):
        return jax.ShapeDtypeStruct(shape, t)

    return pl.pallas_call(
        front_kernel,
        out_shape=[
            arr(32, 128, WIDTH), arr(32, 128, WIDTH), arr(16, 2, 128, 256), arr(32, 128, 256), arr(32, 128, 256),
            arr(448, WIDTH), arr(320, WIDTH), arr(4, 4, 2, 8, 128, t=F32), arr(8, 128, t=F32),
        ],
        in_specs=[VM, ANY, VM, ANY, ANY, ANY, ANY],
        out_specs=[ANY, ANY, VM, VM, VM, VM, VM, VM, VM],
        scratch_shapes=[
            vmem(128, WIDTH), vmem(2, 2, 128, WIDTH), vmem(32, 128, 256, t=F32), vmem(32, 128, 64),
            vmem(16, 2, 128, 256), vmem(WIDTH, 256), vmem(WIDTH, 192), vmem(WIDTH, 64), vmem(WIDTH, 256),
            vmem(4, 4, 32, 256), vmem(4, 4, 3, 32, 128), vmem(4, 4, 4, 32, 256), vmem(4, 3, 4, 4, 32, 128),
            vmem(8, WIDTH, t=F32), vmem(96, 128, t=F32),
            dma((2, 2, 20)), dma((2, 2, 20)), dma((2, 2, 16)), dma((2, 2, 16)), dma((N_MORE,)), dma((N_MORE,)),
            dma((16,)), dma((16,)), dma((4,)), dma((18,)),
        ],
        compiler_params=pltpu.CompilerParams(
            collective_id=1, has_side_effects=True, vmem_limit_bytes=60 * 2**20
        ),
    )(tok, g_own, small, w_qkv, w_in, w_out, w_back)


def dot(a, b):
    return jnp.dot(a, b, preferred_element_type=F32)


def spin(v, cos, sin):
    a, b = v[0:16], v[16:32]
    return jnp.concatenate([a * cos - b * sin, b * cos + a * sin, v[32:]], axis=0)


def attend_kernel(
    order, x_ref, cos_ref, sin_ref, out_ref, q_n, k_n, v_n, q_t, k_t, v_t, do_t, s_buf, p_buf, dk, dv, fin
):
    def load(b, _):
        here = pl.ds(pl.multiple_of(order[b] * 128, 128), 128)
        t = x_ref[b].astype(F32).T
        cos, sin = cos_ref[:, here], sin_ref[:, here]
        q = spin(t[0:64], cos, sin) * 0.125
        k = spin(t[64:128], cos, sin)
        q_t[:, here] = q.astype(BF)
        k_t[:, here] = k.astype(BF)
        v_t[:, here] = t[128:192].astype(BF)
        do_t[:, here] = t[192:256].astype(BF)
        q_n[here, :] = q.T.astype(BF)
        k_n[here, :] = k.T.astype(BF)
        v_n[here, :] = x_ref[b][:, 128:192]
        return 0

    lax.fori_loop(0, 32, load, 0)
    dk[...] = jnp.zeros_like(dk)
    dv[...] = jnp.zeros_like(dv)
    square = (TILE, TILE)
    allowed = lax.broadcasted_iota(jnp.int32, square, 0) <= lax.broadcasted_iota(jnp.int32, square, 1)
    for i in range(LENGTH // TILE):
        qs = pl.ds(i * TILE, TILE)
        qt, qn, do = q_t[:, qs], q_n[qs, :], do_t[:, qs].astype(F32)

        def first(j, top):
            ks = pl.ds(pl.multiple_of(j * TILE, TILE), TILE)
            s = dot(k_n[ks, :], qt)
            s_buf[ks, :] = s
            return jnp.maximum(top, jnp.max(s, axis=0, keepdims=True))

        top = jnp.full((1, TILE), negative, F32)
        if i:
            top = lax.fori_loop(0, i, first, top)
        s = jnp.where(allowed, dot(k_n[qs, :], qt), negative)
        s_buf[qs, :] = s
        top = jnp.maximum(top, jnp.max(s, axis=0, keepdims=True))

        def second(j, carry):
            total, o = carry
            ks = pl.ds(pl.multiple_of(j * TILE, TILE), TILE)
            p = jnp.exp(s_buf[ks, :] - top)
            pb = p.astype(BF)
            p_buf[ks, :] = pb
            return total + jnp.sum(p, axis=0, keepdims=True), o + dot(v_t[:, ks], pb)

        total, o = lax.fori_loop(
            0, i + 1, second, (jnp.zeros((1, TILE), F32), jnp.zeros((64, TILE), F32))
        )
        inv = 1.0 / total
        o = o * inv
        do = do * inv
        delta = jnp.sum(do * o, axis=0, keepdims=True)
        dt = do.astype(BF)
        dn = do.T.astype(BF)

        def third(j, dq):
            ks = pl.ds(pl.multiple_of(j * TILE, TILE), TILE)
            dp = dot(v_n[ks, :], dt)
            pb = p_buf[ks, :]
            ds = (pb.astype(F32) * (dp - delta)).astype(BF)
            dk[ks, :] += dot(ds, qn)
            dv[ks, :] += dot(pb, dn)
            return dq + dot(k_t[:, ks], ds)

        dq = lax.fori_loop(0, i + 1, third, jnp.zeros((64, TILE), F32))
        fin[0:64, qs] = o
        fin[64:128, qs] = spin(dq, cos_ref[:, qs], -sin_ref[:, qs]) * 0.125

    def store(b, _):
        here = pl.ds(pl.multiple_of(order[b] * 128, 128), 128)
        k = spin(dk[here, :].T, cos_ref[:, here], -sin_ref[:, here])
        t = jnp.concatenate([fin[:, here], k, dv[here, :].T], axis=0)
        out_ref[b] = t.T.astype(BF)
        return 0

    lax.fori_loop(0, 32, store, 0)


def attend(order, x):
    freq = rope_base ** (-(jnp.arange(16, dtype=F32) * 2.0 / 32))
    angle = jnp.arange(LENGTH, dtype=F32)[None, :] * freq[:, None]
    natural, turned = pltpu.VMEM((LENGTH, 64), BF), pltpu.VMEM((64, LENGTH), BF)
    return pl.pallas_call(
        attend_kernel,
        out_shape=jax.ShapeDtypeStruct((32, 128, 256), BF),
        in_specs=[pl.BlockSpec(memory_space=pltpu.SMEM), VM, VM, VM],
        out_specs=VM,
        scratch_shapes=[natural] * 3
        + [turned] * 4
        + [pltpu.VMEM((LENGTH, TILE), F32), pltpu.VMEM((LENGTH, TILE), BF)]
        + [pltpu.VMEM((LENGTH, 64), F32)] * 2
        + [pltpu.VMEM((128, LENGTH), F32)],
        compiler_params=pltpu.CompilerParams(vmem_limit_bytes=60 * 2**20),
    )(order, x, jnp.cos(angle), jnp.sin(angle))


TURN = [(2, 2), (1, 2), (3, 2), (0, 2), (2, 1), (2, 3), (2, 0), (1, 1)]
TURN += [(1, 3), (3, 1), (3, 3), (0, 1), (0, 3), (1, 0), (3, 0), (0, 0)]


def back_kernel(
    done, active, d_hidden, rows_w, cols_t, n_all, g_all, branch, d_normed, g_cols, g_rows, sums,
    m_all, psend, acc, far, near, gsum, buf, ps, pr, send, recv, xs, xr, loc,
):
    x, y, zh, zl, c = place()
    z = zh * 2 + zl
    other = spot(x, y, zh, zl, 1 - c)
    beyond = spot(x, y, 1 - zh, zl, c)

    def dev(half, da, db):
        dx, dy = (da, db) if half == 0 else (db, da)
        return spot((x + dx + 4) % 4, (y + dy + 4) % 4, zh, zl, c)

    def rows(half, part):
        return pl.ds(half * 64 + (32 if part == 2 else 0), 64 if part == 0 else 32)

    greet([dev(0, 1, 0), dev(0, -1, 0), dev(0, 0, 1), dev(0, 0, -1), other, beyond])
    started = []

    def go(cp):
        cp.start()
        started.append(cp)

    lanes = (pl.ds(0, 128), pl.ds(128, 128))
    for i, ls in enumerate(lanes):
        src, dst = done.at[:, 1 - zh, :, ls], m_all.at[:, zh, :, ls]
        go(remote(src, dst, xs.at[i], xr.at[i], beyond))
    m_all[:, zh] = done[:, zh]

    def exchanged(i):
        ref = m_all.at[:, 1 - zh, :, lanes[i]]
        remote(ref, ref, xs.at[i], xr.at[i], beyond).wait_recv()

    def products(src, lhs, height, begin, end, low=None):
        def load(p, k):
            return pltpu.make_async_copy(src.at[pl.ds(2 * p, 2)], buf.at[k], loc.at[k])

        load(begin, begin % 2).start()

        def one(p, _):
            k = lax.rem(p, 2)

            @pl.when(p + 1 < end)
            def _():
                load(p + 1, 1 - k).start()

            load(p, k).wait()
            block_of = lhs(p).astype(F32)
            turned = block_of.T.astype(BF)
            if low is not None:
                sums[0:1, low : low + height] += jnp.sum(block_of, axis=0, keepdims=True)

            def tile(t, _):
                cs = pl.ds(pl.multiple_of(t * TILE, TILE), TILE)
                v = dot(turned, buf[k, :, :, cs].reshape(256, TILE))
                gsum[0:height, cs] = jnp.where(p == 0, v, gsum[0:height, cs] + v)
                return 0

            lax.fori_loop(0, WIDTH // TILE, tile, 0)
            return 0

        lax.fori_loop(begin, end, one, 0)

    def hidden_part(ref):
        return lambda p: ref[pl.ds(2 * p, 2)].reshape(256, 256)

    def head_part(low, high):
        return lambda p: m_all[p, :, :, low:high].reshape(256, high - low)

    def left(p):
        return jnp.concatenate([hidden_part(active)(p), head_part(0, 64)(p)], axis=1)

    def put_cols(low, high):
        def one(i, _):
            r = pl.ds(pl.multiple_of(i * 256, 256), 256)
            g_cols[r, low:high] = gsum[0 : high - low, r].T.astype(BF)
            return 0

        lax.fori_loop(0, 8, one, 0)

    def step_to(h, g, s):
        return dev(h, 0, s) if g < 4 else dev(h, s, 0)

    def block(h, g, o):
        da, db = (g, o) if g < 4 else (o, 0)
        dx, dy = (da, db) if h == 0 else (db, da)
        return (dx % 4) * 4 + dy % 4

    def send_far(q, h, g):
        k = block(h, g, 2)
        for role, s in ((0, 1), (1, -1)):
            src, dst = acc.at[q, k, rows(h, role + 1)], far.at[q, h, g, role]
            go(remote(src, dst, send.at[q, h, g, role], recv.at[q, h, g, role], step_to(h, g, s)))

    def relay(q, h, g):
        for role, s in ((0, 1), (1, -1)):
            ref = far.at[q, h, g, role]
            remote(ref, ref, send.at[q, h, g, role], recv.at[q, h, g, role], other).wait_recv()
            k, r = block(h, g, s), rows(h, role + 1)
            acc[q, k, r] = (acc[q, k, r].astype(F32) + ref[...].astype(F32)).astype(BF)
            src, dst, i = acc.at[q, k, rows(h, 0)], near.at[q, h, g, role], 2 + role
            go(remote(src, dst, send.at[q, h, g, i], recv.at[q, h, g, i], step_to(h, g, s)))

    def land(q, h, g):
        k, r = block(h, g, 0), rows(h, 0)
        for role in (0, 1):
            ref = near.at[q, h, g, role]
            i = 2 + role
            remote(ref, ref, send.at[q, h, g, i], recv.at[q, h, g, i], other).wait_recv()
        tot = acc[q, k, r].astype(F32) + near[q, h, g, 0].astype(F32) + near[q, h, g, 1].astype(F32)
        if g < 4:
            acc[q, k, r] = tot.astype(BF)
        else:
            (branch, d_normed)[q][r] = tot

    def chip(n):
        dx, dy = TURN[n]
        return ((x + dx) % 4) * 4 + (y + dy) % 4

    def operands(q, p, core):
        if q == 0:
            return active[2 * p + core], m_all[p, core, :, 0:64], rows_w
        return d_hidden[2 * p + core], m_all[p, core, :, 64:256], cols_t

    sent = []

    def for_partner(q, n):
        k = TURN[n][0] * 4 + TURN[n][1]
        s = len(sent)
        if s >= 4:
            sent[s - 4].wait_send()
        a, b, w = operands(q, chip(n), 1 - c)

        def tile(t, _):
            cs = pl.ds(pl.multiple_of(t * TILE, TILE), TILE)
            psend[s % 4, :, cs] = (dot(a, w[0:256, cs]) + dot(b, w[256:, cs])).astype(BF)
            return 0

        lax.fori_loop(0, WIDTH // TILE, tile, 0)
        cp = remote(psend.at[s % 4], acc.at[q, k], ps.at[q, k], pr.at[q, k], other)
        cp.start()
        sent.append(cp)

    def for_own(q, n):
        dx, dy = TURN[n]
        k = dx * 4 + dy
        ref = acc.at[q, k]
        remote(ref, ref, ps.at[q, k], pr.at[q, k], other).wait_recv()
        a, b, w = operands(q, chip(n), c)

        def tile(t, _):
            cs = pl.ds(pl.multiple_of(t * TILE, TILE), TILE)
            v = dot(a, w[0:256, cs]) + dot(b, w[256:, cs])
            acc[q, k, :, cs] = (v + acc[q, k, :, cs].astype(F32)).astype(BF)
            return 0

        lax.fori_loop(0, WIDTH // TILE, tile, 0)
        if dy == 2:
            send_far(q, 0, dx)
        if dx == 2:
            send_far(q, 1, dy)

    sums[...] = jnp.zeros_like(sums)
    groups = [(h, g) for g in (2, 1, 3, 0) for h in (0, 1)]
    products(n_all, hidden_part(d_hidden), 256, 0, 16, 0)
    put_cols(0, 256)
    exchanged(0)
    for_partner(0, 0)
    for n in range(1, 16):
        for_partner(0, n)
        for_own(0, n - 1)
    for_own(0, 15)
    exchanged(1)
    for_partner(1, 0)
    for n in range(1, 16):
        for_partner(1, n)
        for_own(1, n - 1)
        if n >= 2 and n % 2 == 0 and n <= 14:
            relay(0, *groups[n // 2 - 1])
    relay(0, *groups[7])
    for_own(1, 15)
    for h, g in groups:
        relay(1, h, g)
    products(n_all, head_part(64, 256), 192, 0, 16, 256)
    put_cols(256, 448)
    for h, g in groups:
        land(0, h, g)
        if g == 2:
            send_far(0, h, 4)
    products(g_all, left, 320, 0, 8)
    for h in (0, 1):
        relay(0, h, 4)
    products(g_all, left, 320, 8, 16)
    g_rows[...] = gsum[...].astype(BF)
    for h, g in groups:
        land(1, h, g)
        if g == 2:
            send_far(1, h, 4)
    for h in (0, 1):
        land(0, h, 4)
    for h in (0, 1):
        relay(1, h, 4)
    for h in (0, 1):
        land(1, h, 4)
    for cp in sent[-4:]:
        cp.wait_send()
    for cp in started:
        cp.wait_send()


def back(done, active, d_hidden, rows_w, cols_t, n_all, g_all):
    dma = pltpu.SemaphoreType.DMA

    def vmem(*shape, t=BF):
        return pltpu.VMEM(shape, t)

    return pl.pallas_call(
        back_kernel,
        out_shape=[
            jax.ShapeDtypeStruct((128, WIDTH), F32),
            jax.ShapeDtypeStruct((128, WIDTH), F32),
            jax.ShapeDtypeStruct((WIDTH, 448), BF),
            jax.ShapeDtypeStruct((320, WIDTH), BF),
            jax.ShapeDtypeStruct((8, 448), F32),
        ],
        in_specs=[VM] * 5 + [ANY] * 2,
        out_specs=[VM] * 5,
        scratch_shapes=[
            vmem(16, 2, 128, 256), vmem(4, 128, WIDTH), vmem(2, 16, 128, WIDTH), vmem(2, 2, 5, 2, 32, WIDTH),
            vmem(2, 2, 5, 2, 64, WIDTH), vmem(320, WIDTH, t=F32), vmem(2, 2, 128, WIDTH),
            dma((2, 16)), dma((2, 16)), dma((2, 2, 5, 4)), dma((2, 2, 5, 4)), dma((2,)), dma((2,)), dma((2,)),
        ],
        compiler_params=pltpu.CompilerParams(
            collective_id=2, has_side_effects=True, vmem_limit_bytes=63 * 2**20
        ),
    )(done, active, d_hidden, rows_w, cols_t, n_all, g_all)


def grads_kernel(
    cols, rws, vec, cols_out, rows_out, vec_out,
    far, near, mine, total, a1, rfar, rbuf, vp, vs, vx, vy, vq, vz, vr, send, recv,
):
    x, y, zh, zl, c = place()
    z = zh * 2 + zl
    other = spot(x, y, zh, zl, 1 - c)
    started = []
    counter = [0]

    def wrap(v):
        return (v + 4) % 4

    def at(dx, dy):
        return spot(wrap(x + dx), wrap(y + dy), zh, zl, c)

    def at_z(dz):
        w = wrap(z + dz)
        return spot(x, y, w // 2, w % 2, c)

    twin = spot(x, y, zh, 1 - zl, c)
    greet([at(1, 0), at(-1, 0), at(2, 0), at(0, 1), at(0, -1), at(0, 2), at_z(1), at_z(-1), at_z(2), other])

    def new():
        counter[0] += 1
        return counter[0] - 1

    def copy(src, dst, i, to):
        return remote(src, dst, send.at[i], recv.at[i], to)

    def push(src, dst, to, land):
        i = new()
        cp = copy(src, dst, i, to)
        cp.start()
        started.append(cp)
        return lambda: copy(land, land, i, to).wait_recv()

    def only(test):
        return pl.when(test)

    zf = wrap(z + 2)
    parts = ((1, pl.ds(0, 8)), (-1, pl.ds(8, 8)))
    got_far = [push(cols.at[p, zf], far.at[r], at_z(s), far.at[r]) for r, (s, p) in enumerate(parts)]

    halves = (pl.ds(0, 160), pl.ds(160, 160))
    r_far, r_mid, r_twin, r_core = (new(), new()), new(), new(), (new(), new())
    down, up = at_z(-1), at_z(1)
    receiver = c == zh

    def early(to):
        return [copy(rws.at[halves[k]], rfar.at[k], r_far[k], to) for k in (0, 1)]

    for flag, to in ((0, down), (1, up)):

        @only((c != zh) & (zl == flag))
        def _():
            for cp in early(to):
                cp.start()

    got_v = push(vec, vp, other, vp)

    got_near = []
    for r, (s, p) in enumerate(parts):
        got_far[r]()
        mine[r] = cols[:, wrap(z + s)]
        mine[r, p] = (mine[r, p].astype(F32) + far[r].astype(F32)).astype(BF)
        got_near.append(push(mine.at[r], near.at[r], at_z(s), near.at[r]))

    got_v()
    vs[...] = vp[...] + vec[...]
    waits = [push(vs.at[wrap(x + d)], vx.at[k], at(d, 0), vx.at[k]) for k, d in enumerate((1, -1, 2))]

    for flag, to in ((0, up), (1, down)):

        @only(receiver & (zl == flag))
        def _():
            for cp in early(to):
                cp.wait_recv()
            theirs = 1 - flag
            rbuf[0] = (rws[halves[theirs]].astype(F32) + rfar[theirs].astype(F32)).astype(BF)
            copy(rbuf.at[0], rbuf.at[1], r_mid, to).start()

    for w in waits:
        w()
    vy[...] = vs[x] + vx[0] + vx[1] + vx[2]
    waits = [push(vy.at[wrap(y + d)], vq.at[k], at(0, d), vq.at[k]) for k, d in enumerate((1, -1, 2))]

    for w in got_near:
        w()
    v = cols[:, z].astype(F32) + near[0].astype(F32) + near[1].astype(F32)
    total[...] = v.astype(BF).reshape(4, 4, 32, 448)
    a1[x] = total[x]
    got_x = [push(total.at[wrap(x + d)], a1.at[x], at(d, 0), a1.at[wrap(x - d)]) for d in (1, -1, 2)]

    for w in waits:
        w()
    vz[...] = vy[y] + vq[0] + vq[1] + vq[2]
    waits = [push(vz, vr.at[k], at_z(d), vr.at[k]) for k, d in enumerate((1, -1, 2))]

    for flag, to in ((0, up), (1, down)):

        @only(receiver & (zl == flag))
        def _():
            h = halves[flag]
            copy(rbuf.at[0], rbuf.at[1], r_mid, to).wait()
            v = rws[h].astype(F32) + rfar[flag].astype(F32) + rbuf[1].astype(F32)
            rows_out[h] = v.astype(BF)
            copy(rows_out.at[h], rows_out.at[h], r_twin, to).start()
            copy(rows_out.at[h], rows_out.at[h], r_core[0], other).start()

    for w in got_x:
        w()
    cols_out[c, zl, :, y] = a1[:, y]
    got_y = [
        push(a1.at[:, wrap(y + d)], cols_out.at[c, zl, :, y], at(0, d), cols_out.at[c, zl, :, wrap(y - d)])
        for d in (1, -1, 2)
    ]
    for w in waits:
        w()
    vec_out[...] = vz[...] + vr[0] + vr[1] + vr[2]
    for w in got_y:
        w()
    block = cols_out.at[c, zl]
    got_core = [push(block, block, other, cols_out.at[1 - c, zl])]
    push(block, block, twin, cols_out.at[c, 1 - zl])()
    block = cols_out.at[c, 1 - zl]
    got_core.append(push(block, block, other, cols_out.at[1 - c, 1 - zl]))

    for flag, to in ((0, up), (1, down)):
        h, g = halves[flag], halves[1 - flag]

        @only(receiver & (zl == flag))
        def _():
            copy(rows_out.at[g], rows_out.at[g], r_twin, to).wait_recv()
            copy(rows_out.at[g], rows_out.at[g], r_core[1], other).start()
            copy(rows_out.at[h], rows_out.at[h], r_twin, to).wait_send()
            copy(rows_out.at[h], rows_out.at[h], r_core[0], other).wait_send()
            copy(rows_out.at[g], rows_out.at[g], r_core[1], other).wait_send()

        @only((c != zh) & (zl == flag))
        def _():
            for cp in early(to):
                cp.wait_send()
            copy(rows_out.at[h], rows_out.at[h], r_core[0], other).wait_recv()
            copy(rows_out.at[g], rows_out.at[g], r_core[1], other).wait_recv()

    for w in got_core:
        w()
    for cp in started:
        cp.wait_send()


def grads(cols, rws, vec):
    dma = pltpu.SemaphoreType.DMA

    def vmem(*shape, t=BF):
        return pltpu.VMEM(shape, t)

    return pl.pallas_call(
        grads_kernel,
        out_shape=[
            jax.ShapeDtypeStruct((2, 2, 4, 4, 32, 448), BF),
            jax.ShapeDtypeStruct((320, WIDTH), BF),
            jax.ShapeDtypeStruct((16, 128), F32),
        ],
        in_specs=[VM] * 3,
        out_specs=[VM] * 3,
        scratch_shapes=[
            vmem(2, 8, 32, 448), vmem(2, 16, 32, 448), vmem(2, 16, 32, 448), vmem(4, 4, 32, 448),
            vmem(4, 4, 32, 448), vmem(2, 160, WIDTH), vmem(2, 160, WIDTH), vmem(4, 4, 16, 128, t=F32),
            vmem(4, 4, 16, 128, t=F32), vmem(3, 4, 16, 128, t=F32), vmem(4, 16, 128, t=F32),
            vmem(3, 16, 128, t=F32), vmem(16, 128, t=F32), vmem(3, 16, 128, t=F32), dma((40,)), dma((40,)),
        ],
        compiler_params=pltpu.CompilerParams(
            collective_id=4, has_side_effects=True, vmem_limit_bytes=60 * 2**20
        ),
    )(cols, rws, vec)


def finish_kernel(cols, rws, g_qkv, g_in, g_out, g_back):
    g_back[...] = rws[0:256].astype(F32)
    g_out[...] = rws[256:320].astype(F32)

    def one(p, _):
        for h in (0, 1):
            r = pl.ds(32 * h, 32)
            a, b = cols[0, h, p].astype(F32), cols[1, h, p].astype(F32)
            g_in[r, pl.ds(pl.multiple_of(p * 512, 512), 256)] = a[:, 0:256]
            g_in[r, pl.ds(pl.multiple_of(p * 512 + 256, 256), 256)] = b[:, 0:256]
            for m in range(3):
                k = 256 + 64 * m
                both = jnp.concatenate([a[:, k : k + 64], b[:, k : k + 64]], axis=1)
                g_qkv[r, pl.ds(pl.multiple_of(m * WIDTH + p * 128, 128), 128)] = both
        return 0

    lax.fori_loop(0, 16, one, 0)


def finish(cols, rws):
    def arr(*shape):
        return jax.ShapeDtypeStruct(shape, F32)

    return pl.pallas_call(
        finish_kernel,
        out_shape=[arr(64, 6144), arr(64, 8192), arr(64, WIDTH), arr(256, WIDTH)],
        in_specs=[VM] * 2,
        out_specs=[VM] * 4,
        compiler_params=pltpu.CompilerParams(vmem_limit_bytes=60 * 2**20),
    )(cols, rws)


def layer_norm(tokens, gain, shift):
    mean = jnp.mean(tokens, axis=-1, keepdims=True)
    centred = tokens - mean
    var = jnp.mean(centred * centred, axis=-1, keepdims=True)
    return centred * lax.rsqrt(var + eps_norm) * gain + shift


def body(
    tokens,
    span_order,
    ln_gain,
    ln_bias,
    qkv_weight,
    qkv_bias,
    out_weight,
    out_bias,
    fc1_weight,
    fc1_bias,
    fc2_weight,
    fc2_bias,
    cotangent,
):
    x, y, zh, zl, c = place()
    me = (x * 4 + y) * 2 + c

    tok = tokens.reshape(128, WIDTH)
    g_own = cotangent.reshape(128, WIDTH)
    own = [ln_gain, ln_bias, out_bias, fc2_bias, qkv_bias, jnp.zeros((64,), BF), fc1_bias]
    own = [v.astype(F32) for v in own] + [span_order.reshape(32).astype(F32), jnp.zeros((224,), F32)]
    small = jnp.concatenate(own).reshape(8, 128)
    n_all, g_all, fields, active, d_hidden, cols_t, rows_w, small_all, small_other = front(
        tok, g_own, small, qkv_weight, fc1_weight, out_weight, fc2_weight
    )
    small_all = small_all.reshape(32, 8, 128)
    gain, shift = small_all[:, 0, :64].reshape(WIDTH), small_all[:, 0, 64:].reshape(WIDTH)
    b_sum = (small_all[:, 1, :64] + small_all[:, 1, 64:]).reshape(WIDTH)
    order = jnp.where(c == zh, span_order.reshape(32), small_other[6, :32].astype(jnp.int32))

    done = attend(order, fields.reshape(32, 128, 256)).reshape(16, 2, 128, 256)
    branch, d_normed, g_cols, g_rows, sums = back(done, active, d_hidden, rows_w, cols_t, n_all, g_all)
    flat = tok.astype(F32)
    block_out = (flat + branch + b_sum).astype(BF).reshape(1, 128, WIDTH)
    _, norm_pull = jax.vjp(layer_norm, flat, gain, shift)
    d_flat, d_gain, d_shift = norm_pull(d_normed)
    d_tokens = (g_own.astype(F32) + d_flat).astype(BF).reshape(1, 128, WIDTH)

    sums = sums[0]
    bq = jnp.zeros((3, HEADS, 64), F32)
    bq = lax.dynamic_update_slice_in_dim(bq, sums[256:].reshape(3, 1, 64), me, 1).reshape(32, 192)
    bi = jnp.zeros((HEADS, 256), F32)
    bi = lax.dynamic_update_slice_in_dim(bi, sums[None, :256], me, 0)
    bo = jnp.sum(g_own.astype(F32), axis=0)
    vec = [v.reshape(32, 64) for v in (d_gain, d_shift, bo)] + [bq, bi, jnp.zeros((32, 384), F32)]
    vec = jnp.concatenate(vec, axis=1).reshape(4, 4, 16, 128)
    cols, rws, vec = grads(g_cols.reshape(16, 4, 32, 448), g_rows, vec)
    g_qkv, g_in, g_out, g_back = finish(cols.reshape(2, 2, 16, 32, 448), rws)
    vec = lax.dynamic_index_in_dim(vec.reshape(2, 1024), zh, 0, keepdims=False)
    return (
        block_out,
        d_tokens,
        vec[:64],
        vec[64:128],
        g_qkv,
        vec[192:384],
        g_out,
        vec[128:192],
        g_in,
        vec[384:640],
        g_back,
        vec[128:192],
    )


def solution(mesh):
    act, rows, vec = P("rep", "shard", None), P("shard", None), P("shard")
    return jax.shard_map(
        body,
        mesh=mesh,
        in_specs=(act, P("rep", None), vec, vec, rows, vec, rows, vec, rows, vec, rows, vec, act),
        out_specs=(act, act, vec, vec, rows, vec, rows, vec, rows, vec, rows, vec),
        check_vma=False,
    )
```

```python
import jax
import jax.numpy as jnp
from jax import lax
from jax.experimental import pallas as pl
from jax.experimental.pallas import tpu as pltpu
from jax.sharding import PartitionSpec as P

F32 = jnp.float32
BF = jnp.bfloat16
MESH = pl.DeviceIdType.MESH
WIDTH = 2048
LENGTH = 4096
TILE = 512
STRIPS = LENGTH // TILE
eps_norm = 1e-05
rope_base = 10000.0
negative = -1e30
VM = pl.BlockSpec(memory_space=pltpu.VMEM)
SM = pl.BlockSpec(memory_space=pltpu.SMEM)
ANY = pl.BlockSpec(memory_space=pl.ANY)
DMA = pltpu.SemaphoreType.DMA


def vmem(*shape, t=BF):
    return pltpu.VMEM(shape, t)


def arr(*shape, t=BF):
    return jax.ShapeDtypeStruct(shape, t)


def dot(a, b):
    return jnp.dot(a, b, preferred_element_type=F32)


def wrap(v):
    return (v + 4) % 4


def place():
    rep = lax.axis_index("rep")
    sh = lax.axis_index("shard")
    return sh // 8, (sh // 2) % 4, sh % 2, rep // 2, rep % 2


class Here:
    def __init__(self, send, recv):
        self.x, self.y, self.zh, self.zl, self.c = place()
        self.z = self.zh * 2 + self.zl
        self.send, self.recv = send, recv
        self.count = 0
        self.started = []
        self.other = self.spot(self.x, self.y, self.z, 1 - self.c)
        self.beyond = self.at_z(2)
        self.twin = self.spot(self.x, self.y, self.zh * 2 + 1 - self.zl, self.c)

    def spot(self, x, y, z, c):
        return ((z % 2) * 2 + c, (x * 4 + y) * 2 + z // 2)

    def at(self, dx, dy):
        return self.spot(wrap(self.x + dx), wrap(self.y + dy), self.z, self.c)

    def at_z(self, dz):
        return self.spot(self.x, self.y, wrap(self.z + dz), self.c)

    def pair(self, dx, dy):
        return wrap(self.x + dx) * 4 + wrap(self.y + dy)

    def greet(self, far_xy=False, z=False, beyond=False):
        peers = [self.at(1, 0), self.at(-1, 0), self.at(0, 1), self.at(0, -1), self.other]
        if far_xy:
            peers += [self.at(2, 0), self.at(0, 2)]
        if z:
            peers += [self.at_z(1), self.at_z(-1)]
        if beyond:
            peers += [self.beyond]
        barrier = pltpu.get_barrier_semaphore()
        for d in peers:
            pl.semaphore_signal(barrier, inc=1, device_id=d, device_id_type=MESH)
        pl.semaphore_wait(barrier, len(peers))

    def new(self, n=1):
        self.count += n
        return self.count - n

    def copy(self, src, dst, i, to):
        return pltpu.make_async_remote_copy(
            src_ref=src, dst_ref=dst, send_sem=self.send.at[i], recv_sem=self.recv.at[i],
            device_id=to, device_id_type=MESH,
        )

    def go(self, src, dst, i, to):
        cp = self.copy(src, dst, i, to)
        cp.start()
        self.started.append(cp)
        return cp

    def came(self, ref, i):
        self.copy(ref, ref, i, self.other).wait_recv()

    def push(self, src, dst, to, land):
        i = self.new()
        self.go(src, dst, i, to)
        return lambda: self.came(land, i)

    def finish(self):
        for cp in self.started:
            cp.wait_send()


OFFS = [(p, q) for p in (0, -1, 1, 2) for q in (0, -1, 1, 2)]
GROUP = {0: 0, -1: 1, 1: 2, 2: 3}
def rows_of(half, part):
    return pl.ds(half * 64 + (32 if part == 2 else 0), 64 if part == 0 else 32)


class Gather:
    def __init__(self, me, own, out, loc):
        self.me, self.own, self.out, self.loc = me, own, out, loc
        self.link = me.new(40)
        self.core = me.new(32)

    def dev(self, h, da, db):
        return self.me.at(da, db) if h == 0 else self.me.at(db, da)

    def ref(self, h, off, part, core):
        dx, dy = off if h == 0 else (off[1], off[0])
        return self.out.at[self.me.pair(dx, dy) * 2 + core, rows_of(h, part)]

    def pass_on(self, h, role, off, part, to, own=False):
        dst = self.ref(h, off, part, self.me.c)
        src = self.own.at[rows_of(h, part)] if own else dst
        self.me.go(src, dst, self.link + 20 * h + role, self.dev(h, *to))

    def arrived(self, h, role, off, part):
        self.me.came(self.ref(h, off, part, self.me.c), self.link + 20 * h + role)

    def share(self, h, off, own=False):
        dst = self.ref(h, off, 0, self.me.c)
        src = self.own.at[rows_of(h, 0)] if own else dst
        self.me.go(src, dst, self.core + 16 * h + OFFS.index(off), self.me.other)

    def shared(self, off):
        for h in (0, 1):
            o = off if h == 0 else (off[1], off[0])
            self.me.came(self.ref(h, o, 0, 1 - self.me.c), self.core + 16 * h + OFFS.index(o))

    def second(self, h, ao, own=False):
        k = GROUP[ao]
        self.pass_on(h, 4 + 2 * k, (ao, 0), 0, (0, 1), own)
        self.pass_on(h, 5 + 2 * k, (ao, 0), 0, (0, -1), own)

    def near(self, h, ao):
        k = GROUP[ao]
        self.arrived(h, 4 + 2 * k, (ao, -1), 0)
        self.pass_on(h, 12 + 2 * k, (ao, -1), 1, (0, 1))
        self.share(h, (ao, -1))
        self.arrived(h, 5 + 2 * k, (ao, 1), 0)
        self.pass_on(h, 13 + 2 * k, (ao, 1), 2, (0, -1))
        self.share(h, (ao, 1))

    def far(self, h, ao):
        k = GROUP[ao]
        self.arrived(h, 12 + 2 * k, (ao, 2), 1)
        self.arrived(h, 13 + 2 * k, (ao, 2), 2)
        self.share(h, (ao, 2))

    def begin(self):
        p = self.me.pair(0, 0)
        self.local = pltpu.make_async_copy(self.own, self.out.at[p * 2 + self.me.c], self.loc)
        self.local.start()
        for h in (0, 1):
            self.pass_on(h, 0, (0, 0), 0, (1, 0), True)
            self.pass_on(h, 1, (0, 0), 0, (-1, 0), True)
        for h in (0, 1):
            self.second(h, 0, True)
            self.share(h, (0, 0), True)

    def first(self, h):
        self.arrived(h, 0, (-1, 0), 0)
        self.pass_on(h, 2, (-1, 0), 1, (1, 0))
        self.second(h, -1)
        self.share(h, (-1, 0))
        self.arrived(h, 1, (1, 0), 0)
        self.pass_on(h, 3, (1, 0), 2, (-1, 0))
        self.second(h, 1)
        self.share(h, (1, 0))

    def middle(self, h):
        self.arrived(h, 2, (2, 0), 1)
        self.arrived(h, 3, (2, 0), 2)
        self.second(h, 2)
        self.share(h, (2, 0))

    def events(self, start=0.0):
        todo = []
        for h in (0, 1):
            steps = [(6.5, lambda h=h: self.first(h)), (15.5, lambda h=h: self.middle(h))]
            steps += [(t, lambda h=h, o=o: self.near(h, o)) for t, o in ((12.5, 0), (21, -1), (27, 1), (36, 2))]
            steps += [(t, lambda h=h, o=o: self.far(h, o)) for t, o in ((30, 0), (39, -1), (42, 1), (45, 2))]
            todo += [(start + t, f) for t, f in steps]
        return todo


ARRIVALS = (
    (5, (0, 0)), (14, (-1, 0)), (14, (1, 0)), (14, (0, -1)), (14, (0, 1)), (22.5, (-1, -1)), (28.5, (-1, 1)),
    (28.5, (1, -1)), (28.5, (1, 1)), (32, (2, 0)), (32, (0, 2)), (40.5, (-1, 2)), (40.5, (2, -1)),
    (43.5, (1, 2)), (43.5, (2, 1)), (46.5, (2, 2)),
)


class Pairs:
    def __init__(self, gather, buf, loc, work):
        self.gather, self.buf, self.loc, self.work = gather, buf, loc, work
        self.queue, self.step = [], 0

    def take(self, off):
        self.gather.shared(off)
        if off == (0, 0):
            self.gather.local.wait()
        p, k = self.gather.me.pair(*off), self.step % 4
        self.step += 1
        cp = pltpu.make_async_copy(self.gather.out.at[pl.ds(p * 2, 2)], self.buf.at[k], self.loc.at[k])
        cp.start()
        self.queue.append((p, k, cp))
        if len(self.queue) > 3:
            self.run()

    def run(self):
        p, k, cp = self.queue.pop(0)
        cp.wait()
        self.work(p, k)

    def rest(self):
        while self.queue:
            self.run()

    def over(self, k, wa, wb):
        def inner(i, carry):
            va, vb = carry
            cs = pl.ds(pl.multiple_of(i * 512, 512), 512)
            v = self.buf[k, :, :, cs].reshape(256, 512)
            return va + dot(v, wa[cs, :]), vb + dot(v, wb[cs, :])

        start = jnp.zeros((256, wa.shape[1]), F32), jnp.zeros((256, wb.shape[1]), F32)
        return lax.fori_loop(0, 4, inner, start)

    def events(self, start=0.0, least=0.0):
        return [(max(start + t, least) + 1e-3 * i, lambda o=o: self.take(o)) for i, (t, o) in enumerate(ARRIVALS)]


TURN = [(2, 2), (1, 2), (3, 2), (0, 2), (2, 1), (2, 3), (2, 0), (1, 1)]
TURN += [(1, 3), (3, 1), (3, 3), (0, 1), (0, 3), (1, 0), (3, 0), (0, 0)]


class Total:
    def __init__(self, me, operands, w, out, lhs, psend, acc, far, near):
        self.me, self.operands, self.w, self.out, self.lhs = me, operands, w, out, lhs
        self.psend, self.acc, self.far, self.near = psend, acc, far, near
        self.link, self.core = me.new(40), me.new(16)
        self.sent = []

    def dev(self, h, da, db):
        return self.me.at(da, db) if h == 0 else self.me.at(db, da)

    def step_to(self, h, g, s):
        return self.dev(h, 0, s) if g < 4 else self.dev(h, s, 0)

    def sem(self, h, g, role):
        return self.link + 20 * h + 4 * g + role

    def block(self, h, g, o):
        da, db = (g, o) if g < 4 else (o, 0)
        dx, dy = (da, db) if h == 0 else (db, da)
        return (dx % 4) * 4 + dy % 4

    def send_far(self, h, g):
        k = self.block(h, g, 2)
        for role, s in ((0, 1), (1, -1)):
            src, dst = self.acc.at[k, rows_of(h, role + 1)], self.far.at[h, g, role]
            self.me.go(src, dst, self.sem(h, g, role), self.step_to(h, g, s))

    def relay(self, h, g):
        acc = self.acc
        for role, s in ((0, 1), (1, -1)):
            ref = self.far.at[h, g, role]
            self.me.came(ref, self.sem(h, g, role))
            k, r = self.block(h, g, s), rows_of(h, role + 1)
            acc[k, r] = (acc[k, r].astype(F32) + ref[...].astype(F32)).astype(BF)
            src, dst = acc.at[k, rows_of(h, 0)], self.near.at[h, g, role]
            self.me.go(src, dst, self.sem(h, g, 2 + role), self.step_to(h, g, s))

    def land(self, h, g):
        k, r = self.block(h, g, 0), rows_of(h, 0)
        for role in (0, 1):
            self.me.came(self.near.at[h, g, role], self.sem(h, g, 2 + role))
        tot = self.acc[k, r].astype(F32)
        tot = tot + self.near[h, g, 0].astype(F32) + self.near[h, g, 1].astype(F32)
        if g < 4:
            self.acc[k, r] = tot.astype(BF)
        else:
            self.out[r] = tot
        if g == 2:
            self.send_far(h, 4)

    def fill(self, i, core):
        for q in range(4):
            p = self.me.pair(*TURN[4 * i + q])
            a, b = self.operands(p, core)
            r = pl.ds(128 * q, 128)
            self.lhs[r, 0:256] = a
            self.lhs[r, 256 : 256 + b.shape[-1]] = b

    def for_partner(self, i):
        if i >= 2:
            for cp in self.sent[4 * i - 8 : 4 * i - 4]:
                cp.wait_send()
        self.fill(i, 1 - self.me.c)
        s = 4 * (i % 2)

        def tile(t, _):
            cs = pl.ds(pl.multiple_of(t * TILE, TILE), TILE)
            v = dot(self.lhs[...], self.w[:, cs]).astype(BF)
            self.psend[s : s + 4, :, cs] = v.reshape(4, 128, TILE)
            return 0

        lax.fori_loop(0, WIDTH // TILE, tile, 0)
        for q in range(4):
            dx, dy = TURN[4 * i + q]
            k = dx * 4 + dy
            cp = self.me.copy(self.psend.at[s + q], self.acc.at[k], self.core + k, self.me.other)
            cp.start()
            self.sent.append(cp)

    def for_own(self, i):
        turns = TURN[4 * i : 4 * i + 4]
        self.fill(i, self.me.c)
        for dx, dy in turns:
            k = dx * 4 + dy
            self.me.came(self.acc.at[k], self.core + k)

        def tile(t, _):
            cs = pl.ds(pl.multiple_of(t * TILE, TILE), TILE)
            v = dot(self.lhs[...], self.w[:, cs])
            for q, (dx, dy) in enumerate(turns):
                k = dx * 4 + dy
                self.acc[k, :, cs] = (v[128 * q : 128 * q + 128] + self.acc[k, :, cs].astype(F32)).astype(BF)
            return 0

        lax.fori_loop(0, WIDTH // TILE, tile, 0)
        for dx, dy in turns:
            if dy == 2:
                self.send_far(0, dx)
            if dx == 2:
                self.send_far(1, dy)

    def products(self):
        todo = [lambda: self.for_partner(0)]
        for i in range(1, 4):
            todo += [lambda i=i: self.for_partner(i), lambda i=i: self.for_own(i - 1)]
        return todo + [lambda: self.for_own(3)]

    def events(self, start=0.0):
        todo = []
        for h in (0, 1):
            steps = [(t, lambda h=h, g=g: self.relay(h, g)) for t, g in ((9, 2), (13, 1), (16, 3), (19, 0), (45, 4))]
            steps += [(t, lambda h=h, g=g: self.land(h, g)) for t, g in ((25, 2), (31, 1), (37, 3), (43, 0), (52, 4))]
            todo += [(start + t + 0.01 * h, f) for t, f in steps]
        return todo

    def finish(self):
        for cp in self.sent[-8:]:
            cp.wait_send()


SUM_SCRATCH = [
    vmem(8, 128, WIDTH), vmem(16, 128, WIDTH), vmem(2, 5, 2, 32, WIDTH), vmem(2, 5, 2, 64, WIDTH),
]


def weave(events, units, now=0.0):
    events, units = sorted(events, key=lambda e: e[0]), list(units)
    while events or units:
        if events and (not units or events[0][0] <= now):
            due, f = events.pop(0)
            now = max(now, due) + 0.2
        else:
            cost, f = units.pop(0)
            now += cost
        f()


def pick(read, which):
    v = read(0)
    for p in range(1, 32):
        v = jnp.where(which == p, read(p), v)
    return v


def spin(v, cos, sin):
    a, b = v[0:16], v[16:32]
    return jnp.concatenate([a * cos - b * sin, b * cos + a * sin, v[32:]], axis=0)


def gelu_both(u):
    k0, k1 = 0.7978845608028654, 0.044715
    sq = u * u
    t = jnp.tanh(k0 * u * (1.0 + k1 * sq))
    half = 0.5 * (1.0 + t)
    return u * half, half + 0.5 * u * (1.0 - t * t) * k0 * (1.0 + 3.0 * k1 * sq)


def front_kernel(
    tok, small, w_qkv, w_in, w_out, w_back,
    n_all, fields, active, slope, cols_t, rows_w, small_all, small_other,
    n_own, buf, f_send, w_f, w_m, wf1, wq1, wf2, wq2, table, bq, send, recv, loc, lsem,
):
    me = Here(send, recv)
    x, y, z, zh, zl, c = me.x, me.y, me.z, me.zh, me.zl, me.c
    me.greet(True, True, True)

    small_all[x, y, zh] = small[...]
    got_small = me.push(small, small_other, me.other, small_other)
    first = [
        me.push(small, small_all.at[x, y, zh], me.at(d, 0), small_all.at[wrap(x - d), y, zh])
        for d in (1, -1, 2)
    ]

    mine = pl.ds(pl.multiple_of(zl * 32, 32), 32)

    def col_copies(dx):
        xx = wrap(x + dx)
        for yy in range(4):
            q = xx * 4 + yy
            lanes = pl.ds(pl.multiple_of((q * 2 + c) * 256, 256), 256)
            yield w_in.at[mine, lanes], wf1.at[yy, x], wf1.at[yy, wrap(x - dx)]
            for m in range(3):
                lanes = pl.ds(pl.multiple_of(m * WIDTH + q * 128, 128), 128)
                yield w_qkv.at[mine, lanes], wq1.at[yy, x, m], wq1.at[yy, wrap(x - dx), m]

    mates = []
    for i, (src, dst, _) in enumerate(col_copies(0)):
        cp = pltpu.make_async_copy(src, dst, lsem.at[i])
        cp.start()
        mates.append(cp)
    waits = [me.push(s, t, me.at(d, 0), land) for d in (1, -1, 2) for s, t, land in col_copies(d)]

    ri = me.new(2)
    to_row = me.spot(x, y, 3 - z, c)

    def far_rows():
        for i, src, part in ((0, w_back, pl.ds(0, 256)), (1, w_out, pl.ds(256, 64))):
            yield me.copy(src, rows_w.at[part], ri + i, to_row)

    def near_rows():
        for i, src, part in ((0, w_back, pl.ds(0, 256)), (1, w_out, pl.ds(256, 64))):
            yield pltpu.make_async_copy(src, rows_w.at[part], lsem.at[16 + i])

    @pl.when(c == zh)
    def _():
        for cp in [*far_rows(), *near_rows()]:
            cp.start()

    for w in first:
        w()
    line = small_all.at[:, y, zh]
    second = [me.push(line, line, me.at(0, d), small_all.at[:, wrap(y - d), zh]) for d in (1, -1, 2)]
    for w in waits:
        w()
    for cp in mates:
        cp.wait()
    waits = []
    for d in (1, -1, 2):
        yy, land = wrap(y + d), wrap(y - d)
        waits.append(me.push(wf1.at[yy], wf2.at[:, y, z], me.at(0, d), wf2.at[:, land, z]))
        waits.append(me.push(wq1.at[yy], wq2.at[:, :, y, z], me.at(0, d), wq2.at[:, :, land, z]))
    wf2[:, y, z] = wf1[y]
    wq2[:, :, y, z] = wq1[y]
    for w in second:
        w()
    sheet = small_all.at[:, :, zh]
    me.push(sheet, sheet, me.beyond, small_all.at[:, :, 1 - zh])()
    got_small()
    for j in range(32):
        piece = small_all[j // 8, (j // 2) % 4, j % 2]
        for i in (0, 1):
            table[pl.ds(i, 1), pl.ds(64 * j, 64)] = piece[0:1, 64 * i : 64 * i + 64]

    def norm(i, _):
        r = pl.ds(pl.multiple_of(i * 32, 32), 32)
        v = tok[r, :].astype(F32)
        v = v - jnp.mean(v, axis=-1, keepdims=True)
        v = v * lax.rsqrt(jnp.mean(v * v, axis=-1, keepdims=True) + eps_norm)
        n_own[r, :] = (v * table[0:1, :] + table[1:2, :]).astype(BF)
        return 0

    lax.fori_loop(0, 4, norm, 0)
    gather = Gather(me, n_own, n_all, loc.at[4])
    gather.begin()
    for j in range(32):
        piece = small_all[j // 8, (j // 2) % 4, j % 2]
        for i in range(3):
            bq[pl.ds(3 * j + i, 1), 0:64] = piece[2 + i // 2 : 3 + i // 2, 64 * (i % 2) : 64 * (i % 2) + 64]
    quarter = []

    def round_z():
        for w in waits:
            w()
        for s in (1, -1):
            land = wrap(z - s)
            quarter.append(me.push(wf2.at[:, :, z], wf2.at[:, :, z], me.at_z(s), wf2.at[:, :, land]))
            quarter.append(me.push(wq2.at[:, :, :, z], wq2.at[:, :, :, z], me.at_z(s), wq2.at[:, :, :, land]))

    last = []

    def round_z_again():
        for w in quarter:
            w()
        for s, k in ((1, 0), (-1, 2)):
            zz, part, far_z = wrap(z - s), pl.ds(k, 2), wrap(z + 2)
            ref, land = wf2.at[part, :, zz], wf2.at[part, :, far_z]
            last.append(me.push(ref, ref, me.at_z(s), land))
            ref, land = wq2.at[part, :, :, zz], wq2.at[part, :, :, far_z]
            last.append(me.push(ref, ref, me.at_z(s), land))

    def take_columns():
        for w in last:
            w()
        for xx in range(4):
            r = pl.ds(xx * 512, 512)
            w_f[r, :] = wf2[xx].reshape(512, 256)
            for m in range(3):
                v = wq2[xx, m].reshape(512, 128)
                w_m[r, 64 * m : 64 * m + 64] = jnp.where(c == 0, v[:, 0:64], v[:, 64:128])

    here = small_all[x, y, c]
    b_in = jnp.concatenate([here[4:5, :], here[5:6, :]], axis=1)
    t = (x * 4 + y) * 2 + c
    b_m = jnp.concatenate([bq[pl.ds(t + 32 * m, 1), 0:64] for m in range(3)], axis=1)
    fi = me.new(16)

    def work(p, k):
        two = pl.ds(p * 2, 2)
        hidden, mixed = pairs.over(k, w_f, w_m)
        f_send[p, :, :, 0:192] = (mixed + b_m).astype(BF).reshape(2, 128, 192)
        f_send[p, :, :, 192:256] = jnp.zeros((2, 128, 64), BF)
        fields[p, zh] = f_send[p, zh]
        me.go(f_send.at[p, 1 - zh], fields.at[p, zh], fi + p, me.beyond)
        act, grad = gelu_both(hidden + b_in)
        active[two] = act.astype(BF).reshape(2, 128, 256)
        slope[two] = grad.astype(BF).reshape(2, 128, 256)

    pairs = Pairs(gather, buf, loc, work)

    def turn_cols():
        def one(i, _):
            r = pl.ds(pl.multiple_of(i * 256, 256), 256)
            cols_t[0:256, r] = w_f[r, :].astype(F32).T.astype(BF)
            cols_t[256:448, r] = w_m[r, :].astype(F32).T.astype(BF)
            return 0

        lax.fori_loop(0, 8, one, 0)

    events = gather.events() + [(4, round_z), (12.6, round_z_again), (21.1, take_columns), (30.1, turn_cols)]
    weave(events + pairs.events(0, 27.1), [])
    pairs.rest()
    for cp in near_rows():
        @pl.when(c == zh)
        def _():
            cp.wait()

    for cp in far_rows():
        @pl.when(c != zh)
        def _():
            cp.wait_recv()

    def came(p, _):
        me.came(fields.at[p, 1 - zh], fi + p)
        return 0

    lax.fori_loop(0, 16, came, 0)
    me.finish()
    for cp in far_rows():
        @pl.when(c == zh)
        def _():
            cp.wait_send()


def front(tok, small, w_qkv, w_in, w_out, w_back):
    return pl.pallas_call(
        front_kernel,
        out_shape=[
            arr(32, 128, WIDTH), arr(16, 2, 128, 256), arr(32, 128, 256), arr(32, 128, 256),
            arr(448, WIDTH), arr(320, WIDTH), arr(4, 4, 2, 8, 128, t=F32), arr(8, 128, t=F32),
        ],
        in_specs=[VM, VM, ANY, ANY, ANY, ANY],
        out_specs=[ANY] + [VM] * 7,
        scratch_shapes=[
            vmem(128, WIDTH), vmem(4, 2, 128, WIDTH), vmem(16, 2, 128, 256), vmem(WIDTH, 256), vmem(WIDTH, 192),
            vmem(4, 4, 32, 256), vmem(4, 4, 3, 32, 128), vmem(4, 4, 4, 32, 256), vmem(4, 3, 4, 4, 32, 128),
            vmem(8, WIDTH, t=F32), vmem(96, 128, t=F32), DMA((180,)), DMA((180,)), DMA((5,)), DMA((18,)),
        ],
        compiler_params=pltpu.CompilerParams(
            collective_id=1, has_side_effects=True, vmem_limit_bytes=60 * 2**20
        ),
    )(tok, small, w_qkv, w_in, w_out, w_back)


def tile_at(i, j):
    return i * (i + 1) // 2 + j


def attend_kernel(
    order, inverse, fields, cos_ref, sin_ref, g_own, rows_w, slope,
    g_all, d_hidden, d_att, att, probs, q_n, v_n, k_t, o_t, scale,
    buf, d_send, a_send, w_ot, w_bt, k_n, q_t, v_t, s_buf, p_buf, send, recv, loc, psem,
):
    me = Here(send, recv)
    zh = me.zh
    me.greet(beyond=True)
    gather = Gather(me, g_own, g_all, loc.at[4])
    gather.begin()
    for ref in (d_send, a_send):
        ref[:, :, :, 64:128] = jnp.zeros((16, 2, 128, 64), BF)
    for ref in (q_n, v_n):
        ref[:, 64:128] = jnp.zeros((LENGTH, 64), BF)

    def turn_rows():
        def one(i, _):
            r = pl.ds(pl.multiple_of(i * 256, 256), 256)
            w_bt[r, :] = rows_w[0:256, r].astype(F32).T.astype(BF)
            w_ot[r, :] = rows_w[256:320, r].astype(F32).T.astype(BF)
            return 0

        lax.fori_loop(0, 8, one, 0)

    def load(begin):
        def one(i, _):
            here = pl.ds(pl.multiple_of(i * 128, 128), 128)
            t = pick(lambda p: fields[p], inverse[i]).astype(F32).T
            cos, sin = cos_ref[:, here], sin_ref[:, here]
            q = spin(t[0:64], cos, sin) * 0.125
            k = spin(t[64:128], cos, sin)
            v = t[128:192]
            q_t[:, here] = q.astype(BF)
            k_t[:, here] = k.astype(BF)
            v_t[:, here] = v.astype(BF)
            q_n[here, 0:64] = q.T.astype(BF)
            k_n[here, :] = k.T.astype(BF)
            v_n[here, 0:64] = v.T.astype(BF)
            return 0

        return lambda: lax.fori_loop(begin, begin + 8, one, 0)

    square = (TILE, TILE)
    allowed = lax.broadcasted_iota(jnp.int32, square, 0) <= lax.broadcasted_iota(jnp.int32, square, 1)
    tops = {}

    def scores(i):
        qs = pl.ds(i * TILE, TILE)
        qt = q_t[:, qs]

        def one(j, top):
            ks = pl.ds(pl.multiple_of(j * TILE, TILE), TILE)
            s = dot(k_n[ks, :], qt)
            s_buf[ks, :] = s
            return jnp.maximum(top, jnp.max(s, axis=0, keepdims=True))

        top = jnp.full((1, TILE), negative, F32)
        if i:
            top = lax.fori_loop(0, i, one, top)
        s = jnp.where(allowed, dot(k_n[qs, :], qt), negative)
        s_buf[qs, :] = s
        tops[i] = jnp.maximum(top, jnp.max(s, axis=0, keepdims=True))

    def out_copy(i, j):
        return pltpu.make_async_copy(p_buf.at[i % 2, j], probs.at[tile_at(i, j)], psem.at[i % 2, j])

    def values(i):
        qs = pl.ds(i * TILE, TILE)
        top = tops[i]
        if i >= 2:
            for j in range(i - 1):
                out_copy(i - 2, j).wait()

        def one(j, carry):
            total, o = carry
            ks = pl.ds(pl.multiple_of(j * TILE, TILE), TILE)
            p = jnp.exp(s_buf[ks, :] - top)
            pb = p.astype(BF)
            p_buf[i % 2, j] = pb
            return total + jnp.sum(p, axis=0, keepdims=True), o + dot(v_t[:, ks], pb)

        start = jnp.zeros((1, TILE), F32), jnp.zeros((64, TILE), F32)
        total, o = lax.fori_loop(0, i + 1, one, start)
        for j in range(i + 1):
            out_copy(i, j).start()
        inv = 1.0 / total
        o_t[:, qs] = o * inv
        scale[0:1, qs] = inv

    ai = me.new()

    def give():
        def one(b, _):
            o = pick(lambda p: o_t[:, 128 * p : 128 * p + 128], order[b])
            a_send[b // 2, lax.rem(b, 2), :, 0:64] = o.T.astype(BF)
            return 0

        lax.fori_loop(0, 32, one, 0)
        att[:, zh] = a_send[:, zh]
        me.go(a_send.at[:, 1 - zh], att.at[:, zh], ai, me.beyond)

    di = me.new(16)

    def work(p, k):
        two = pl.ds(p * 2, 2)
        da, do = pairs.over(k, w_bt, w_ot)
        d_send[p, :, :, 0:64] = do.astype(BF).reshape(2, 128, 64)
        d_att[p, zh] = d_send[p, zh]
        me.go(d_send.at[p, 1 - zh], d_att.at[p, zh], di + p, me.beyond)
        d_hidden[two] = (da * slope[two].reshape(256, 256).astype(F32)).astype(BF).reshape(2, 128, 256)

    pairs = Pairs(gather, buf, loc, work)

    side = [(1.5, turn_rows)] + [(0.8, load(8 * k)) for k in range(4)]
    for i in range(STRIPS):
        side += [(0.25 * (i + 1), lambda i=i: scores(i)), (0.3 * (i + 1), lambda i=i: values(i))]
    side.append((2.0, give))
    weave(gather.events() + pairs.events(0, 5.0), side)
    pairs.rest()
    for i in (STRIPS - 2, STRIPS - 1):
        for j in range(i + 1):
            out_copy(i, j).wait()
    me.came(att.at[:, 1 - zh], ai)

    def came(p, _):
        me.came(d_att.at[p, 1 - zh], di + p)
        return 0

    lax.fori_loop(0, 16, came, 0)
    me.finish()


def attend(order, inverse, fields, cos, sin, g_own, rows_w, slope):
    return pl.pallas_call(
        attend_kernel,
        out_shape=[
            arr(32, 128, WIDTH), arr(32, 128, 256), arr(16, 2, 128, 128), arr(16, 2, 128, 128),
            arr(tile_at(STRIPS, 0), TILE, TILE), arr(LENGTH, 128), arr(LENGTH, 128), arr(64, LENGTH),
            arr(64, LENGTH, t=F32), arr(8, LENGTH, t=F32),
        ],
        in_specs=[SM, SM, VM, VM, VM, VM, VM, VM],
        out_specs=[ANY, VM, VM, VM, ANY] + [VM] * 5,
        scratch_shapes=[
            vmem(4, 2, 128, WIDTH), vmem(16, 2, 128, 128), vmem(16, 2, 128, 128), vmem(WIDTH, 64), vmem(WIDTH, 256),
            vmem(LENGTH, 64), vmem(64, LENGTH), vmem(64, LENGTH), vmem(LENGTH, TILE, t=F32),
            vmem(2, STRIPS, TILE, TILE), DMA((100,)), DMA((100,)), DMA((5,)), DMA((2, STRIPS)),
        ],
        compiler_params=pltpu.CompilerParams(
            collective_id=2, has_side_effects=True, vmem_limit_bytes=60 * 2**20
        ),
    )(order, inverse, fields, cos, sin, g_own, rows_w, slope)


class Outer:
    def __init__(self, src, lhs, height, put, turned, buf, loc, sums=None):
        self.src, self.lhs, self.height, self.put = src, lhs, height, put
        self.turned, self.buf, self.loc, self.sums = turned, buf, loc, sums

    def load(self, t, k):
        cs = pl.ds(pl.multiple_of(t * 256, 256), 256)
        return pltpu.make_async_copy(self.src.at[:, :, cs], self.buf.at[k], self.loc.at[k])

    def prepare(self):
        self.load(0, 0).start()

        def one(p, _):
            v = self.lhs(p).astype(F32)
            if self.sums is not None:
                self.sums[0:1, 0 : self.height] += jnp.sum(v, axis=0, keepdims=True)
            self.turned[0 : self.height, pl.ds(pl.multiple_of(p * 256, 256), 256)] = v.T.astype(BF)
            return 0

        lax.fori_loop(0, 16, one, 0)

    def part(self, begin, end):
        def one(t, _):
            k = lax.rem(t, 2)

            @pl.when(t + 1 < 8)
            def _():
                self.load(t + 1, 1 - k).start()

            self.load(t, k).wait()
            v = dot(self.turned[0 : self.height, :], self.buf[k].reshape(LENGTH, 256))
            self.put(pl.ds(pl.multiple_of(t * 256, 256), 256), v)
            return 0

        lax.fori_loop(begin, end, one, 0)

    def parts(self, n):
        todo = [self.prepare]
        return todo + [lambda i=i: self.part(8 * i // n, 8 * (i + 1) // n) for i in range(n)]


def two_blocks(ref):
    return lambda p: ref[pl.ds(2 * p, 2)].reshape(256, ref.shape[-1])


def turn_kernel(
    order, inverse, d_att, att, active, rows_w, o_t, scale, q_n, v_n, k_t, cos_ref, sin_ref, d_hidden,
    probs, n_all,
    branch, dm, g_cols, sums,
    do_t, p_buf, dk, dv, dq, d_pos, m_send, turned, buf, lhs, psend, acc, far, near, send, recv, loc, psem,
):
    me = Here(send, recv)
    zh = me.zh
    me.greet(beyond=True)

    def operands(p, core):
        return active[2 * p + core], att[p, core][:, 0:64]

    total = Total(me, operands, rows_w, branch, lhs, psend, acc, far, near)
    d_pos[:, :, 192:256] = jnp.zeros((32, 128, 64), BF)
    dk[...] = jnp.zeros_like(dk)
    dv[...] = jnp.zeros_like(dv)
    sums[...] = jnp.zeros_like(sums)

    def load():
        def one(i, _):
            here = pl.ds(pl.multiple_of(i * 128, 128), 128)
            do_t[:, here] = pick(lambda p: d_att[p], inverse[i]).astype(F32).T[0:64]
            return 0

        lax.fori_loop(0, 32, one, 0)

    order_of = [(i, j) for i in range(STRIPS) for j in range(i + 1)]

    def in_copy(n):
        return pltpu.make_async_copy(probs.at[n], p_buf.at[lax.rem(n, 4)], psem.at[lax.rem(n, 4)])

    state = {}

    def strip(i):
        qs = pl.ds(i * TILE, TILE)
        inv = scale[0:1, qs]
        do = do_t[:, qs] * inv
        delta = jnp.sum(do * o_t[:, qs], axis=0, keepdims=True)
        dt = do.astype(BF)
        dn = do.T.astype(BF)
        qn = q_n[qs, 0:64]
        base = tile_at(i, 0)

        def one(j, dq_t):
            n = base + j

            @pl.when(n + 3 < len(order_of))
            def _():
                in_copy(n + 3).start()

            in_copy(n).wait()
            ks = pl.ds(pl.multiple_of(j * TILE, TILE), TILE)
            dp = dot(v_n[ks, 0:64], dt)
            pb = p_buf[lax.rem(n, 4)]
            ds = (pb.astype(F32) * (dp - delta)).astype(BF)
            dk[ks, :] += dot(ds, qn)
            dv[ks, :] += dot(pb, dn)
            return dq_t + dot(k_t[:, ks], ds)

        def piece(begin, end):
            def run():
                start = state.get(i, jnp.zeros((64, TILE), F32))
                state[i] = lax.fori_loop(begin, end, one, start)

            return run

        def last():
            dq[:, qs] = spin(state[i], cos_ref[:, qs], -sin_ref[:, qs]) * 0.125

        return piece, last

    mi = me.new()

    def give():
        def one(i, _):
            here = pl.ds(pl.multiple_of(i * 128, 128), 128)
            k = spin(dk[here, :].T, cos_ref[:, here], -sin_ref[:, here])
            t = jnp.concatenate([dq[:, here], k, dv[here, :].T], axis=0)
            d_pos[i, :, 0:192] = t.T.astype(BF)
            return 0

        lax.fori_loop(0, 32, one, 0)

        def two(b, _):
            m_send[b // 2, lax.rem(b, 2)] = pick(lambda p: d_pos[p], order[b])
            return 0

        lax.fori_loop(0, 32, two, 0)
        dm[:, zh] = m_send[:, zh]
        me.go(m_send.at[:, 1 - zh], dm.at[:, zh], mi, me.beyond)

    side = [(2.0, load)]
    for i in range(STRIPS):

        def make(i=i):
            piece, last = strip(i)
            cuts = [0, i + 1] if i < 4 else [0, (i + 1) // 2, i + 1]
            for a, b in zip(cuts, cuts[1:]):
                yield piece(a, b)
            yield last

        holder = {}

        def begin(i=i, holder=holder, make=make):
            holder["todo"] = list(make())
            holder["todo"].pop(0)()

        def again(holder=holder):
            holder["todo"].pop(0)()

        more = 1 if i < 4 else 2
        side += [(0.8 * (i + 1) / more, begin)] + [(0.8 * (i + 1) / more, again)] * (more - 1) + [(0.2, again)]
    side.append((2.5, give))

    for n in range(3):
        in_copy(n).start()

    def put(r, v):
        g_cols[r, :] = v.T.astype(BF)

    outer = Outer(n_all, two_blocks(d_hidden), 256, put, turned, buf, loc, sums).parts(4)
    side += [(2.0, f) for f in outer]
    for f in total.products():
        f()
    weave(total.events(), side, 14.0)
    me.came(dm.at[:, 1 - zh], mi)
    total.finish()
    me.finish()


def turn(order, inverse, d_att, att, active, rows_w, o_t, scale, q_n, v_n, k_t, cos, sin, d_hidden, probs, n_all):
    return pl.pallas_call(
        turn_kernel,
        out_shape=[
            arr(128, WIDTH, t=F32), arr(16, 2, 128, 256), arr(WIDTH, 256), arr(8, 256, t=F32),
        ],
        in_specs=[SM, SM] + [VM] * 12 + [ANY] * 2,
        out_specs=[VM] * 4,
        scratch_shapes=[
            vmem(64, LENGTH, t=F32), vmem(4, TILE, TILE), vmem(LENGTH, 64, t=F32), vmem(LENGTH, 64, t=F32),
            vmem(64, LENGTH, t=F32), vmem(32, 128, 256), vmem(16, 2, 128, 256), vmem(256, LENGTH), vmem(2, 32, 128, 256), vmem(512, 320),
            *SUM_SCRATCH, DMA((60,)), DMA((60,)), DMA((2,)), DMA((4,)),
        ],
        compiler_params=pltpu.CompilerParams(
            collective_id=3, has_side_effects=True, vmem_limit_bytes=62 * 2**20
        ),
    )(order, inverse, d_att, att, active, rows_w, o_t, scale, q_n, v_n, k_t, cos, sin, d_hidden, probs, n_all)


def back_kernel(
    dm, d_hidden, cols_t, active, att, n_all, g_all, d_normed, g_cols, g_rows, sums,
    turned, turned_r, buf, lhs, psend, acc, far, near, send, recv, loc,
):
    me = Here(send, recv)
    me.greet()

    def operands(p, core):
        return d_hidden[2 * p + core], dm[p, core][:, 0:192]

    total = Total(me, operands, cols_t, d_normed, lhs, psend, acc, far, near)
    sums[...] = jnp.zeros_like(sums)
    def put(r, v):
        g_cols[r, 0:192] = v.T.astype(BF)
        g_cols[r, 192:256] = jnp.zeros((256, 64), BF)

    def put_r(r, v):
        g_rows[:, r] = v.astype(BF)

    def left(p):
        return jnp.concatenate([two_blocks(active)(p), att[p].reshape(256, 128)[:, 0:64]], axis=1)

    side = Outer(n_all, lambda p: dm[p].reshape(256, 256)[:, 0:192], 192, put, turned, buf, loc, sums).parts(4)
    side += Outer(g_all, left, 320, put_r, turned_r, buf, loc).parts(4)
    for f in total.products():
        f()
    weave(total.events(), [(2.0, f) for f in side], 14.0)
    total.finish()
    me.finish()


def back(dm, d_hidden, cols_t, active, att, n_all, g_all):
    return pl.pallas_call(
        back_kernel,
        out_shape=[arr(128, WIDTH, t=F32), arr(WIDTH, 256), arr(320, WIDTH), arr(8, 192, t=F32)],
        in_specs=[VM] * 5 + [ANY] * 2,
        out_specs=[VM] * 4,
        scratch_shapes=[
            vmem(192, LENGTH), vmem(320, LENGTH), vmem(2, 32, 128, 256), vmem(512, 448),
            *SUM_SCRATCH, DMA((60,)), DMA((60,)), DMA((2,)),
        ],
        compiler_params=pltpu.CompilerParams(
            collective_id=5, has_side_effects=True, vmem_limit_bytes=60 * 2**20
        ),
    )(dm, d_hidden, cols_t, active, att, n_all, g_all)


def spot(x, y, zh, zl, c):
    return (zl * 2 + c, (x * 4 + y) * 2 + zh)


def greet(peers):
    barrier = pltpu.get_barrier_semaphore()
    for d in peers:
        pl.semaphore_signal(barrier, inc=1, device_id=d, device_id_type=MESH)
    pl.semaphore_wait(barrier, len(peers))


def grads_kernel(
    cols, rws, vec, cols_out, rows_out, vec_out,
    far, near, mine, total, a1, rfar, rbuf, vp, vs, vx, vy, vq, vz, vr, send, recv,
):
    x, y, zh, zl, c = place()
    z = zh * 2 + zl
    other = spot(x, y, zh, zl, 1 - c)
    started = []
    counter = [0]

    def at(dx, dy):
        return spot(wrap(x + dx), wrap(y + dy), zh, zl, c)

    def at_z(dz):
        w = wrap(z + dz)
        return spot(x, y, w // 2, w % 2, c)

    twin = spot(x, y, zh, 1 - zl, c)
    greet([at(1, 0), at(-1, 0), at(2, 0), at(0, 1), at(0, -1), at(0, 2), at_z(1), at_z(-1), at_z(2), other])

    def new():
        counter[0] += 1
        return counter[0] - 1

    def copy(src, dst, i, to):
        return pltpu.make_async_remote_copy(
            src_ref=src, dst_ref=dst, send_sem=send.at[i], recv_sem=recv.at[i], device_id=to, device_id_type=MESH
        )

    def push(src, dst, to, land):
        i = new()
        cp = copy(src, dst, i, to)
        cp.start()
        started.append(cp)
        return lambda: copy(land, land, i, to).wait_recv()

    def only(test):
        return pl.when(test)

    zf = wrap(z + 2)
    parts = ((1, pl.ds(0, 8)), (-1, pl.ds(8, 8)))
    got_far = [push(cols.at[p, zf], far.at[r], at_z(s), far.at[r]) for r, (s, p) in enumerate(parts)]

    halves = (pl.ds(0, 160), pl.ds(160, 160))
    r_far, r_mid, r_twin, r_core = (new(), new()), new(), new(), (new(), new())
    down, up = at_z(-1), at_z(1)
    receiver = c == zh

    def early(to):
        return [copy(rws.at[halves[k]], rfar.at[k], r_far[k], to) for k in (0, 1)]

    for flag, to in ((0, down), (1, up)):

        @only((c != zh) & (zl == flag))
        def _():
            for cp in early(to):
                cp.start()

    got_v = push(vec, vp, other, vp)

    got_near = []
    for r, (s, p) in enumerate(parts):
        got_far[r]()
        mine[r] = cols[:, wrap(z + s)]
        mine[r, p] = (mine[r, p].astype(F32) + far[r].astype(F32)).astype(BF)
        got_near.append(push(mine.at[r], near.at[r], at_z(s), near.at[r]))

    got_v()
    vs[...] = vp[...] + vec[...]
    waits = [push(vs.at[wrap(x + d)], vx.at[k], at(d, 0), vx.at[k]) for k, d in enumerate((1, -1, 2))]

    for flag, to in ((0, up), (1, down)):

        @only(receiver & (zl == flag))
        def _():
            for cp in early(to):
                cp.wait_recv()
            theirs = 1 - flag
            rbuf[0] = (rws[halves[theirs]].astype(F32) + rfar[theirs].astype(F32)).astype(BF)
            copy(rbuf.at[0], rbuf.at[1], r_mid, to).start()

    for w in waits:
        w()
    vy[...] = vs[x] + vx[0] + vx[1] + vx[2]
    waits = [push(vy.at[wrap(y + d)], vq.at[k], at(0, d), vq.at[k]) for k, d in enumerate((1, -1, 2))]

    for w in got_near:
        w()
    v = cols[:, z].astype(F32) + near[0].astype(F32) + near[1].astype(F32)
    total[...] = v.astype(BF).reshape(4, 4, 32, 512)
    a1[x] = total[x]
    got_x = [push(total.at[wrap(x + d)], a1.at[x], at(d, 0), a1.at[wrap(x - d)]) for d in (1, -1, 2)]

    for w in waits:
        w()
    vz[...] = vy[y] + vq[0] + vq[1] + vq[2]
    waits = [push(vz, vr.at[k], at_z(d), vr.at[k]) for k, d in enumerate((1, -1, 2))]

    for flag, to in ((0, up), (1, down)):

        @only(receiver & (zl == flag))
        def _():
            h = halves[flag]
            copy(rbuf.at[0], rbuf.at[1], r_mid, to).wait()
            v = rws[h].astype(F32) + rfar[flag].astype(F32) + rbuf[1].astype(F32)
            rows_out[h] = v.astype(BF)
            copy(rows_out.at[h], rows_out.at[h], r_twin, to).start()
            copy(rows_out.at[h], rows_out.at[h], r_core[0], other).start()

    for w in got_x:
        w()
    cols_out[c, zl, :, y] = a1[:, y]
    got_y = [
        push(a1.at[:, wrap(y + d)], cols_out.at[c, zl, :, y], at(0, d), cols_out.at[c, zl, :, wrap(y - d)])
        for d in (1, -1, 2)
    ]
    for w in waits:
        w()
    vec_out[...] = vz[...] + vr[0] + vr[1] + vr[2]
    for w in got_y:
        w()
    block = cols_out.at[c, zl]
    got_core = [push(block, block, other, cols_out.at[1 - c, zl])]
    push(block, block, twin, cols_out.at[c, 1 - zl])()
    block = cols_out.at[c, 1 - zl]
    got_core.append(push(block, block, other, cols_out.at[1 - c, 1 - zl]))

    for flag, to in ((0, up), (1, down)):
        h, g = halves[flag], halves[1 - flag]

        @only(receiver & (zl == flag))
        def _():
            copy(rows_out.at[g], rows_out.at[g], r_twin, to).wait_recv()
            copy(rows_out.at[g], rows_out.at[g], r_core[1], other).start()
            copy(rows_out.at[h], rows_out.at[h], r_twin, to).wait_send()
            copy(rows_out.at[h], rows_out.at[h], r_core[0], other).wait_send()
            copy(rows_out.at[g], rows_out.at[g], r_core[1], other).wait_send()

        @only((c != zh) & (zl == flag))
        def _():
            for cp in early(to):
                cp.wait_send()
            copy(rows_out.at[h], rows_out.at[h], r_core[0], other).wait_recv()
            copy(rows_out.at[g], rows_out.at[g], r_core[1], other).wait_recv()

    for w in got_core:
        w()
    for cp in started:
        cp.wait_send()


def grads(cols, rws, vec):
    dma = pltpu.SemaphoreType.DMA

    def vmem(*shape, t=BF):
        return pltpu.VMEM(shape, t)

    return pl.pallas_call(
        grads_kernel,
        out_shape=[
            jax.ShapeDtypeStruct((2, 2, 4, 4, 32, 512), BF),
            jax.ShapeDtypeStruct((320, WIDTH), BF),
            jax.ShapeDtypeStruct((16, 128), F32),
        ],
        in_specs=[VM] * 3,
        out_specs=[VM] * 3,
        scratch_shapes=[
            vmem(2, 8, 32, 512), vmem(2, 16, 32, 512), vmem(2, 16, 32, 512), vmem(4, 4, 32, 512),
            vmem(4, 4, 32, 512), vmem(2, 160, WIDTH), vmem(2, 160, WIDTH), vmem(4, 4, 16, 128, t=F32),
            vmem(4, 4, 16, 128, t=F32), vmem(3, 4, 16, 128, t=F32), vmem(4, 16, 128, t=F32),
            vmem(3, 16, 128, t=F32), vmem(16, 128, t=F32), vmem(3, 16, 128, t=F32), dma((40,)), dma((40,)),
        ],
        compiler_params=pltpu.CompilerParams(
            collective_id=4, has_side_effects=True, vmem_limit_bytes=60 * 2**20
        ),
    )(cols, rws, vec)


def finish_kernel(cols, rws, g_qkv, g_in, g_out, g_back):
    g_back[...] = rws[0:256].astype(F32)
    g_out[...] = rws[256:320].astype(F32)

    def one(p, _):
        for h in (0, 1):
            r = pl.ds(32 * h, 32)
            a, b = cols[0, h, p].astype(F32), cols[1, h, p].astype(F32)
            g_in[r, pl.ds(pl.multiple_of(p * 512, 512), 256)] = a[:, 0:256]
            g_in[r, pl.ds(pl.multiple_of(p * 512 + 256, 256), 256)] = b[:, 0:256]
            for m in range(3):
                k = 256 + 64 * m
                both = jnp.concatenate([a[:, k : k + 64], b[:, k : k + 64]], axis=1)
                g_qkv[r, pl.ds(pl.multiple_of(m * WIDTH + p * 128, 128), 128)] = both
        return 0

    lax.fori_loop(0, 16, one, 0)


def finish(cols, rws):
    def arr(*shape):
        return jax.ShapeDtypeStruct(shape, F32)

    return pl.pallas_call(
        finish_kernel,
        out_shape=[arr(64, 6144), arr(64, 8192), arr(64, WIDTH), arr(256, WIDTH)],
        in_specs=[VM] * 2,
        out_specs=[VM] * 4,
        compiler_params=pltpu.CompilerParams(vmem_limit_bytes=60 * 2**20),
    )(cols, rws)


def layer_norm(tokens, gain, shift):
    mean = jnp.mean(tokens, axis=-1, keepdims=True)
    centred = tokens - mean
    var = jnp.mean(centred * centred, axis=-1, keepdims=True)
    return centred * lax.rsqrt(var + eps_norm) * gain + shift


def body(
    tokens,
    span_order,
    ln_gain,
    ln_bias,
    qkv_weight,
    qkv_bias,
    out_weight,
    out_bias,
    fc1_weight,
    fc1_bias,
    fc2_weight,
    fc2_bias,
    cotangent,
):
    x, y, zh, zl, c = place()
    me = (x * 4 + y) * 2 + c

    tok = tokens.reshape(128, WIDTH)
    g_own = cotangent.reshape(128, WIDTH)
    own = [ln_gain, ln_bias, out_bias, fc2_bias, qkv_bias, jnp.zeros((64,), BF), fc1_bias]
    own = [v.astype(F32) for v in own] + [span_order.reshape(32).astype(F32), jnp.zeros((224,), F32)]
    small = jnp.concatenate(own).reshape(8, 128)
    n_all, fields, active, slope, cols_t, rows_w, small_all, small_other = front(
        tok, small, qkv_weight, fc1_weight, out_weight, fc2_weight
    )
    small_all = small_all.reshape(32, 8, 128)
    gain, shift = small_all[:, 0, :64].reshape(WIDTH), small_all[:, 0, 64:].reshape(WIDTH)
    b_sum = (small_all[:, 1, :64] + small_all[:, 1, 64:]).reshape(WIDTH)
    order = jnp.where(c == zh, span_order.reshape(32), small_other[6, :32].astype(jnp.int32))

    blocks = jnp.arange(32, dtype=jnp.int32)
    inverse = jnp.sum(jnp.where(order[None, :] == blocks[:, None], blocks[None, :], 0), axis=1)
    freq = rope_base ** (-(jnp.arange(16, dtype=F32) * 2.0 / 32))
    angle = jnp.arange(LENGTH, dtype=F32)[None, :] * freq[:, None]
    cos, sin = jnp.cos(angle), jnp.sin(angle)
    g_all, d_hidden, d_att, att, probs, q_n, v_n, k_t, o_t, scale = attend(
        order, inverse, fields.reshape(32, 128, 256), cos, sin, g_own, rows_w, slope
    )
    branch, dm, g_cols_in, sums_in = turn(
        order, inverse, d_att.reshape(32, 128, 128), att, active, rows_w, o_t, scale, q_n, v_n, k_t, cos, sin,
        d_hidden, probs, n_all,
    )
    d_normed, g_cols_m, g_rows, sums_m = back(dm, d_hidden, cols_t, active, att, n_all, g_all)
    g_cols = jnp.concatenate([g_cols_in, g_cols_m], axis=1)
    sums = jnp.concatenate([sums_in[0], sums_m[0]])
    flat = tok.astype(F32)
    block_out = (flat + branch + b_sum).astype(BF).reshape(1, 128, WIDTH)
    _, norm_pull = jax.vjp(layer_norm, flat, gain, shift)
    d_flat, d_gain, d_shift = norm_pull(d_normed)
    d_tokens = (g_own.astype(F32) + d_flat).astype(BF).reshape(1, 128, WIDTH)

    bq = jnp.zeros((3, 32, 64), F32)
    bq = lax.dynamic_update_slice_in_dim(bq, sums[256:].reshape(3, 1, 64), me, 1).reshape(32, 192)
    bi = jnp.zeros((32, 256), F32)
    bi = lax.dynamic_update_slice_in_dim(bi, sums[None, :256], me, 0)
    bo = jnp.sum(g_own.astype(F32), axis=0)
    vec = [v.reshape(32, 64) for v in (d_gain, d_shift, bo)] + [bq, bi, jnp.zeros((32, 384), F32)]
    vec = jnp.concatenate(vec, axis=1).reshape(4, 4, 16, 128)
    cols, rws, vec = grads(g_cols.reshape(16, 4, 32, 512), g_rows, vec)
    g_qkv, g_in, g_out, g_back = finish(cols.reshape(2, 2, 16, 32, 512), rws)
    vec = lax.dynamic_index_in_dim(vec.reshape(2, 1024), zh, 0, keepdims=False)
    return (
        block_out,
        d_tokens,
        vec[:64],
        vec[64:128],
        g_qkv,
        vec[192:384],
        g_out,
        vec[128:192],
        g_in,
        vec[384:640],
        g_back,
        vec[128:192],
    )


def solution(mesh):
    act, rows, vec = P("rep", "shard", None), P("shard", None), P("shard")
    return jax.shard_map(
        body,
        mesh=mesh,
        in_specs=(act, P("rep", None), vec, vec, rows, vec, rows, vec, rows, vec, rows, vec, act),
        out_specs=(act, act, vec, vec, rows, vec, rows, vec, rows, vec, rows, vec),
        check_vma=False,
    )
```

```python
import jax
import jax.numpy as jnp
import numpy as np
from jax import lax
from jax.experimental import pallas as pl
from jax.experimental.pallas import tpu as pltpu
from jax.sharding import PartitionSpec as P

F32 = jnp.float32
BF = jnp.bfloat16
MESH = pl.DeviceIdType.MESH
WIDTH = 2048
LENGTH = 4096
TILE = 512
STRIPS = LENGTH // TILE
eps_norm = 1e-05
rope_base = 10000.0
negative = -1e30
VM = pl.BlockSpec(memory_space=pltpu.VMEM)
SM = pl.BlockSpec(memory_space=pltpu.SMEM)
ANY = pl.BlockSpec(memory_space=pl.ANY)
DMA = pltpu.SemaphoreType.DMA


def vmem(*shape, t=BF):
    return pltpu.VMEM(shape, t)


def arr(*shape, t=BF):
    return jax.ShapeDtypeStruct(shape, t)


def dot(a, b):
    return jnp.dot(a, b, preferred_element_type=F32)


def wrap(v):
    return (v + 4) % 4


def place():
    rep = lax.axis_index("rep")
    sh = lax.axis_index("shard")
    return sh // 8, (sh // 2) % 4, sh % 2, rep // 2, rep % 2


class Here:
    def __init__(self, send, recv):
        self.x, self.y, self.zh, self.zl, self.c = place()
        self.z = self.zh * 2 + self.zl
        self.send, self.recv = send, recv
        self.count = 0
        self.started = []
        self.other = self.spot(self.x, self.y, self.z, 1 - self.c)
        self.beyond = self.at_z(2)
        self.twin = self.spot(self.x, self.y, self.zh * 2 + 1 - self.zl, self.c)

    def spot(self, x, y, z, c):
        return ((z % 2) * 2 + c, (x * 4 + y) * 2 + z // 2)

    def at(self, dx, dy):
        return self.spot(wrap(self.x + dx), wrap(self.y + dy), self.z, self.c)

    def at_z(self, dz):
        return self.spot(self.x, self.y, wrap(self.z + dz), self.c)

    def pair(self, dx, dy):
        return wrap(self.x + dx) * 4 + wrap(self.y + dy)

    def greet(self, far_xy=False, z=False, beyond=False):
        peers = [self.at(1, 0), self.at(-1, 0), self.at(0, 1), self.at(0, -1), self.other]
        if far_xy:
            peers += [self.at(2, 0), self.at(0, 2)]
        if z:
            peers += [self.at_z(1), self.at_z(-1)]
        if beyond:
            peers += [self.beyond]
        barrier = pltpu.get_barrier_semaphore()
        for d in peers:
            pl.semaphore_signal(barrier, inc=1, device_id=d, device_id_type=MESH)
        pl.semaphore_wait(barrier, len(peers))

    def new(self, n=1):
        self.count += n
        return self.count - n

    def copy(self, src, dst, i, to):
        return pltpu.make_async_remote_copy(
            src_ref=src, dst_ref=dst, send_sem=self.send.at[i], recv_sem=self.recv.at[i],
            device_id=to, device_id_type=MESH,
        )

    def go(self, src, dst, i, to):
        cp = self.copy(src, dst, i, to)
        cp.start()
        self.started.append(cp)
        return cp

    def came(self, ref, i):
        self.copy(ref, ref, i, self.other).wait_recv()

    def push(self, src, dst, to, land):
        i = self.new()
        self.go(src, dst, i, to)
        return lambda: self.came(land, i)

    def finish(self):
        for cp in self.started:
            cp.wait_send()


OFFS = [(p, q) for p in (0, -1, 1, 2) for q in (0, -1, 1, 2)]
GROUP = {0: 0, -1: 1, 1: 2, 2: 3}
def rows_of(half, part):
    return pl.ds(half * 64 + (32 if part == 2 else 0), 64 if part == 0 else 32)


class Gather:
    def __init__(self, me, own, out, loc):
        self.me, self.own, self.out, self.loc = me, own, out, loc
        self.link = me.new(40)
        self.core = me.new(32)

    def dev(self, h, da, db):
        return self.me.at(da, db) if h == 0 else self.me.at(db, da)

    def ref(self, h, off, part, core):
        dx, dy = off if h == 0 else (off[1], off[0])
        return self.out.at[self.me.pair(dx, dy) * 2 + core, rows_of(h, part)]

    def pass_on(self, h, role, off, part, to, own=False):
        dst = self.ref(h, off, part, self.me.c)
        src = self.own.at[rows_of(h, part)] if own else dst
        self.me.go(src, dst, self.link + 20 * h + role, self.dev(h, *to))

    def arrived(self, h, role, off, part):
        self.me.came(self.ref(h, off, part, self.me.c), self.link + 20 * h + role)

    def share(self, h, off, own=False):
        dst = self.ref(h, off, 0, self.me.c)
        src = self.own.at[rows_of(h, 0)] if own else dst
        self.me.go(src, dst, self.core + 16 * h + OFFS.index(off), self.me.other)

    def shared(self, off):
        for h in (0, 1):
            o = off if h == 0 else (off[1], off[0])
            self.me.came(self.ref(h, o, 0, 1 - self.me.c), self.core + 16 * h + OFFS.index(o))

    def second(self, h, ao, own=False):
        k = GROUP[ao]
        self.pass_on(h, 4 + 2 * k, (ao, 0), 0, (0, 1), own)
        self.pass_on(h, 5 + 2 * k, (ao, 0), 0, (0, -1), own)

    def near(self, h, ao):
        k = GROUP[ao]
        self.arrived(h, 4 + 2 * k, (ao, -1), 0)
        self.pass_on(h, 12 + 2 * k, (ao, -1), 1, (0, 1))
        self.share(h, (ao, -1))
        self.arrived(h, 5 + 2 * k, (ao, 1), 0)
        self.pass_on(h, 13 + 2 * k, (ao, 1), 2, (0, -1))
        self.share(h, (ao, 1))

    def far(self, h, ao):
        k = GROUP[ao]
        self.arrived(h, 12 + 2 * k, (ao, 2), 1)
        self.arrived(h, 13 + 2 * k, (ao, 2), 2)
        self.share(h, (ao, 2))

    def begin(self):
        p = self.me.pair(0, 0)
        self.local = pltpu.make_async_copy(self.own, self.out.at[p * 2 + self.me.c], self.loc)
        self.local.start()
        for h in (0, 1):
            self.pass_on(h, 0, (0, 0), 0, (1, 0), True)
            self.pass_on(h, 1, (0, 0), 0, (-1, 0), True)
        for h in (0, 1):
            self.second(h, 0, True)
            self.share(h, (0, 0), True)

    def first(self, h):
        self.arrived(h, 0, (-1, 0), 0)
        self.pass_on(h, 2, (-1, 0), 1, (1, 0))
        self.second(h, -1)
        self.share(h, (-1, 0))
        self.arrived(h, 1, (1, 0), 0)
        self.pass_on(h, 3, (1, 0), 2, (-1, 0))
        self.second(h, 1)
        self.share(h, (1, 0))

    def middle(self, h):
        self.arrived(h, 2, (2, 0), 1)
        self.arrived(h, 3, (2, 0), 2)
        self.second(h, 2)
        self.share(h, (2, 0))

    def events(self, start=0.0):
        todo = []
        for h in (0, 1):
            steps = [(6.5, lambda h=h: self.first(h)), (15.5, lambda h=h: self.middle(h))]
            steps += [(t, lambda h=h, o=o: self.near(h, o)) for t, o in ((12.5, 0), (21, -1), (27, 1), (36, 2))]
            steps += [(t, lambda h=h, o=o: self.far(h, o)) for t, o in ((30, 0), (39, -1), (42, 1), (45, 2))]
            todo += [(start + t, f) for t, f in steps]
        return todo


ARRIVALS = (
    (5, (0, 0)), (14, (-1, 0)), (14, (1, 0)), (14, (0, -1)), (14, (0, 1)), (22.5, (-1, -1)), (28.5, (-1, 1)),
    (28.5, (1, -1)), (28.5, (1, 1)), (32, (2, 0)), (32, (0, 2)), (40.5, (-1, 2)), (40.5, (2, -1)),
    (43.5, (1, 2)), (43.5, (2, 1)), (46.5, (2, 2)),
)


class Pairs:
    def __init__(self, gather, buf, loc, work):
        self.gather, self.buf, self.loc, self.work = gather, buf, loc, work
        self.queue, self.step = [], 0

    def take(self, off):
        self.gather.shared(off)
        if off == (0, 0):
            self.gather.local.wait()
        p, k = self.gather.me.pair(*off), self.step % 4
        self.step += 1
        cp = pltpu.make_async_copy(self.gather.out.at[pl.ds(p * 2, 2)], self.buf.at[k], self.loc.at[k])
        cp.start()
        self.queue.append((p, k, cp))
        if len(self.queue) > 3:
            self.run()

    def run(self):
        p, k, cp = self.queue.pop(0)
        cp.wait()
        self.work(p, k)

    def rest(self):
        while self.queue:
            self.run()

    def over(self, k, wa, wb):
        def inner(i, carry):
            va, vb = carry
            cs = pl.ds(pl.multiple_of(i * 512, 512), 512)
            v = self.buf[k, :, :, cs].reshape(256, 512)
            return va + dot(v, wa[cs, :]), vb + dot(v, wb[cs, :])

        start = jnp.zeros((256, wa.shape[1]), F32), jnp.zeros((256, wb.shape[1]), F32)
        return lax.fori_loop(0, 4, inner, start)

    def events(self, start=0.0, least=0.0):
        return [(max(start + t, least) + 1e-3 * i, lambda o=o: self.take(o)) for i, (t, o) in enumerate(ARRIVALS)]


TURN = [(2, 2), (1, 2), (3, 2), (0, 2), (2, 1), (2, 3), (2, 0), (1, 1)]
TURN += [(1, 3), (3, 1), (3, 3), (0, 1), (0, 3), (1, 0), (3, 0), (0, 0)]


class Total:
    def __init__(self, me, operands, w, out, lhs, psend, acc, far, near):
        self.me, self.operands, self.w, self.out, self.lhs = me, operands, w, out, lhs
        self.psend, self.acc, self.far, self.near = psend, acc, far, near
        self.link, self.core = me.new(40), me.new(16)
        self.sent = []

    def dev(self, h, da, db):
        return self.me.at(da, db) if h == 0 else self.me.at(db, da)

    def step_to(self, h, g, s):
        return self.dev(h, 0, s) if g < 4 else self.dev(h, s, 0)

    def sem(self, h, g, role):
        return self.link + 20 * h + 4 * g + role

    def block(self, h, g, o):
        da, db = (g, o) if g < 4 else (o, 0)
        dx, dy = (da, db) if h == 0 else (db, da)
        return (dx % 4) * 4 + dy % 4

    def send_far(self, h, g):
        k = self.block(h, g, 2)
        for role, s in ((0, 1), (1, -1)):
            src, dst = self.acc.at[k, rows_of(h, role + 1)], self.far.at[h, g, role]
            self.me.go(src, dst, self.sem(h, g, role), self.step_to(h, g, s))

    def relay(self, h, g):
        acc = self.acc
        for role, s in ((0, 1), (1, -1)):
            ref = self.far.at[h, g, role]
            self.me.came(ref, self.sem(h, g, role))
            k, r = self.block(h, g, s), rows_of(h, role + 1)
            acc[k, r] = (acc[k, r].astype(F32) + ref[...].astype(F32)).astype(BF)
            src, dst = acc.at[k, rows_of(h, 0)], self.near.at[h, g, role]
            self.me.go(src, dst, self.sem(h, g, 2 + role), self.step_to(h, g, s))

    def land(self, h, g):
        k, r = self.block(h, g, 0), rows_of(h, 0)
        for role in (0, 1):
            self.me.came(self.near.at[h, g, role], self.sem(h, g, 2 + role))
        tot = self.acc[k, r].astype(F32)
        tot = tot + self.near[h, g, 0].astype(F32) + self.near[h, g, 1].astype(F32)
        if g < 4:
            self.acc[k, r] = tot.astype(BF)
        else:
            self.out[r] = tot
        if g == 2:
            self.send_far(h, 4)

    def fill(self, i, core):
        for q in range(4):
            p = self.me.pair(*TURN[4 * i + q])
            a, b = self.operands(p, core)
            r = pl.ds(128 * q, 128)
            self.lhs[r, 0:256] = a
            self.lhs[r, 256 : 256 + b.shape[-1]] = b

    def for_partner(self, i):
        if i >= 2:
            for cp in self.sent[4 * i - 8 : 4 * i - 4]:
                cp.wait_send()
        self.fill(i, 1 - self.me.c)
        s = 4 * (i % 2)

        def tile(t, _):
            cs = pl.ds(pl.multiple_of(t * TILE, TILE), TILE)
            v = dot(self.lhs[...], self.w[:, cs]).astype(BF)
            self.psend[s : s + 4, :, cs] = v.reshape(4, 128, TILE)
            return 0

        lax.fori_loop(0, WIDTH // TILE, tile, 0)
        for q in range(4):
            dx, dy = TURN[4 * i + q]
            k = dx * 4 + dy
            cp = self.me.copy(self.psend.at[s + q], self.acc.at[k], self.core + k, self.me.other)
            cp.start()
            self.sent.append(cp)

    def for_own(self, i):
        turns = TURN[4 * i : 4 * i + 4]
        self.fill(i, self.me.c)
        for dx, dy in turns:
            k = dx * 4 + dy
            self.me.came(self.acc.at[k], self.core + k)

        def tile(t, _):
            cs = pl.ds(pl.multiple_of(t * TILE, TILE), TILE)
            v = dot(self.lhs[...], self.w[:, cs])
            for q, (dx, dy) in enumerate(turns):
                k = dx * 4 + dy
                self.acc[k, :, cs] = (v[128 * q : 128 * q + 128] + self.acc[k, :, cs].astype(F32)).astype(BF)
            return 0

        lax.fori_loop(0, WIDTH // TILE, tile, 0)
        for dx, dy in turns:
            if dy == 2:
                self.send_far(0, dx)
            if dx == 2:
                self.send_far(1, dy)

    def products(self):
        todo = [lambda: self.for_partner(0)]
        for i in range(1, 4):
            todo += [lambda i=i: self.for_partner(i), lambda i=i: self.for_own(i - 1)]
        return todo + [lambda: self.for_own(3)]

    def events(self, start=0.0):
        todo = []
        for h in (0, 1):
            steps = [(t, lambda h=h, g=g: self.relay(h, g)) for t, g in ((9, 2), (13, 1), (16, 3), (19, 0), (45, 4))]
            steps += [(t, lambda h=h, g=g: self.land(h, g)) for t, g in ((25, 2), (31, 1), (37, 3), (43, 0), (52, 4))]
            todo += [(start + t + 0.01 * h, f) for t, f in steps]
        return todo

    def finish(self):
        for cp in self.sent[-8:]:
            cp.wait_send()


SUM_SCRATCH = [
    vmem(8, 128, WIDTH), vmem(16, 128, WIDTH), vmem(2, 5, 2, 32, WIDTH), vmem(2, 5, 2, 64, WIDTH),
]


def weave(events, units, now=0.0):
    events, units = sorted(events, key=lambda e: e[0]), list(units)
    while events or units:
        if events and (not units or events[0][0] <= now):
            due, f = events.pop(0)
            now = max(now, due) + 0.2
        else:
            cost, f = units.pop(0)
            now += cost
        more = f()
        if isinstance(more, list):
            events += [(now + later, g) for later, g in more]
        events.sort(key=lambda e: e[0])


def pick(read, which):
    v = read(0)
    for p in range(1, 32):
        v = jnp.where(which == p, read(p), v)
    return v


def spin(v, cos, sin):
    a, b = v[0:16], v[16:32]
    return jnp.concatenate([a * cos - b * sin, b * cos + a * sin, v[32:]], axis=0)


def gelu_both(u):
    k0, k1 = 0.7978845608028654, 0.044715
    sq = u * u
    t = jnp.tanh(k0 * u * (1.0 + k1 * sq))
    half = 0.5 * (1.0 + t)
    return u * half, half + 0.5 * u * (1.0 - t * t) * k0 * (1.0 + 3.0 * k1 * sq)


def front_kernel(
    tok, small, w_qkv, w_in, w_out, w_back,
    n_all, fields, active, slope, cols_t, rows_w, small_all, small_other,
    n_own, hat, buf, f_send, w_f, w_m, wf1, wq1, wf2, wq2, table, bq, send, recv, loc, lsem,
):
    me = Here(send, recv)
    x, y, z, zh, zl, c = me.x, me.y, me.z, me.zh, me.zl, me.c
    me.greet(True, True, True)

    small_all[x, y, zh] = small[...]
    got_small = me.push(small, small_other, me.other, small_other)
    first = [
        me.push(small, small_all.at[x, y, zh], me.at(d, 0), small_all.at[wrap(x - d), y, zh])
        for d in (1, -1, 2)
    ]

    mine = pl.ds(pl.multiple_of(zl * 32, 32), 32)

    def col_copies(dx):
        xx = wrap(x + dx)
        for yy in range(4):
            q = xx * 4 + yy
            lanes = pl.ds(pl.multiple_of((q * 2 + c) * 256, 256), 256)
            yield w_in.at[mine, lanes], wf1.at[yy, x], wf1.at[yy, wrap(x - dx)]
            for m in range(3):
                lanes = pl.ds(pl.multiple_of(m * WIDTH + q * 128, 128), 128)
                yield w_qkv.at[mine, lanes], wq1.at[yy, x, m], wq1.at[yy, wrap(x - dx), m]

    mates = []
    for i, (src, dst, _) in enumerate(col_copies(0)):
        cp = pltpu.make_async_copy(src, dst, lsem.at[i])
        cp.start()
        mates.append(cp)
    waits = [me.push(s, t, me.at(d, 0), land) for d in (1, -1, 2) for s, t, land in col_copies(d)]

    ri = me.new(2)
    to_row = me.spot(x, y, 3 - z, c)

    def far_rows():
        for i, src, part in ((0, w_back, pl.ds(0, 256)), (1, w_out, pl.ds(256, 64))):
            yield me.copy(src, rows_w.at[part], ri + i, to_row)

    def near_rows():
        for i, src, part in ((0, w_back, pl.ds(0, 256)), (1, w_out, pl.ds(256, 64))):
            yield pltpu.make_async_copy(src, rows_w.at[part], lsem.at[16 + i])

    @pl.when(c == zh)
    def _():
        for cp in [*far_rows(), *near_rows()]:
            cp.start()

    def norm(i, _):
        r = pl.ds(pl.multiple_of(i * 32, 32), 32)
        v = tok[r, :].astype(F32)
        v = v - jnp.mean(v, axis=-1, keepdims=True)
        hat[r, :] = v * lax.rsqrt(jnp.mean(v * v, axis=-1, keepdims=True) + eps_norm)
        return 0

    for w in first:
        w()
    line = small_all.at[:, y, zh]
    second = [me.push(line, line, me.at(0, d), small_all.at[:, wrap(y - d), zh]) for d in (1, -1, 2)]
    lax.fori_loop(0, 4, norm, 0)
    for w in waits:
        w()
    for cp in mates:
        cp.wait()
    waits = []
    for d in (1, -1, 2):
        yy, land = wrap(y + d), wrap(y - d)
        waits.append(me.push(wf1.at[yy], wf2.at[:, y, z], me.at(0, d), wf2.at[:, land, z]))
        waits.append(me.push(wq1.at[yy], wq2.at[:, :, y, z], me.at(0, d), wq2.at[:, :, land, z]))
    wf2[:, y, z] = wf1[y]
    wq2[:, :, y, z] = wq1[y]
    for w in second:
        w()
    sheet = small_all.at[:, :, zh]
    me.push(sheet, sheet, me.beyond, small_all.at[:, :, 1 - zh])()
    got_small()
    for j in range(32):
        piece = small_all[j // 8, (j // 2) % 4, j % 2]
        for i in (0, 1):
            table[pl.ds(i, 1), pl.ds(64 * j, 64)] = piece[0:1, 64 * i : 64 * i + 64]

    def affine(i, _):
        r = pl.ds(pl.multiple_of(i * 32, 32), 32)
        n_own[r, :] = (hat[r, :] * table[0:1, :] + table[1:2, :]).astype(BF)
        return 0

    lax.fori_loop(0, 4, affine, 0)
    gather = Gather(me, n_own, n_all, loc.at[4])
    gather.begin()
    for j in range(32):
        piece = small_all[j // 8, (j // 2) % 4, j % 2]
        for i in range(3):
            bq[pl.ds(3 * j + i, 1), 0:64] = piece[2 + i // 2 : 3 + i // 2, 64 * (i % 2) : 64 * (i % 2) + 64]
    quarter = []

    def round_z():
        for w in waits:
            w()
        for s in (1, -1):
            land = wrap(z - s)
            quarter.append(me.push(wf2.at[:, :, z], wf2.at[:, :, z], me.at_z(s), wf2.at[:, :, land]))
            quarter.append(me.push(wq2.at[:, :, :, z], wq2.at[:, :, :, z], me.at_z(s), wq2.at[:, :, :, land]))

    last = []

    def round_z_again():
        for w in quarter:
            w()
        for s, k in ((1, 0), (-1, 2)):
            zz, part, far_z = wrap(z - s), pl.ds(k, 2), wrap(z + 2)
            ref, land = wf2.at[part, :, zz], wf2.at[part, :, far_z]
            last.append(me.push(ref, ref, me.at_z(s), land))
            ref, land = wq2.at[part, :, :, zz], wq2.at[part, :, :, far_z]
            last.append(me.push(ref, ref, me.at_z(s), land))

    def take_columns():
        for w in last:
            w()
        for xx in range(4):
            r = pl.ds(xx * 512, 512)
            w_f[r, :] = wf2[xx].reshape(512, 256)
            for m in range(3):
                v = wq2[xx, m].reshape(512, 128)
                w_m[r, 64 * m : 64 * m + 64] = jnp.where(c == 0, v[:, 0:64], v[:, 64:128])

    here = small_all[x, y, c]
    b_in = jnp.concatenate([here[4:5, :], here[5:6, :]], axis=1)
    t = (x * 4 + y) * 2 + c
    b_m = jnp.concatenate([bq[pl.ds(t + 32 * m, 1), 0:64] for m in range(3)], axis=1)
    fi = me.new(16)

    def work(p, k):
        two = pl.ds(p * 2, 2)
        hidden, mixed = pairs.over(k, w_f, w_m)
        f_send[p, :, :, 0:192] = (mixed + b_m).astype(BF).reshape(2, 128, 192)
        f_send[p, :, :, 192:256] = jnp.zeros((2, 128, 64), BF)
        fields[p, zh] = f_send[p, zh]
        me.go(f_send.at[p, 1 - zh], fields.at[p, zh], fi + p, me.beyond)
        act, grad = gelu_both(hidden + b_in)
        active[two] = act.astype(BF).reshape(2, 128, 256)
        slope[two] = grad.astype(BF).reshape(2, 128, 256)

    pairs = Pairs(gather, buf, loc, work)

    def turn_cols():
        def one(i, _):
            r = pl.ds(pl.multiple_of(i * 256, 256), 256)
            cols_t[0:256, r] = w_f[r, :].astype(F32).T.astype(BF)
            cols_t[256:448, r] = w_m[r, :].astype(F32).T.astype(BF)
            return 0

        lax.fori_loop(0, 8, one, 0)

    events = gather.events() + [(4, round_z), (12.6, round_z_again), (21.1, take_columns), (30.1, turn_cols)]
    weave(events + pairs.events(0, 27.1), [])
    pairs.rest()
    for cp in near_rows():
        @pl.when(c == zh)
        def _():
            cp.wait()

    for cp in far_rows():
        @pl.when(c != zh)
        def _():
            cp.wait_recv()

    def came(p, _):
        me.came(fields.at[p, 1 - zh], fi + p)
        return 0

    lax.fori_loop(0, 16, came, 0)
    me.finish()
    for cp in far_rows():
        @pl.when(c == zh)
        def _():
            cp.wait_send()


def front(tok, small, w_qkv, w_in, w_out, w_back):
    return pl.pallas_call(
        front_kernel,
        out_shape=[
            arr(32, 128, WIDTH), arr(16, 2, 128, 256), arr(32, 128, 256), arr(32, 128, 256),
            arr(448, WIDTH), arr(320, WIDTH), arr(4, 4, 2, 8, 128, t=F32), arr(8, 128, t=F32),
        ],
        in_specs=[VM, VM, ANY, ANY, ANY, ANY],
        out_specs=[ANY] + [VM] * 7,
        scratch_shapes=[
            vmem(128, WIDTH), vmem(128, WIDTH, t=F32), vmem(4, 2, 128, WIDTH), vmem(16, 2, 128, 256), vmem(WIDTH, 256), vmem(WIDTH, 192),
            vmem(4, 4, 32, 256), vmem(4, 4, 3, 32, 128), vmem(4, 4, 4, 32, 256), vmem(4, 3, 4, 4, 32, 128),
            vmem(8, WIDTH, t=F32), vmem(96, 128, t=F32), DMA((180,)), DMA((180,)), DMA((5,)), DMA((18,)),
        ],
        compiler_params=pltpu.CompilerParams(
            collective_id=1, has_side_effects=True, vmem_limit_bytes=60 * 2**20
        ),
    )(tok, small, w_qkv, w_in, w_out, w_back)


def tile_at(i, j):
    return i * (i + 1) // 2 + j


def attend_kernel(
    order, inverse, fields, cos_ref, sin_ref, g_own, rows_w, slope,
    g_all, d_hidden, d_att, att, probs, q_n, v_n, k_t, o_t, scale,
    buf, d_send, a_send, w_ot, w_bt, k_n, q_t, v_t, s_buf, p_buf, send, recv, loc, psem,
):
    me = Here(send, recv)
    zh = me.zh
    me.greet(beyond=True)
    gather = Gather(me, g_own, g_all, loc.at[4])
    gather.begin()
    for ref in (d_send, a_send):
        ref[:, :, :, 64:128] = jnp.zeros((16, 2, 128, 64), BF)
    for ref in (q_n, v_n):
        ref[:, 64:128] = jnp.zeros((LENGTH, 64), BF)

    def turn_rows():
        def one(i, _):
            r = pl.ds(pl.multiple_of(i * 256, 256), 256)
            w_bt[r, :] = rows_w[0:256, r].astype(F32).T.astype(BF)
            w_ot[r, :] = rows_w[256:320, r].astype(F32).T.astype(BF)
            return 0

        lax.fori_loop(0, 8, one, 0)

    def load(begin):
        def one(i, _):
            here = pl.ds(pl.multiple_of(i * 128, 128), 128)
            t = pick(lambda p: fields[p], inverse[i]).astype(F32).T
            cos, sin = cos_ref[:, here], sin_ref[:, here]
            q = spin(t[0:64], cos, sin) * 0.125
            k = spin(t[64:128], cos, sin)
            v = t[128:192]
            q_t[:, here] = q.astype(BF)
            k_t[:, here] = k.astype(BF)
            v_t[:, here] = v.astype(BF)
            q_n[here, 0:64] = q.T.astype(BF)
            k_n[here, :] = k.T.astype(BF)
            v_n[here, 0:64] = v.T.astype(BF)
            return 0

        return lambda: lax.fori_loop(begin, begin + 8, one, 0)

    square = (TILE, TILE)
    allowed = lax.broadcasted_iota(jnp.int32, square, 0) <= lax.broadcasted_iota(jnp.int32, square, 1)
    tops = {}

    def scores(i):
        qs = pl.ds(i * TILE, TILE)
        qt = q_t[:, qs]

        def one(j, top):
            ks = pl.ds(pl.multiple_of(j * TILE, TILE), TILE)
            s = dot(k_n[ks, :], qt)
            s_buf[ks, :] = s
            return jnp.maximum(top, jnp.max(s, axis=0, keepdims=True))

        top = jnp.full((1, TILE), negative, F32)
        if i:
            top = lax.fori_loop(0, i, one, top)
        s = jnp.where(allowed, dot(k_n[qs, :], qt), negative)
        s_buf[qs, :] = s
        tops[i] = jnp.maximum(top, jnp.max(s, axis=0, keepdims=True))

    def out_copy(i, j):
        return pltpu.make_async_copy(p_buf.at[i % 2, j], probs.at[tile_at(i, j)], psem.at[i % 2, j])

    def values(i):
        qs = pl.ds(i * TILE, TILE)
        top = tops[i]
        if i >= 2:
            for j in range(i - 1):
                out_copy(i - 2, j).wait()

        def one(j, carry):
            total, o = carry
            ks = pl.ds(pl.multiple_of(j * TILE, TILE), TILE)
            p = jnp.exp(s_buf[ks, :] - top)
            pb = p.astype(BF)
            p_buf[i % 2, j] = pb
            return total + jnp.sum(p, axis=0, keepdims=True), o + dot(v_t[:, ks], pb)

        start = jnp.zeros((1, TILE), F32), jnp.zeros((64, TILE), F32)
        total, o = lax.fori_loop(0, i + 1, one, start)
        for j in range(i + 1):
            out_copy(i, j).start()
        inv = 1.0 / total
        o_t[:, qs] = o * inv
        scale[0:1, qs] = inv

    ai = me.new()

    def give():
        def one(b, _):
            o = pick(lambda p: o_t[:, 128 * p : 128 * p + 128], order[b])
            a_send[b // 2, lax.rem(b, 2), :, 0:64] = o.T.astype(BF)
            return 0

        lax.fori_loop(0, 32, one, 0)
        att[:, zh] = a_send[:, zh]
        me.go(a_send.at[:, 1 - zh], att.at[:, zh], ai, me.beyond)

    di = me.new(16)

    def work(p, k):
        two = pl.ds(p * 2, 2)
        da, do = pairs.over(k, w_bt, w_ot)
        d_send[p, :, :, 0:64] = do.astype(BF).reshape(2, 128, 64)
        d_att[p, zh] = d_send[p, zh]
        me.go(d_send.at[p, 1 - zh], d_att.at[p, zh], di + p, me.beyond)
        d_hidden[two] = (da * slope[two].reshape(256, 256).astype(F32)).astype(BF).reshape(2, 128, 256)

    pairs = Pairs(gather, buf, loc, work)

    side = [(1.5, turn_rows)] + [(0.8, load(8 * k)) for k in range(4)]
    for i in range(STRIPS):
        side += [(0.25 * (i + 1), lambda i=i: scores(i)), (0.3 * (i + 1), lambda i=i: values(i))]
    side.append((2.0, give))
    weave(gather.events() + pairs.events(0, 5.0), side)
    pairs.rest()
    for i in (STRIPS - 2, STRIPS - 1):
        for j in range(i + 1):
            out_copy(i, j).wait()
    me.came(att.at[:, 1 - zh], ai)

    def came(p, _):
        me.came(d_att.at[p, 1 - zh], di + p)
        return 0

    lax.fori_loop(0, 16, came, 0)
    me.finish()


def attend(order, inverse, fields, cos, sin, g_own, rows_w, slope):
    return pl.pallas_call(
        attend_kernel,
        out_shape=[
            arr(32, 128, WIDTH), arr(32, 128, 256), arr(16, 2, 128, 128), arr(16, 2, 128, 128),
            arr(tile_at(STRIPS, 0), TILE, TILE), arr(LENGTH, 128), arr(LENGTH, 128), arr(64, LENGTH),
            arr(64, LENGTH, t=F32), arr(8, LENGTH, t=F32),
        ],
        in_specs=[SM, SM, VM, VM, VM, VM, VM, VM],
        out_specs=[ANY, VM, VM, VM, ANY] + [VM] * 5,
        scratch_shapes=[
            vmem(4, 2, 128, WIDTH), vmem(16, 2, 128, 128), vmem(16, 2, 128, 128), vmem(WIDTH, 64), vmem(WIDTH, 256),
            vmem(LENGTH, 64), vmem(64, LENGTH), vmem(64, LENGTH), vmem(LENGTH, TILE, t=F32),
            vmem(2, STRIPS, TILE, TILE), DMA((100,)), DMA((100,)), DMA((5,)), DMA((2, STRIPS)),
        ],
        compiler_params=pltpu.CompilerParams(
            collective_id=2, has_side_effects=True, vmem_limit_bytes=60 * 2**20
        ),
    )(order, inverse, fields, cos, sin, g_own, rows_w, slope)


class Outer:
    def __init__(self, src, lhs, height, put, turned, buf, loc, sums=None):
        self.src, self.lhs, self.height, self.put = src, lhs, height, put
        self.turned, self.buf, self.loc, self.sums = turned, buf, loc, sums

    def load(self, t, k):
        cs = pl.ds(pl.multiple_of(t * 256, 256), 256)
        return pltpu.make_async_copy(self.src.at[:, :, cs], self.buf.at[k], self.loc.at[k])

    def prepare(self):
        self.load(0, 0).start()

        def one(p, _):
            v = self.lhs(p).astype(F32)
            if self.sums is not None:
                self.sums[0:1, 0 : self.height] += jnp.sum(v, axis=0, keepdims=True)
            self.turned[0 : self.height, pl.ds(pl.multiple_of(p * 256, 256), 256)] = v.T.astype(BF)
            return 0

        lax.fori_loop(0, 16, one, 0)

    def part(self, begin, end):
        def one(t, _):
            k = lax.rem(t, 2)

            @pl.when(t + 1 < 8)
            def _():
                self.load(t + 1, 1 - k).start()

            self.load(t, k).wait()
            v = dot(self.turned[0 : self.height, :], self.buf[k].reshape(LENGTH, 256))
            self.put(pl.ds(pl.multiple_of(t * 256, 256), 256), v)
            return 0

        lax.fori_loop(begin, end, one, 0)

    def parts(self, n):
        todo = [self.prepare]
        return todo + [lambda i=i: self.part(8 * i // n, 8 * (i + 1) // n) for i in range(n)]


def two_blocks(ref):
    return lambda p: ref[pl.ds(2 * p, 2)].reshape(256, ref.shape[-1])


def turn_kernel(
    order, inverse, d_att, att, active, rows_w, o_t, scale, q_n, v_n, k_t, cos_ref, sin_ref, d_hidden,
    probs, n_all,
    branch, dm, g_cols, sums,
    do_t, p_buf, dk, dv, dq, d_pos, m_send, turned, buf, lhs, psend, acc, far, near, send, recv, loc, psem,
):
    me = Here(send, recv)
    zh = me.zh
    me.greet(beyond=True)

    def operands(p, core):
        return active[2 * p + core], att[p, core][:, 0:64]

    total = Total(me, operands, rows_w, branch, lhs, psend, acc, far, near)
    d_pos[:, :, 192:256] = jnp.zeros((32, 128, 64), BF)
    dk[...] = jnp.zeros_like(dk)
    dv[...] = jnp.zeros_like(dv)
    sums[...] = jnp.zeros_like(sums)

    def load():
        def one(i, _):
            here = pl.ds(pl.multiple_of(i * 128, 128), 128)
            do_t[:, here] = pick(lambda p: d_att[p], inverse[i]).astype(F32).T[0:64]
            return 0

        lax.fori_loop(0, 32, one, 0)

    order_of = [(i, j) for i in range(STRIPS) for j in range(i + 1)]

    def in_copy(n):
        return pltpu.make_async_copy(probs.at[n], p_buf.at[lax.rem(n, 4)], psem.at[lax.rem(n, 4)])

    state = {}

    def strip(i):
        qs = pl.ds(i * TILE, TILE)
        inv = scale[0:1, qs]
        do = do_t[:, qs] * inv
        delta = jnp.sum(do * o_t[:, qs], axis=0, keepdims=True)
        dt = do.astype(BF)
        dn = do.T.astype(BF)
        qn = q_n[qs, 0:64]
        base = tile_at(i, 0)

        def one(j, dq_t):
            n = base + j

            @pl.when(n + 3 < len(order_of))
            def _():
                in_copy(n + 3).start()

            in_copy(n).wait()
            ks = pl.ds(pl.multiple_of(j * TILE, TILE), TILE)
            dp = dot(v_n[ks, 0:64], dt)
            pb = p_buf[lax.rem(n, 4)]
            ds = (pb.astype(F32) * (dp - delta)).astype(BF)
            dk[ks, :] += dot(ds, qn)
            dv[ks, :] += dot(pb, dn)
            return dq_t + dot(k_t[:, ks], ds)

        def piece(begin, end):
            def run():
                start = state.get(i, jnp.zeros((64, TILE), F32))
                state[i] = lax.fori_loop(begin, end, one, start)

            return run

        def last():
            dq[:, qs] = spin(state[i], cos_ref[:, qs], -sin_ref[:, qs]) * 0.125

        return piece, last

    mi = me.new()

    def give():
        def one(i, _):
            here = pl.ds(pl.multiple_of(i * 128, 128), 128)
            k = spin(dk[here, :].T, cos_ref[:, here], -sin_ref[:, here])
            t = jnp.concatenate([dq[:, here], k, dv[here, :].T], axis=0)
            d_pos[i, :, 0:192] = t.T.astype(BF)
            return 0

        lax.fori_loop(0, 32, one, 0)

        def two(b, _):
            m_send[b // 2, lax.rem(b, 2)] = pick(lambda p: d_pos[p], order[b])
            return 0

        lax.fori_loop(0, 32, two, 0)
        dm[:, zh] = m_send[:, zh]
        me.go(m_send.at[:, 1 - zh], dm.at[:, zh], mi, me.beyond)

    side = [(2.0, load)]
    for i in range(STRIPS):

        def make(i=i):
            piece, last = strip(i)
            cuts = [0, i + 1] if i < 4 else [0, (i + 1) // 2, i + 1]
            for a, b in zip(cuts, cuts[1:]):
                yield piece(a, b)
            yield last

        holder = {}

        def begin(i=i, holder=holder, make=make):
            holder["todo"] = list(make())
            holder["todo"].pop(0)()

        def again(holder=holder):
            holder["todo"].pop(0)()

        more = 1 if i < 4 else 2
        side += [(0.8 * (i + 1) / more, begin)] + [(0.8 * (i + 1) / more, again)] * (more - 1) + [(0.2, again)]
    side.append((2.5, give))

    for n in range(3):
        in_copy(n).start()

    def put(r, v):
        g_cols[r, :] = v.T.astype(BF)

    outer = Outer(n_all, two_blocks(d_hidden), 256, put, turned, buf, loc, sums).parts(4)
    side += [(2.0, f) for f in outer]
    for f in total.products():
        f()
    weave(total.events(), side, 14.0)
    me.came(dm.at[:, 1 - zh], mi)
    total.finish()
    me.finish()


def turn(order, inverse, d_att, att, active, rows_w, o_t, scale, q_n, v_n, k_t, cos, sin, d_hidden, probs, n_all):
    return pl.pallas_call(
        turn_kernel,
        out_shape=[
            arr(128, WIDTH, t=F32), arr(16, 2, 128, 256), arr(WIDTH, 256), arr(8, 256, t=F32),
        ],
        in_specs=[SM, SM] + [VM] * 12 + [ANY] * 2,
        out_specs=[VM] * 4,
        scratch_shapes=[
            vmem(64, LENGTH, t=F32), vmem(4, TILE, TILE), vmem(LENGTH, 64, t=F32), vmem(LENGTH, 64, t=F32),
            vmem(64, LENGTH, t=F32), vmem(32, 128, 256), vmem(16, 2, 128, 256), vmem(256, LENGTH), vmem(2, 32, 128, 256), vmem(512, 320),
            *SUM_SCRATCH, DMA((60,)), DMA((60,)), DMA((2,)), DMA((4,)),
        ],
        compiler_params=pltpu.CompilerParams(
            collective_id=3, has_side_effects=True, vmem_limit_bytes=62 * 2**20
        ),
    )(order, inverse, d_att, att, active, rows_w, o_t, scale, q_n, v_n, k_t, cos, sin, d_hidden, probs, n_all)


class Columns:
    def __init__(self, me, cols, out, far, near, mine, total, a1):
        self.me, self.cols, self.out = me, cols, out
        self.far, self.near, self.mine, self.total, self.a1 = far, near, mine, total, a1
        self.parts = ((1, pl.ds(0, 8)), (-1, pl.ds(8, 8)))

    def start(self):
        me, zf = self.me, wrap(self.me.z + 2)
        self.waits = [
            me.push(self.cols.at[p, zf], self.far.at[r], me.at_z(s), self.far.at[r])
            for r, (s, p) in enumerate(self.parts)
        ]
        return [(6.0, self.second)]

    def second(self):
        me, mine, old = self.me, self.mine, self.waits
        self.waits = []
        for r, (s, p) in enumerate(self.parts):
            old[r]()
            mine[r] = self.cols[:, wrap(me.z + s)]
            mine[r, p] = (mine[r, p].astype(F32) + self.far[r].astype(F32)).astype(BF)
            self.waits.append(me.push(mine.at[r], self.near.at[r], me.at_z(s), self.near.at[r]))
        return [(8.0, self.third)]

    def third(self):
        me, total, a1 = self.me, self.total, self.a1
        for w in self.waits:
            w()
        v = self.cols[:, me.z].astype(F32) + self.near[0].astype(F32) + self.near[1].astype(F32)
        total[...] = v.astype(BF).reshape(total.shape)
        a1[me.x] = total[me.x]
        self.waits = [
            me.push(total.at[wrap(me.x + d)], a1.at[me.x], me.at(d, 0), a1.at[wrap(me.x - d)])
            for d in (1, -1, 2)
        ]
        return [(5.0, self.fourth)]

    def fourth(self):
        me, a1, here = self.me, self.a1, self.out.at[self.me.c, self.me.zl]
        for w in self.waits:
            w()
        self.out[me.c, me.zl, :, me.y] = a1[:, me.y]
        self.waits = [
            me.push(a1.at[:, wrap(me.y + d)], here.at[:, me.y], me.at(0, d), here.at[:, wrap(me.y - d)])
            for d in (1, -1, 2)
        ]
        return [(5.0, self.fifth)]

    def fifth(self):
        me, out = self.me, self.out
        for w in self.waits:
            w()
        block = out.at[me.c, me.zl]
        self.core = [me.push(block, block, me.other, out.at[1 - me.c, me.zl])]
        self.waits = [me.push(block, block, me.twin, out.at[me.c, 1 - me.zl])]
        return [(7.0, self.sixth)]

    def sixth(self):
        me, out = self.me, self.out
        self.waits[0]()
        block = out.at[me.c, 1 - me.zl]
        self.core.append(me.push(block, block, me.other, out.at[1 - me.c, 1 - me.zl]))

    def finish(self):
        for w in self.core:
            w()


class Rows:
    def __init__(self, me, rws, out, far, mid):
        self.me, self.rws, self.out, self.far, self.mid = me, rws, out, far, mid
        self.halves = (pl.ds(0, 160), pl.ds(160, 160))
        self.sem = me.new(6)

    def early(self, to):
        return [
            self.me.copy(self.rws.at[h], self.far.at[k], self.sem + k, to) for k, h in enumerate(self.halves)
        ]

    def across(self, to):
        return self.me.copy(self.mid.at[0], self.mid.at[1], self.sem + 2, to)

    def give(self, h, i, to):
        return self.me.copy(self.out.at[h], self.out.at[h], self.sem + i, to)

    def cases(self, keeps):
        me = self.me
        up, down = me.at_z(1), me.at_z(-1)
        for flag in (0, 1):
            if keeps:
                yield (me.c == me.zh) & (me.zl == flag), flag, (up, down)[flag]
            else:
                yield (me.c != me.zh) & (me.zl == flag), flag, (down, up)[flag]

    def start(self):
        for test, _, to in self.cases(False):

            @pl.when(test)
            def _():
                for cp in self.early(to):
                    cp.start()

        return [(15.0, self.second)]

    def second(self):
        for test, flag, to in self.cases(True):

            @pl.when(test)
            def _():
                for cp in self.early(to):
                    cp.wait_recv()
                k = 1 - flag
                self.mid[0] = (self.rws[self.halves[k]].astype(F32) + self.far[k].astype(F32)).astype(BF)
                self.across(to).start()

        return [(8.0, self.third)]

    def third(self):
        for test, flag, to in self.cases(True):

            @pl.when(test)
            def _():
                h = self.halves[flag]
                self.across(to).wait()
                v = self.rws[h].astype(F32) + self.far[flag].astype(F32) + self.mid[1].astype(F32)
                self.out[h] = v.astype(BF)
                self.give(h, 3, to).start()
                self.give(h, 4, self.me.other).start()

        return [(8.0, self.fourth)]

    def fourth(self):
        for test, flag, to in self.cases(True):

            @pl.when(test)
            def _():
                h, g = self.halves[flag], self.halves[1 - flag]
                self.give(g, 3, to).wait_recv()
                self.give(g, 5, self.me.other).start()
                self.give(h, 3, to).wait_send()
                self.give(h, 4, self.me.other).wait_send()
                self.give(g, 5, self.me.other).wait_send()

        for test, flag, to in self.cases(False):

            @pl.when(test)
            def _():
                h, g = self.halves[flag], self.halves[1 - flag]
                for cp in self.early(to):
                    cp.wait_send()
                self.give(h, 4, self.me.other).wait_recv()
                self.give(g, 5, self.me.other).wait_recv()


class Vectors:
    def __init__(self, me, own, out, vp, vx, vy, vq, vz, vr):
        self.me, self.own, self.out = me, own, out
        self.vp, self.vx, self.vy, self.vq, self.vz, self.vr = vp, vx, vy, vq, vz, vr

    def done(self):
        for w in self.waits:
            w()

    def start(self):
        self.waits = [self.me.push(self.own, self.vp, self.me.other, self.vp)]
        return [(1.5, self.along_x)]

    def along_x(self):
        me = self.me
        self.done()
        self.vp[...] = self.vp[...] + self.own[...]
        self.waits = [
            me.push(self.vp.at[wrap(me.x + d)], self.vx.at[k], me.at(d, 0), self.vx.at[k])
            for k, d in enumerate((1, -1, 2))
        ]
        return [(2.0, self.along_y)]

    def along_y(self):
        me = self.me
        self.done()
        self.vy[...] = self.vp[me.x] + self.vx[0] + self.vx[1] + self.vx[2]
        self.waits = [
            me.push(self.vy.at[wrap(me.y + d)], self.vq.at[k], me.at(0, d), self.vq.at[k])
            for k, d in enumerate((1, -1, 2))
        ]
        return [(2.0, self.along_z)]

    def along_z(self):
        me = self.me
        self.done()
        self.vz[...] = self.vy[me.y] + self.vq[0] + self.vq[1] + self.vq[2]
        self.waits = [
            me.push(self.vz, self.vr.at[k], me.at_z(d), self.vr.at[k]) for k, d in enumerate((1, -1, 2))
        ]

    def finish(self):
        self.done()
        self.out[...] = self.vz[...] + self.vr[0] + self.vr[1] + self.vr[2]


def back_kernel(
    dm, d_hidden, cols_t, active, att, cols_in, sums_in, tok, g_own, gain, n_all, g_all,
    d_tok, out_in, out_m, out_rows, out_vec,
    d_normed, cols_m, rws, sums, line, vec, turned, turned_r, buf, lhs, psend, acc, far, near,
    c_far, c_near, c_mine, c_total, c_a1, r_far, r_mid, vp, vx, vy, vq, vz, vr, send, recv, loc,
):
    me = Here(send, recv)
    me.greet(True, True, True)

    def operands(p, core):
        return d_hidden[2 * p + core], dm[p, core][:, 0:192]

    total = Total(me, operands, cols_t, d_normed, lhs, psend, acc, far, near)
    strips = [
        Columns(me, ref, out, c_far.at[i], c_near.at[i], c_mine.at[i], c_total.at[i], c_a1.at[i])
        for i, (ref, out) in enumerate(((cols_in, out_in), (cols_m, out_m)))
    ]
    rows = Rows(me, rws, out_rows, r_far, r_mid)
    vectors = Vectors(me, vec, out_vec, vp, vx, vy, vq, vz, vr)
    strips[0].start()
    sums[...] = jnp.zeros_like(sums)
    line[...] = jnp.zeros_like(line)
    vec[...] = jnp.zeros_like(vec)

    def put(r, v):
        flat = v.T.astype(BF)
        q = r.start // 128
        for k in (0, 1):
            cols_m[q + k, :, :, 0:192] = flat[128 * k : 128 * k + 128].reshape(4, 32, 192)
            cols_m[q + k, :, :, 192:256] = jnp.zeros((4, 32, 64), BF)

    def put_r(r, v):
        rws[:, r] = v.astype(BF)

    def left(p):
        return jnp.concatenate([two_blocks(active)(p), att[p].reshape(256, 128)[:, 0:64]], axis=1)

    def norm_back():
        def one(i, _):
            r = pl.ds(pl.multiple_of(i * 32, 32), 32)
            v, g, d = tok[r, :].astype(F32), g_own[r, :].astype(F32), d_normed[r, :]
            v = v - jnp.mean(v, axis=-1, keepdims=True)
            s = lax.rsqrt(jnp.mean(v * v, axis=-1, keepdims=True) + eps_norm)
            hat = v * s
            e = d * gain[...]
            e = e - jnp.mean(e, axis=-1, keepdims=True) - hat * jnp.mean(e * hat, axis=-1, keepdims=True)
            d_tok[r, :] = (g + s * e).astype(BF)
            line[0:1, :] += jnp.sum(d * hat, axis=0, keepdims=True)
            line[1:2, :] += jnp.sum(d, axis=0, keepdims=True)
            line[2:3, :] += jnp.sum(g, axis=0, keepdims=True)
            return 0

        lax.fori_loop(0, 4, one, 0)
        for j in range(32):
            q, base = vec.at[j // 8, (j // 2) % 4], 8 * (j % 2)
            ls = pl.ds(64 * j, 64)
            q[base : base + 1, 0:64] = line[0:1, ls]
            q[base : base + 1, 64:128] = line[1:2, ls]
            q[base + 1 : base + 2, 0:64] = line[2:3, ls]
        t = (me.x * 4 + me.y) * 2 + me.c
        for k in (0, 1):
            vec[me.x, me.y, pl.ds(8 * me.c + 3 + k, 1), :] = sums_in[0:1, 128 * k : 128 * k + 128]
        for m in range(3):
            f = t + 32 * m
            j = f // 3
            v = sums[0:1, 64 * m : 64 * m + 64]
            for i, (row, lane) in enumerate(((1, 64), (2, 0), (2, 64))):

                @pl.when(f % 3 == i)
                def _():
                    vec[j // 8, (j // 2) % 4, pl.ds(8 * (j % 2) + row, 1), lane : lane + 64] = v

        return [(0.0, vectors.start)]

    units = Outer(g_all, left, 320, put_r, turned_r, buf, loc).parts(4) + [rows.start]
    units += Outer(n_all, lambda p: dm[p].reshape(256, 256)[:, 0:192], 192, put, turned, buf, loc, sums).parts(4)
    units += [strips[1].start]
    for f in total.products():
        f()
    events = total.events() + [(14.0, strips[0].second), (52.5, norm_back)]
    weave(events, [(2.0, f) for f in units], 14.0)
    vectors.finish()
    for s in strips:
        s.finish()
    total.finish()
    me.finish()


def back(*operands):
    wide = [vmem(2, 2, 8, 32, 256), vmem(2, 2, 16, 32, 256), vmem(2, 2, 16, 32, 256)]
    return pl.pallas_call(
        back_kernel,
        out_shape=[
            arr(128, WIDTH), arr(2, 2, 4, 4, 32, 256), arr(2, 2, 4, 4, 32, 256), arr(320, WIDTH),
            arr(16, 128, t=F32),
        ],
        in_specs=[VM] * 10 + [ANY] * 2,
        out_specs=[VM] * 5,
        scratch_shapes=[
            vmem(128, WIDTH, t=F32), vmem(16, 4, 32, 256), vmem(320, WIDTH), vmem(8, 192, t=F32),
            vmem(8, WIDTH, t=F32), vmem(4, 4, 16, 128, t=F32), vmem(192, LENGTH), vmem(320, LENGTH),
            vmem(2, 32, 128, 256), vmem(512, 448), *SUM_SCRATCH,
            *wide, vmem(2, 4, 4, 32, 256), vmem(2, 4, 4, 32, 256), vmem(2, 160, WIDTH), vmem(2, 160, WIDTH),
            vmem(4, 4, 16, 128, t=F32), vmem(3, 4, 16, 128, t=F32), vmem(4, 16, 128, t=F32),
            vmem(3, 16, 128, t=F32), vmem(16, 128, t=F32), vmem(3, 16, 128, t=F32),
            DMA((110,)), DMA((110,)), DMA((2,)),
        ],
        compiler_params=pltpu.CompilerParams(
            collective_id=4, has_side_effects=True, vmem_limit_bytes=62 * 2**20
        ),
    )(*operands)


def finish_kernel(cols_in, cols_m, rws, g_qkv, g_in, g_out, g_back):
    g_back[...] = rws[0:256].astype(F32)
    g_out[...] = rws[256:320].astype(F32)

    def one(p, _):
        for h in (0, 1):
            r = pl.ds(32 * h, 32)
            g_in[r, pl.ds(pl.multiple_of(p * 512, 512), 256)] = cols_in[0, h, p].astype(F32)
            g_in[r, pl.ds(pl.multiple_of(p * 512 + 256, 256), 256)] = cols_in[1, h, p].astype(F32)
            a, b = cols_m[0, h, p].astype(F32), cols_m[1, h, p].astype(F32)
            for m in range(3):
                k = 64 * m
                both = jnp.concatenate([a[:, k : k + 64], b[:, k : k + 64]], axis=1)
                g_qkv[r, pl.ds(pl.multiple_of(m * WIDTH + p * 128, 128), 128)] = both
        return 0

    lax.fori_loop(0, 16, one, 0)


def finish(cols_in, cols_m, rws):
    return pl.pallas_call(
        finish_kernel,
        out_shape=[arr(64, 6144, t=F32), arr(64, 8192, t=F32), arr(64, WIDTH, t=F32), arr(256, WIDTH, t=F32)],
        in_specs=[VM] * 3,
        out_specs=[VM] * 4,
        compiler_params=pltpu.CompilerParams(vmem_limit_bytes=60 * 2**20),
    )(cols_in, cols_m, rws)


def body(
    tokens,
    span_order,
    ln_gain,
    ln_bias,
    qkv_weight,
    qkv_bias,
    out_weight,
    out_bias,
    fc1_weight,
    fc1_bias,
    fc2_weight,
    fc2_bias,
    cotangent,
):
    x, y, zh, zl, c = place()

    tok = tokens.reshape(128, WIDTH)
    g_own = cotangent.reshape(128, WIDTH)
    own = [ln_gain, ln_bias, out_bias, fc2_bias, qkv_bias, jnp.zeros((64,), BF), fc1_bias]
    own = [v.astype(F32) for v in own] + [span_order.reshape(32).astype(F32), jnp.zeros((224,), F32)]
    small = jnp.concatenate(own).reshape(8, 128)
    n_all, fields, active, slope, cols_t, rows_w, small_all, small_other = front(
        tok, small, qkv_weight, fc1_weight, out_weight, fc2_weight
    )
    small_all = small_all.reshape(32, 8, 128)
    gain = small_all[:, 0, :64].reshape(WIDTH)
    b_sum = (small_all[:, 1, :64] + small_all[:, 1, 64:]).reshape(WIDTH)
    order = jnp.where(c == zh, span_order.reshape(32), small_other[6, :32].astype(jnp.int32))

    blocks = jnp.arange(32, dtype=jnp.int32)
    inverse = jnp.sum(jnp.where(order[None, :] == blocks[:, None], blocks[None, :], 0), axis=1)
    freq = rope_base ** (-np.arange(16) * 2.0 / 32)
    angle = np.arange(LENGTH)[None, :] * freq[:, None]
    cos, sin = jnp.asarray(np.cos(angle), F32), jnp.asarray(np.sin(angle), F32)
    g_all, d_hidden, d_att, att, probs, q_n, v_n, k_t, o_t, scale = attend(
        order, inverse, fields.reshape(32, 128, 256), cos, sin, g_own, rows_w, slope
    )
    branch, dm, g_cols_in, sums_in = turn(
        order, inverse, d_att.reshape(32, 128, 128), att, active, rows_w, o_t, scale, q_n, v_n, k_t, cos, sin,
        d_hidden, probs, n_all,
    )
    d_tokens, cols_in, cols_m, rws, vec = back(
        dm, d_hidden, cols_t, active, att, g_cols_in.reshape(16, 4, 32, 256), sums_in, tok, g_own,
        gain.reshape(1, WIDTH), n_all, g_all,
    )
    d_tokens = d_tokens.reshape(1, 128, WIDTH)
    block_out = (tok.astype(F32) + branch + b_sum).astype(BF).reshape(1, 128, WIDTH)
    g_qkv, g_in, g_out, g_back = finish(
        cols_in.reshape(2, 2, 16, 32, 256), cols_m.reshape(2, 2, 16, 32, 256), rws
    )
    vec = lax.dynamic_index_in_dim(vec.reshape(2, 1024), zh, 0, keepdims=False)
    return (
        block_out,
        d_tokens,
        vec[:64],
        vec[64:128],
        g_qkv,
        vec[192:384],
        g_out,
        vec[128:192],
        g_in,
        vec[384:640],
        g_back,
        vec[128:192],
    )


def solution(mesh):
    act, rows, vec = P("rep", "shard", None), P("shard", None), P("shard")
    return jax.shard_map(
        body,
        mesh=mesh,
        in_specs=(act, P("rep", None), vec, vec, rows, vec, rows, vec, rows, vec, rows, vec, act),
        out_specs=(act, act, vec, vec, rows, vec, rows, vec, rows, vec, rows, vec),
        check_vma=False,
    )
```

```python
import jax
import jax.numpy as jnp
import numpy as np
from jax import lax
from jax.experimental import pallas as pl
from jax.experimental.pallas import tpu as pltpu
from jax.sharding import PartitionSpec as P

F32 = jnp.float32
BF = jnp.bfloat16
MESH = pl.DeviceIdType.MESH
WIDTH = 2048
LENGTH = 4096
TILE = 512
STRIPS = LENGTH // TILE
eps_norm = 1e-05
rope_base = 10000.0
negative = -1e30
VM = pl.BlockSpec(memory_space=pltpu.VMEM)
SM = pl.BlockSpec(memory_space=pltpu.SMEM)
ANY = pl.BlockSpec(memory_space=pl.ANY)
DMA = pltpu.SemaphoreType.DMA


def vmem(*shape, t=BF):
    return pltpu.VMEM(shape, t)


def arr(*shape, t=BF):
    return jax.ShapeDtypeStruct(shape, t)


def dot(a, b):
    return jnp.dot(a, b, preferred_element_type=F32)


def wrap(v):
    return (v + 4) % 4


def place():
    rep = lax.axis_index("rep")
    sh = lax.axis_index("shard")
    return sh // 8, (sh // 2) % 4, sh % 2, rep // 2, rep % 2


class Here:
    def __init__(self, send, recv):
        self.x, self.y, self.zh, self.zl, self.c = place()
        self.z = self.zh * 2 + self.zl
        self.send, self.recv = send, recv
        self.count = 0
        self.started = []
        self.other = self.spot(self.x, self.y, self.z, 1 - self.c)
        self.beyond = self.at_z(2)
        self.twin = self.spot(self.x, self.y, self.zh * 2 + 1 - self.zl, self.c)

    def spot(self, x, y, z, c):
        return ((z % 2) * 2 + c, (x * 4 + y) * 2 + z // 2)

    def at(self, dx, dy):
        return self.spot(wrap(self.x + dx), wrap(self.y + dy), self.z, self.c)

    def at_z(self, dz):
        return self.spot(self.x, self.y, wrap(self.z + dz), self.c)

    def pair(self, dx, dy):
        return wrap(self.x + dx) * 4 + wrap(self.y + dy)

    def greet(self, far_xy=False, z=False, beyond=False):
        peers = [self.at(1, 0), self.at(-1, 0), self.at(0, 1), self.at(0, -1), self.other]
        if far_xy:
            peers += [self.at(2, 0), self.at(0, 2)]
        if z:
            peers += [self.at_z(1), self.at_z(-1)]
        if beyond:
            peers += [self.beyond]
        barrier = pltpu.get_barrier_semaphore()
        for d in peers:
            pl.semaphore_signal(barrier, inc=1, device_id=d, device_id_type=MESH)
        pl.semaphore_wait(barrier, len(peers))

    def new(self, n=1):
        self.count += n
        return self.count - n

    def copy(self, src, dst, i, to):
        return pltpu.make_async_remote_copy(
            src_ref=src, dst_ref=dst, send_sem=self.send.at[i], recv_sem=self.recv.at[i],
            device_id=to, device_id_type=MESH,
        )

    def go(self, src, dst, i, to):
        cp = self.copy(src, dst, i, to)
        cp.start()
        self.started.append(cp)
        return cp

    def came(self, ref, i):
        self.copy(ref, ref, i, self.other).wait_recv()

    def push(self, src, dst, to, land):
        i = self.new()
        self.go(src, dst, i, to)
        return lambda: self.came(land, i)

    def finish(self):
        for cp in self.started:
            cp.wait_send()


OFFS = [(p, q) for p in (0, -1, 1, 2) for q in (0, -1, 1, 2)]
GROUP = {0: 0, -1: 1, 1: 2, 2: 3}
def rows_of(half, part):
    return pl.ds(half * 64 + (32 if part == 2 else 0), 64 if part == 0 else 32)


class Gather:
    def __init__(self, me, own, out, loc):
        self.me, self.own, self.out, self.loc = me, own, out, loc
        self.link = me.new(40)
        self.core = me.new(32)

    def dev(self, h, da, db):
        return self.me.at(da, db) if h == 0 else self.me.at(db, da)

    def ref(self, h, off, part, core):
        dx, dy = off if h == 0 else (off[1], off[0])
        return self.out.at[self.me.pair(dx, dy) * 2 + core, rows_of(h, part)]

    def pass_on(self, h, role, off, part, to, own=False):
        dst = self.ref(h, off, part, self.me.c)
        src = self.own.at[rows_of(h, part)] if own else dst
        self.me.go(src, dst, self.link + 20 * h + role, self.dev(h, *to))

    def arrived(self, h, role, off, part):
        self.me.came(self.ref(h, off, part, self.me.c), self.link + 20 * h + role)

    def share(self, h, off, own=False):
        dst = self.ref(h, off, 0, self.me.c)
        src = self.own.at[rows_of(h, 0)] if own else dst
        self.me.go(src, dst, self.core + 16 * h + OFFS.index(off), self.me.other)

    def shared(self, off):
        for h in (0, 1):
            o = off if h == 0 else (off[1], off[0])
            self.me.came(self.ref(h, o, 0, 1 - self.me.c), self.core + 16 * h + OFFS.index(o))

    def second(self, h, ao, own=False):
        k = GROUP[ao]
        self.pass_on(h, 4 + 2 * k, (ao, 0), 0, (0, 1), own)
        self.pass_on(h, 5 + 2 * k, (ao, 0), 0, (0, -1), own)

    def near(self, h, ao):
        k = GROUP[ao]
        self.arrived(h, 4 + 2 * k, (ao, -1), 0)
        self.pass_on(h, 12 + 2 * k, (ao, -1), 1, (0, 1))
        self.share(h, (ao, -1))
        self.arrived(h, 5 + 2 * k, (ao, 1), 0)
        self.pass_on(h, 13 + 2 * k, (ao, 1), 2, (0, -1))
        self.share(h, (ao, 1))

    def far(self, h, ao):
        k = GROUP[ao]
        self.arrived(h, 12 + 2 * k, (ao, 2), 1)
        self.arrived(h, 13 + 2 * k, (ao, 2), 2)
        self.share(h, (ao, 2))

    def begin(self):
        p = self.me.pair(0, 0)
        self.local = pltpu.make_async_copy(self.own, self.out.at[p * 2 + self.me.c], self.loc)
        self.local.start()
        for h in (0, 1):
            self.pass_on(h, 0, (0, 0), 0, (1, 0), True)
            self.pass_on(h, 1, (0, 0), 0, (-1, 0), True)
        for h in (0, 1):
            self.second(h, 0, True)
            self.share(h, (0, 0), True)

    def first(self, h):
        self.arrived(h, 0, (-1, 0), 0)
        self.pass_on(h, 2, (-1, 0), 1, (1, 0))
        self.second(h, -1)
        self.share(h, (-1, 0))
        self.arrived(h, 1, (1, 0), 0)
        self.pass_on(h, 3, (1, 0), 2, (-1, 0))
        self.second(h, 1)
        self.share(h, (1, 0))

    def middle(self, h):
        self.arrived(h, 2, (2, 0), 1)
        self.arrived(h, 3, (2, 0), 2)
        self.second(h, 2)
        self.share(h, (2, 0))

    def events(self, start=0.0):
        todo = []
        for h in (0, 1):
            steps = [(6.5, lambda h=h: self.first(h)), (15.5, lambda h=h: self.middle(h))]
            steps += [(t, lambda h=h, o=o: self.near(h, o)) for t, o in ((12.5, 0), (21, -1), (27, 1), (36, 2))]
            steps += [(t, lambda h=h, o=o: self.far(h, o)) for t, o in ((30, 0), (39, -1), (42, 1), (45, 2))]
            todo += [(start + t, f) for t, f in steps]
        return todo


ARRIVALS = (
    (5, (0, 0)), (14, (-1, 0)), (14, (1, 0)), (14, (0, -1)), (14, (0, 1)), (22.5, (-1, -1)), (28.5, (-1, 1)),
    (28.5, (1, -1)), (28.5, (1, 1)), (32, (2, 0)), (32, (0, 2)), (40.5, (-1, 2)), (40.5, (2, -1)),
    (43.5, (1, 2)), (43.5, (2, 1)), (46.5, (2, 2)),
)


class Pairs:
    def __init__(self, gather, buf, loc, work):
        self.gather, self.buf, self.loc, self.work = gather, buf, loc, work
        self.queue, self.step = [], 0

    def take(self, off):
        self.gather.shared(off)
        if off == (0, 0):
            self.gather.local.wait()
        p, k = self.gather.me.pair(*off), self.step % 4
        self.step += 1
        cp = pltpu.make_async_copy(self.gather.out.at[pl.ds(p * 2, 2)], self.buf.at[k], self.loc.at[k])
        cp.start()
        self.queue.append((p, k, cp))
        if len(self.queue) > 1:
            self.run()

    def run(self):
        p, k, cp = self.queue.pop(0)
        cp.wait()
        self.work(p, k)

    def rest(self):
        while self.queue:
            self.run()

    def over(self, k, wa, wb):
        v = self.buf[k].reshape(256, WIDTH)
        return dot(v, wa[...]), dot(v, wb[...])

    def events(self, start=0.0, least=0.0):
        return [(max(start + t, least) + 1e-3 * i, lambda o=o: self.take(o)) for i, (t, o) in enumerate(ARRIVALS)]


TURN = [(2, 2), (1, 2), (3, 2), (0, 2), (2, 1), (2, 3), (2, 0), (1, 1)]
TURN += [(1, 3), (3, 1), (3, 3), (0, 1), (0, 3), (1, 0), (3, 0), (0, 0)]


class Total:
    def __init__(self, me, operands, w, out, lhs, psend, acc, far, near):
        self.me, self.operands, self.w, self.out, self.lhs = me, operands, w, out, lhs
        self.psend, self.acc, self.far, self.near = psend, acc, far, near
        self.link, self.core = me.new(40), me.new(16)
        self.sent = []

    def dev(self, h, da, db):
        return self.me.at(da, db) if h == 0 else self.me.at(db, da)

    def step_to(self, h, g, s):
        return self.dev(h, 0, s) if g < 4 else self.dev(h, s, 0)

    def sem(self, h, g, role):
        return self.link + 20 * h + 4 * g + role

    def block(self, h, g, o):
        da, db = (g, o) if g < 4 else (o, 0)
        dx, dy = (da, db) if h == 0 else (db, da)
        return (dx % 4) * 4 + dy % 4

    def send_far(self, h, g):
        k = self.block(h, g, 2)
        for role, s in ((0, 1), (1, -1)):
            src, dst = self.acc.at[k, rows_of(h, role + 1)], self.far.at[h, g, role]
            self.me.go(src, dst, self.sem(h, g, role), self.step_to(h, g, s))

    def relay(self, h, g):
        acc = self.acc
        for role, s in ((0, 1), (1, -1)):
            ref = self.far.at[h, g, role]
            self.me.came(ref, self.sem(h, g, role))
            k, r = self.block(h, g, s), rows_of(h, role + 1)
            acc[k, r] = (acc[k, r].astype(F32) + ref[...].astype(F32)).astype(BF)
            src, dst = acc.at[k, rows_of(h, 0)], self.near.at[h, g, role]
            self.me.go(src, dst, self.sem(h, g, 2 + role), self.step_to(h, g, s))

    def land(self, h, g):
        k, r = self.block(h, g, 0), rows_of(h, 0)
        for role in (0, 1):
            self.me.came(self.near.at[h, g, role], self.sem(h, g, 2 + role))
        tot = self.acc[k, r].astype(F32)
        tot = tot + self.near[h, g, 0].astype(F32) + self.near[h, g, 1].astype(F32)
        if g < 4:
            self.acc[k, r] = tot.astype(BF)
        else:
            self.out[r] = tot
        if g == 2:
            self.send_far(h, 4)

    def fill(self, i, core):
        for q in range(4):
            p = self.me.pair(*TURN[4 * i + q])
            a, b = self.operands(p, core)
            r = pl.ds(128 * q, 128)
            self.lhs[r, 0:256] = a
            self.lhs[r, 256 : 256 + b.shape[-1]] = b

    def for_partner(self, i):
        if i >= 2:
            for cp in self.sent[4 * i - 8 : 4 * i - 4]:
                cp.wait_send()
        self.fill(i, 1 - self.me.c)
        s = 4 * (i % 2)

        def tile(t, _):
            cs = pl.ds(pl.multiple_of(t * TILE, TILE), TILE)
            v = dot(self.lhs[...], self.w[:, cs]).astype(BF)
            self.psend[s : s + 4, :, cs] = v.reshape(4, 128, TILE)
            return 0

        lax.fori_loop(0, WIDTH // TILE, tile, 0)
        for q in range(4):
            dx, dy = TURN[4 * i + q]
            k = dx * 4 + dy
            cp = self.me.copy(self.psend.at[s + q], self.acc.at[k], self.core + k, self.me.other)
            cp.start()
            self.sent.append(cp)

    def for_own(self, i):
        turns = TURN[4 * i : 4 * i + 4]
        self.fill(i, self.me.c)
        for dx, dy in turns:
            k = dx * 4 + dy
            self.me.came(self.acc.at[k], self.core + k)

        def tile(t, _):
            cs = pl.ds(pl.multiple_of(t * TILE, TILE), TILE)
            v = dot(self.lhs[...], self.w[:, cs])
            for q, (dx, dy) in enumerate(turns):
                k = dx * 4 + dy
                self.acc[k, :, cs] = (v[128 * q : 128 * q + 128] + self.acc[k, :, cs].astype(F32)).astype(BF)
            return 0

        lax.fori_loop(0, WIDTH // TILE, tile, 0)
        for dx, dy in turns:
            if dy == 2:
                self.send_far(0, dx)
            if dx == 2:
                self.send_far(1, dy)

    def products(self):
        todo = [lambda: self.for_partner(0)]
        for i in range(1, 4):
            todo += [lambda i=i: self.for_partner(i), lambda i=i: self.for_own(i - 1)]
        return todo + [lambda: self.for_own(3)]

    def events(self, start=0.0):
        todo = []
        for h in (0, 1):
            steps = [(t, lambda h=h, g=g: self.relay(h, g)) for t, g in ((9, 2), (13, 1), (16, 3), (19, 0), (45, 4))]
            steps += [(t, lambda h=h, g=g: self.land(h, g)) for t, g in ((25, 2), (31, 1), (37, 3), (43, 0), (52, 4))]
            todo += [(start + t + 0.01 * h, f) for t, f in steps]
        return todo

    def finish(self):
        for cp in self.sent[-8:]:
            cp.wait_send()


SUM_SCRATCH = [
    vmem(8, 128, WIDTH), vmem(16, 128, WIDTH), vmem(2, 5, 2, 32, WIDTH), vmem(2, 5, 2, 64, WIDTH),
]


def weave(events, units, now=0.0):
    events, units = sorted(events, key=lambda e: e[0]), list(units)
    while events or units:
        if events and (not units or events[0][0] <= now):
            due, f = events.pop(0)
            now = max(now, due) + 0.2
        else:
            cost, f = units.pop(0)
            now += cost
        more = f()
        if isinstance(more, list):
            events += [(now + later, g) for later, g in more]
        events.sort(key=lambda e: e[0])


def pick(read, which):
    v = read(0)
    for p in range(1, 32):
        v = jnp.where(which == p, read(p), v)
    return v


def spin(v, cos, sin):
    a, b = v[0:16], v[16:32]
    return jnp.concatenate([a * cos - b * sin, b * cos + a * sin, v[32:]], axis=0)


def gelu_both(u):
    k0, k1 = 0.7978845608028654, 0.044715
    sq = u * u
    t = jnp.tanh(k0 * u * (1.0 + k1 * sq))
    half = 0.5 * (1.0 + t)
    return u * half, half + 0.5 * u * (1.0 - t * t) * k0 * (1.0 + 3.0 * k1 * sq)


def front_kernel(
    tok, small, w_qkv, w_in, w_out, w_back,
    n_all, fields, active, slope, cols_t, rows_w, small_all, small_other,
    n_own, hat, buf, f_send, w_f, w_m, wf1, wq1, wf2, wq2, table, bq, send, recv, loc, lsem,
):
    me = Here(send, recv)
    x, y, z, zh, zl, c = me.x, me.y, me.z, me.zh, me.zl, me.c
    me.greet(True, True, True)

    small_all[x, y, zh] = small[...]
    got_small = me.push(small, small_other, me.other, small_other)
    first = [
        me.push(small, small_all.at[x, y, zh], me.at(d, 0), small_all.at[wrap(x - d), y, zh])
        for d in (1, -1, 2)
    ]

    mine = pl.ds(pl.multiple_of(zl * 32, 32), 32)

    def col_copies(dx):
        xx = wrap(x + dx)
        for yy in range(4):
            q = xx * 4 + yy
            lanes = pl.ds(pl.multiple_of((q * 2 + c) * 256, 256), 256)
            yield w_in.at[mine, lanes], wf1.at[yy, x], wf1.at[yy, wrap(x - dx)]
            for m in range(3):
                lanes = pl.ds(pl.multiple_of(m * WIDTH + q * 128, 128), 128)
                yield w_qkv.at[mine, lanes], wq1.at[yy, x, m], wq1.at[yy, wrap(x - dx), m]

    mates = []
    for i, (src, dst, _) in enumerate(col_copies(0)):
        cp = pltpu.make_async_copy(src, dst, lsem.at[i])
        cp.start()
        mates.append(cp)
    waits = [me.push(s, t, me.at(d, 0), land) for d in (1, -1, 2) for s, t, land in col_copies(d)]

    ri = me.new(2)
    to_row = me.spot(x, y, 3 - z, c)

    def far_rows():
        for i, src, part in ((0, w_back, pl.ds(0, 256)), (1, w_out, pl.ds(256, 64))):
            yield me.copy(src, rows_w.at[part], ri + i, to_row)

    def near_rows():
        for i, src, part in ((0, w_back, pl.ds(0, 256)), (1, w_out, pl.ds(256, 64))):
            yield pltpu.make_async_copy(src, rows_w.at[part], lsem.at[16 + i])

    @pl.when(c == zh)
    def _():
        for cp in [*far_rows(), *near_rows()]:
            cp.start()

    def norm(i, _):
        r = pl.ds(pl.multiple_of(i * 32, 32), 32)
        v = tok[r, :].astype(F32)
        v = v - jnp.mean(v, axis=-1, keepdims=True)
        hat[r, :] = v * lax.rsqrt(jnp.mean(v * v, axis=-1, keepdims=True) + eps_norm)
        return 0

    for w in first:
        w()
    line = small_all.at[:, y, zh]
    second = [me.push(line, line, me.at(0, d), small_all.at[:, wrap(y - d), zh]) for d in (1, -1, 2)]
    lax.fori_loop(0, 4, norm, 0)
    for w in waits:
        w()
    for cp in mates:
        cp.wait()
    waits = []
    for d in (1, -1, 2):
        yy, land = wrap(y + d), wrap(y - d)
        waits.append(me.push(wf1.at[yy], wf2.at[:, y, z], me.at(0, d), wf2.at[:, land, z]))
        waits.append(me.push(wq1.at[yy], wq2.at[:, :, y, z], me.at(0, d), wq2.at[:, :, land, z]))
    wf2[:, y, z] = wf1[y]
    wq2[:, :, y, z] = wq1[y]
    for w in second:
        w()
    sheet = small_all.at[:, :, zh]
    me.push(sheet, sheet, me.beyond, small_all.at[:, :, 1 - zh])()
    got_small()
    for j in range(32):
        piece = small_all[j // 8, (j // 2) % 4, j % 2]
        for i in (0, 1):
            table[pl.ds(i, 1), pl.ds(64 * j, 64)] = piece[0:1, 64 * i : 64 * i + 64]

    def affine(i, _):
        r = pl.ds(pl.multiple_of(i * 32, 32), 32)
        n_own[r, :] = (hat[r, :] * table[0:1, :] + table[1:2, :]).astype(BF)
        return 0

    lax.fori_loop(0, 4, affine, 0)
    gather = Gather(me, n_own, n_all, loc.at[4])
    gather.begin()
    for j in range(32):
        piece = small_all[j // 8, (j // 2) % 4, j % 2]
        for i in range(3):
            bq[pl.ds(3 * j + i, 1), 0:64] = piece[2 + i // 2 : 3 + i // 2, 64 * (i % 2) : 64 * (i % 2) + 64]
    quarter = []

    def round_z():
        for w in waits:
            w()
        for s in (1, -1):
            land = wrap(z - s)
            quarter.append(me.push(wf2.at[:, :, z], wf2.at[:, :, z], me.at_z(s), wf2.at[:, :, land]))
            quarter.append(me.push(wq2.at[:, :, :, z], wq2.at[:, :, :, z], me.at_z(s), wq2.at[:, :, :, land]))

    last = []

    def round_z_again():
        for w in quarter:
            w()
        for s, k in ((1, 0), (-1, 2)):
            zz, part, far_z = wrap(z - s), pl.ds(k, 2), wrap(z + 2)
            ref, land = wf2.at[part, :, zz], wf2.at[part, :, far_z]
            last.append(me.push(ref, ref, me.at_z(s), land))
            ref, land = wq2.at[part, :, :, zz], wq2.at[part, :, :, far_z]
            last.append(me.push(ref, ref, me.at_z(s), land))

    def take_columns():
        for w in last:
            w()
        for xx in range(4):
            r = pl.ds(xx * 512, 512)
            w_f[r, :] = wf2[xx].reshape(512, 256)
            for m in range(3):
                v = wq2[xx, m].reshape(512, 128)
                w_m[r, 64 * m : 64 * m + 64] = jnp.where(c == 0, v[:, 0:64], v[:, 64:128])

    here = small_all[x, y, c]
    b_in = jnp.concatenate([here[4:5, :], here[5:6, :]], axis=1)
    t = (x * 4 + y) * 2 + c
    b_m = jnp.concatenate([bq[pl.ds(t + 32 * m, 1), 0:64] for m in range(3)], axis=1)
    fi = me.new(16)

    def work(p, k):
        two = pl.ds(p * 2, 2)
        hidden, mixed = pairs.over(k, w_f, w_m)
        f_send[p, :, :, 0:192] = (mixed + b_m).astype(BF).reshape(2, 128, 192)
        f_send[p, :, :, 192:256] = jnp.zeros((2, 128, 64), BF)
        fields[p, zh] = f_send[p, zh]
        me.go(f_send.at[p, 1 - zh], fields.at[p, zh], fi + p, me.beyond)
        act, grad = gelu_both(hidden + b_in)
        active[two] = act.astype(BF).reshape(2, 128, 256)
        slope[two] = grad.astype(BF).reshape(2, 128, 256)

    pairs = Pairs(gather, buf, loc, work)

    def turn_cols():
        def one(i, _):
            r = pl.ds(pl.multiple_of(i * 256, 256), 256)
            cols_t[0:256, r] = w_f[r, :].astype(F32).T.astype(BF)
            cols_t[256:448, r] = w_m[r, :].astype(F32).T.astype(BF)
            return 0

        lax.fori_loop(0, 8, one, 0)

    events = gather.events() + [(4, round_z), (12.6, round_z_again), (21.1, take_columns), (30.1, turn_cols)]
    weave(events + pairs.events(0, 27.1), [])
    pairs.rest()
    for cp in near_rows():
        @pl.when(c == zh)
        def _():
            cp.wait()

    for cp in far_rows():
        @pl.when(c != zh)
        def _():
            cp.wait_recv()

    def came(p, _):
        me.came(fields.at[p, 1 - zh], fi + p)
        return 0

    lax.fori_loop(0, 16, came, 0)
    me.finish()
    for cp in far_rows():
        @pl.when(c == zh)
        def _():
            cp.wait_send()


def front(tok, small, w_qkv, w_in, w_out, w_back):
    return pl.pallas_call(
        front_kernel,
        out_shape=[
            arr(32, 128, WIDTH), arr(16, 2, 128, 256), arr(32, 128, 256), arr(32, 128, 256),
            arr(448, WIDTH), arr(320, WIDTH), arr(4, 4, 2, 8, 128, t=F32), arr(8, 128, t=F32),
        ],
        in_specs=[VM, VM, ANY, ANY, ANY, ANY],
        out_specs=[ANY] + [VM] * 7,
        scratch_shapes=[
            vmem(128, WIDTH), vmem(128, WIDTH, t=F32), vmem(4, 2, 128, WIDTH), vmem(16, 2, 128, 256), vmem(WIDTH, 256), vmem(WIDTH, 192),
            vmem(4, 4, 32, 256), vmem(4, 4, 3, 32, 128), vmem(4, 4, 4, 32, 256), vmem(4, 3, 4, 4, 32, 128),
            vmem(8, WIDTH, t=F32), vmem(96, 128, t=F32), DMA((180,)), DMA((180,)), DMA((5,)), DMA((18,)),
        ],
        compiler_params=pltpu.CompilerParams(
            collective_id=1, has_side_effects=True, vmem_limit_bytes=60 * 2**20
        ),
    )(tok, small, w_qkv, w_in, w_out, w_back)


def tile_at(i, j):
    return i * (i + 1) // 2 + j


def attend_kernel(
    order, inverse, fields, cos_ref, sin_ref, g_own, rows_w, slope,
    g_all, d_hidden, d_att, att, probs, q_n, v_n, k_t, o_t, scale,
    buf, d_send, a_send, w_ot, w_bt, k_n, q_t, v_t, s_buf, p_buf, send, recv, loc, psem,
):
    me = Here(send, recv)
    zh = me.zh
    me.greet(beyond=True)
    gather = Gather(me, g_own, g_all, loc.at[4])
    gather.begin()
    for ref in (d_send, a_send):
        ref[:, :, :, 64:128] = jnp.zeros((16, 2, 128, 64), BF)
    for ref in (q_n, v_n):
        ref[:, 64:128] = jnp.zeros((LENGTH, 64), BF)

    def turn_rows():
        def one(i, _):
            r = pl.ds(pl.multiple_of(i * 256, 256), 256)
            w_bt[r, :] = rows_w[0:256, r].astype(F32).T.astype(BF)
            w_ot[r, :] = rows_w[256:320, r].astype(F32).T.astype(BF)
            return 0

        lax.fori_loop(0, 8, one, 0)

    def load(begin):
        def one(i, _):
            here = pl.ds(pl.multiple_of(i * 128, 128), 128)
            t = pick(lambda p: fields[p], inverse[i]).astype(F32).T
            cos, sin = cos_ref[:, here], sin_ref[:, here]
            q = spin(t[0:64], cos, sin) * 0.125
            k = spin(t[64:128], cos, sin)
            v = t[128:192]
            q_t[:, here] = q.astype(BF)
            k_t[:, here] = k.astype(BF)
            v_t[:, here] = v.astype(BF)
            q_n[here, 0:64] = q.T.astype(BF)
            k_n[here, :] = k.T.astype(BF)
            v_n[here, 0:64] = v.T.astype(BF)
            return 0

        return lambda: lax.fori_loop(begin, begin + 8, one, 0)

    square = (TILE, TILE)
    allowed = lax.broadcasted_iota(jnp.int32, square, 0) <= lax.broadcasted_iota(jnp.int32, square, 1)
    tops = {}

    def scores(i):
        qs = pl.ds(i * TILE, TILE)
        qt = q_t[:, qs]

        def one(j, top):
            ks = pl.ds(pl.multiple_of(j * TILE, TILE), TILE)
            s = dot(k_n[ks, :], qt)
            s_buf[ks, :] = s
            return jnp.maximum(top, jnp.max(s, axis=0, keepdims=True))

        top = jnp.full((1, TILE), negative, F32)
        if i:
            top = lax.fori_loop(0, i, one, top)
        s = jnp.where(allowed, dot(k_n[qs, :], qt), negative)
        s_buf[qs, :] = s
        tops[i] = jnp.maximum(top, jnp.max(s, axis=0, keepdims=True))

    def out_copy(i, j):
        return pltpu.make_async_copy(p_buf.at[i % 2, j], probs.at[tile_at(i, j)], psem.at[i % 2, j])

    def values(i):
        qs = pl.ds(i * TILE, TILE)
        top = tops[i]
        if i >= 2:
            for j in range(i - 1):
                out_copy(i - 2, j).wait()

        def one(j, carry):
            total, o = carry
            ks = pl.ds(pl.multiple_of(j * TILE, TILE), TILE)
            p = jnp.exp(s_buf[ks, :] - top)
            pb = p.astype(BF)
            p_buf[i % 2, j] = pb
            return total + jnp.sum(p, axis=0, keepdims=True), o + dot(v_t[:, ks], pb)

        start = jnp.zeros((1, TILE), F32), jnp.zeros((64, TILE), F32)
        total, o = lax.fori_loop(0, i + 1, one, start)
        for j in range(i + 1):
            out_copy(i, j).start()
        inv = 1.0 / total
        o_t[:, qs] = o * inv
        scale[0:1, qs] = inv

    ai = me.new()

    def give():
        def one(b, _):
            o = pick(lambda p: o_t[:, 128 * p : 128 * p + 128], order[b])
            a_send[b // 2, lax.rem(b, 2), :, 0:64] = o.T.astype(BF)
            return 0

        lax.fori_loop(0, 32, one, 0)
        att[:, zh] = a_send[:, zh]
        me.go(a_send.at[:, 1 - zh], att.at[:, zh], ai, me.beyond)

    di = me.new(16)

    def work(p, k):
        two = pl.ds(p * 2, 2)
        da, do = pairs.over(k, w_bt, w_ot)
        d_send[p, :, :, 0:64] = do.astype(BF).reshape(2, 128, 64)
        d_att[p, zh] = d_send[p, zh]
        me.go(d_send.at[p, 1 - zh], d_att.at[p, zh], di + p, me.beyond)
        d_hidden[two] = (da * slope[two].reshape(256, 256).astype(F32)).astype(BF).reshape(2, 128, 256)

    pairs = Pairs(gather, buf, loc, work)

    side = [(1.5, turn_rows)] + [(0.8, load(8 * k)) for k in range(4)]
    for i in range(STRIPS):
        side += [(0.25 * (i + 1), lambda i=i: scores(i)), (0.3 * (i + 1), lambda i=i: values(i))]
    side.append((2.0, give))
    weave(gather.events() + pairs.events(0, 5.0), side)
    pairs.rest()
    for i in (STRIPS - 2, STRIPS - 1):
        for j in range(i + 1):
            out_copy(i, j).wait()
    me.came(att.at[:, 1 - zh], ai)

    def came(p, _):
        me.came(d_att.at[p, 1 - zh], di + p)
        return 0

    lax.fori_loop(0, 16, came, 0)
    me.finish()


def attend(order, inverse, fields, cos, sin, g_own, rows_w, slope):
    return pl.pallas_call(
        attend_kernel,
        out_shape=[
            arr(32, 128, WIDTH), arr(32, 128, 256), arr(16, 2, 128, 128), arr(16, 2, 128, 128),
            arr(tile_at(STRIPS, 0), TILE, TILE), arr(LENGTH, 128), arr(LENGTH, 128), arr(64, LENGTH),
            arr(64, LENGTH, t=F32), arr(8, LENGTH, t=F32),
        ],
        in_specs=[SM, SM, VM, VM, VM, VM, VM, VM],
        out_specs=[ANY, VM, VM, VM, ANY] + [VM] * 5,
        scratch_shapes=[
            vmem(4, 2, 128, WIDTH), vmem(16, 2, 128, 128), vmem(16, 2, 128, 128), vmem(WIDTH, 64), vmem(WIDTH, 256),
            vmem(LENGTH, 64), vmem(64, LENGTH), vmem(64, LENGTH), vmem(LENGTH, TILE, t=F32),
            vmem(2, STRIPS, TILE, TILE), DMA((100,)), DMA((100,)), DMA((5,)), DMA((2, STRIPS)),
        ],
        compiler_params=pltpu.CompilerParams(
            collective_id=2, has_side_effects=True, vmem_limit_bytes=60 * 2**20
        ),
    )(order, inverse, fields, cos, sin, g_own, rows_w, slope)


class Outer:
    def __init__(self, src, lhs, height, put, turned, buf, loc, sums=None):
        self.src, self.lhs, self.height, self.put = src, lhs, height, put
        self.turned, self.buf, self.loc, self.sums = turned, buf, loc, sums

    def load(self, t, k):
        cs = pl.ds(pl.multiple_of(t * 256, 256), 256)
        return pltpu.make_async_copy(self.src.at[:, :, cs], self.buf.at[k], self.loc.at[k])

    def prepare(self):
        self.load(0, 0).start()

        def one(p, _):
            v = self.lhs(p).astype(F32)
            if self.sums is not None:
                self.sums[0:1, 0 : self.height] += jnp.sum(v, axis=0, keepdims=True)
            self.turned[0 : self.height, pl.ds(pl.multiple_of(p * 256, 256), 256)] = v.T.astype(BF)
            return 0

        lax.fori_loop(0, 16, one, 0)

    def part(self, begin, end):
        def one(t, _):
            k = lax.rem(t, 2)

            @pl.when(t + 1 < 8)
            def _():
                self.load(t + 1, 1 - k).start()

            self.load(t, k).wait()
            v = dot(self.turned[0 : self.height, :], self.buf[k].reshape(LENGTH, 256))
            self.put(pl.ds(pl.multiple_of(t * 256, 256), 256), v)
            return 0

        lax.fori_loop(begin, end, one, 0)

    def parts(self, n):
        todo = [self.prepare]
        return todo + [lambda i=i: self.part(8 * i // n, 8 * (i + 1) // n) for i in range(n)]


def two_blocks(ref):
    return lambda p: ref[pl.ds(2 * p, 2)].reshape(256, ref.shape[-1])


def turn_kernel(
    order, inverse, d_att, att, active, rows_w, o_t, scale, q_n, v_n, k_t, cos_ref, sin_ref, d_hidden,
    probs, n_all,
    branch, dm, g_cols, sums,
    do_t, p_buf, dk, dv, dq, d_pos, m_send, turned, buf, lhs, psend, acc, far, near, send, recv, loc, psem,
):
    me = Here(send, recv)
    zh = me.zh
    me.greet(beyond=True)

    def operands(p, core):
        return active[2 * p + core], att[p, core][:, 0:64]

    total = Total(me, operands, rows_w, branch, lhs, psend, acc, far, near)
    d_pos[:, :, 192:256] = jnp.zeros((32, 128, 64), BF)
    dk[...] = jnp.zeros_like(dk)
    dv[...] = jnp.zeros_like(dv)
    sums[...] = jnp.zeros_like(sums)

    def load():
        def one(i, _):
            here = pl.ds(pl.multiple_of(i * 128, 128), 128)
            do_t[:, here] = pick(lambda p: d_att[p], inverse[i]).astype(F32).T[0:64]
            return 0

        lax.fori_loop(0, 32, one, 0)

    order_of = [(i, j) for i in range(STRIPS) for j in range(i + 1)]

    def in_copy(n):
        return pltpu.make_async_copy(probs.at[n], p_buf.at[lax.rem(n, 4)], psem.at[lax.rem(n, 4)])

    state = {}

    def strip(i):
        qs = pl.ds(i * TILE, TILE)
        inv = scale[0:1, qs]
        do = do_t[:, qs] * inv
        delta = jnp.sum(do * o_t[:, qs], axis=0, keepdims=True)
        dt = do.astype(BF)
        dn = do.T.astype(BF)
        qn = q_n[qs, 0:64]
        base = tile_at(i, 0)

        def one(j, dq_t):
            n = base + j

            @pl.when(n + 3 < len(order_of))
            def _():
                in_copy(n + 3).start()

            in_copy(n).wait()
            ks = pl.ds(pl.multiple_of(j * TILE, TILE), TILE)
            dp = dot(v_n[ks, 0:64], dt)
            pb = p_buf[lax.rem(n, 4)]
            ds = (pb.astype(F32) * (dp - delta)).astype(BF)
            dk[ks, :] += dot(ds, qn)
            dv[ks, :] += dot(pb, dn)
            return dq_t + dot(k_t[:, ks], ds)

        def piece(begin, end):
            def run():
                start = state.get(i, jnp.zeros((64, TILE), F32))
                state[i] = lax.fori_loop(begin, end, one, start)

            return run

        def last():
            dq[:, qs] = spin(state[i], cos_ref[:, qs], -sin_ref[:, qs]) * 0.125

        return piece, last

    mi = me.new()

    def give():
        def one(i, _):
            here = pl.ds(pl.multiple_of(i * 128, 128), 128)
            k = spin(dk[here, :].T, cos_ref[:, here], -sin_ref[:, here])
            t = jnp.concatenate([dq[:, here], k, dv[here, :].T], axis=0)
            d_pos[i, :, 0:192] = t.T.astype(BF)
            return 0

        lax.fori_loop(0, 32, one, 0)

        def two(b, _):
            m_send[b // 2, lax.rem(b, 2)] = pick(lambda p: d_pos[p], order[b])
            return 0

        lax.fori_loop(0, 32, two, 0)
        dm[:, zh] = m_send[:, zh]
        me.go(m_send.at[:, 1 - zh], dm.at[:, zh], mi, me.beyond)

    side = [(2.0, load)]
    for i in range(STRIPS):

        def make(i=i):
            piece, last = strip(i)
            cuts = [0, i + 1] if i < 4 else [0, (i + 1) // 2, i + 1]
            for a, b in zip(cuts, cuts[1:]):
                yield piece(a, b)
            yield last

        holder = {}

        def begin(i=i, holder=holder, make=make):
            holder["todo"] = list(make())
            holder["todo"].pop(0)()

        def again(holder=holder):
            holder["todo"].pop(0)()

        more = 1 if i < 4 else 2
        side += [(0.8 * (i + 1) / more, begin)] + [(0.8 * (i + 1) / more, again)] * (more - 1) + [(0.2, again)]
    side.append((2.5, give))

    for n in range(3):
        in_copy(n).start()

    def put(r, v):
        g_cols[r, :] = v.T.astype(BF)

    outer = Outer(n_all, two_blocks(d_hidden), 256, put, turned, buf, loc, sums).parts(4)
    side += [(2.0, f) for f in outer]
    for f in total.products():
        f()
    weave(total.events(), side, 14.0)
    me.came(dm.at[:, 1 - zh], mi)
    total.finish()
    me.finish()


def turn(order, inverse, d_att, att, active, rows_w, o_t, scale, q_n, v_n, k_t, cos, sin, d_hidden, probs, n_all):
    return pl.pallas_call(
        turn_kernel,
        out_shape=[
            arr(128, WIDTH, t=F32), arr(16, 2, 128, 256), arr(WIDTH, 256), arr(8, 256, t=F32),
        ],
        in_specs=[SM, SM] + [VM] * 12 + [ANY] * 2,
        out_specs=[VM] * 4,
        scratch_shapes=[
            vmem(64, LENGTH, t=F32), vmem(4, TILE, TILE), vmem(LENGTH, 64, t=F32), vmem(LENGTH, 64, t=F32),
            vmem(64, LENGTH, t=F32), vmem(32, 128, 256), vmem(16, 2, 128, 256), vmem(256, LENGTH), vmem(2, 32, 128, 256), vmem(512, 320),
            *SUM_SCRATCH, DMA((60,)), DMA((60,)), DMA((2,)), DMA((4,)),
        ],
        compiler_params=pltpu.CompilerParams(
            collective_id=3, has_side_effects=True, vmem_limit_bytes=62 * 2**20
        ),
    )(order, inverse, d_att, att, active, rows_w, o_t, scale, q_n, v_n, k_t, cos, sin, d_hidden, probs, n_all)


class Columns:
    def __init__(self, me, cols, out, far, near, mine, total, a1):
        self.me, self.cols, self.out = me, cols, out
        self.far, self.near, self.mine, self.total, self.a1 = far, near, mine, total, a1
        self.parts = ((1, pl.ds(0, 8)), (-1, pl.ds(8, 8)))

    def start(self):
        me, zf = self.me, wrap(self.me.z + 2)
        self.waits = [
            me.push(self.cols.at[p, zf], self.far.at[r], me.at_z(s), self.far.at[r])
            for r, (s, p) in enumerate(self.parts)
        ]
        return [(6.0, self.second)]

    def second(self):
        me, mine, old = self.me, self.mine, self.waits
        self.waits = []
        for r, (s, p) in enumerate(self.parts):
            old[r]()
            mine[r] = self.cols[:, wrap(me.z + s)]
            mine[r, p] = (mine[r, p].astype(F32) + self.far[r].astype(F32)).astype(BF)
            self.waits.append(me.push(mine.at[r], self.near.at[r], me.at_z(s), self.near.at[r]))
        return [(8.0, self.third)]

    def third(self):
        me, total, a1 = self.me, self.total, self.a1
        for w in self.waits:
            w()
        v = self.cols[:, me.z].astype(F32) + self.near[0].astype(F32) + self.near[1].astype(F32)
        total[...] = v.astype(BF).reshape(total.shape)
        a1[me.x] = total[me.x]
        self.waits = [
            me.push(total.at[wrap(me.x + d)], a1.at[me.x], me.at(d, 0), a1.at[wrap(me.x - d)])
            for d in (1, -1, 2)
        ]
        return [(5.0, self.fourth)]

    def fourth(self):
        me, a1, here = self.me, self.a1, self.out.at[self.me.c, self.me.zl]
        for w in self.waits:
            w()
        self.out[me.c, me.zl, :, me.y] = a1[:, me.y]
        self.waits = [
            me.push(a1.at[:, wrap(me.y + d)], here.at[:, me.y], me.at(0, d), here.at[:, wrap(me.y - d)])
            for d in (1, -1, 2)
        ]
        return [(5.0, self.fifth)]

    def fifth(self):
        me, out = self.me, self.out
        for w in self.waits:
            w()
        block = out.at[me.c, me.zl]
        self.core = [me.push(block, block, me.other, out.at[1 - me.c, me.zl])]
        self.waits = [me.push(block, block, me.twin, out.at[me.c, 1 - me.zl])]
        return [(7.0, self.sixth)]

    def sixth(self):
        me, out = self.me, self.out
        self.waits[0]()
        block = out.at[me.c, 1 - me.zl]
        self.core.append(me.push(block, block, me.other, out.at[1 - me.c, 1 - me.zl]))

    def finish(self):
        for w in self.core:
            w()


class Rows:
    def __init__(self, me, rws, out, far, mid):
        self.me, self.rws, self.out, self.far, self.mid = me, rws, out, far, mid
        self.halves = (pl.ds(0, 160), pl.ds(160, 160))
        self.sem = me.new(6)

    def early(self, to):
        return [
            self.me.copy(self.rws.at[h], self.far.at[k], self.sem + k, to) for k, h in enumerate(self.halves)
        ]

    def across(self, to):
        return self.me.copy(self.mid.at[0], self.mid.at[1], self.sem + 2, to)

    def give(self, h, i, to):
        return self.me.copy(self.out.at[h], self.out.at[h], self.sem + i, to)

    def cases(self, keeps):
        me = self.me
        up, down = me.at_z(1), me.at_z(-1)
        for flag in (0, 1):
            if keeps:
                yield (me.c == me.zh) & (me.zl == flag), flag, (up, down)[flag]
            else:
                yield (me.c != me.zh) & (me.zl == flag), flag, (down, up)[flag]

    def start(self):
        for test, _, to in self.cases(False):

            @pl.when(test)
            def _():
                for cp in self.early(to):
                    cp.start()

        return [(15.0, self.second)]

    def second(self):
        for test, flag, to in self.cases(True):

            @pl.when(test)
            def _():
                for cp in self.early(to):
                    cp.wait_recv()
                k = 1 - flag
                self.mid[0] = (self.rws[self.halves[k]].astype(F32) + self.far[k].astype(F32)).astype(BF)
                self.across(to).start()

        return [(8.0, self.third)]

    def third(self):
        for test, flag, to in self.cases(True):

            @pl.when(test)
            def _():
                h = self.halves[flag]
                self.across(to).wait()
                v = self.rws[h].astype(F32) + self.far[flag].astype(F32) + self.mid[1].astype(F32)
                self.out[h] = v.astype(BF)
                self.give(h, 3, to).start()
                self.give(h, 4, self.me.other).start()

        return [(8.0, self.fourth)]

    def fourth(self):
        for test, flag, to in self.cases(True):

            @pl.when(test)
            def _():
                h, g = self.halves[flag], self.halves[1 - flag]
                self.give(g, 3, to).wait_recv()
                self.give(g, 5, self.me.other).start()
                self.give(h, 3, to).wait_send()
                self.give(h, 4, self.me.other).wait_send()
                self.give(g, 5, self.me.other).wait_send()

        for test, flag, to in self.cases(False):

            @pl.when(test)
            def _():
                h, g = self.halves[flag], self.halves[1 - flag]
                for cp in self.early(to):
                    cp.wait_send()
                self.give(h, 4, self.me.other).wait_recv()
                self.give(g, 5, self.me.other).wait_recv()


class Vectors:
    def __init__(self, me, own, out, vp, vx, vy, vq, vz, vr):
        self.me, self.own, self.out = me, own, out
        self.vp, self.vx, self.vy, self.vq, self.vz, self.vr = vp, vx, vy, vq, vz, vr

    def done(self):
        for w in self.waits:
            w()

    def start(self):
        self.waits = [self.me.push(self.own, self.vp, self.me.other, self.vp)]
        return [(1.5, self.along_x)]

    def along_x(self):
        me = self.me
        self.done()
        self.vp[...] = self.vp[...] + self.own[...]
        self.waits = [
            me.push(self.vp.at[wrap(me.x + d)], self.vx.at[k], me.at(d, 0), self.vx.at[k])
            for k, d in enumerate((1, -1, 2))
        ]
        return [(2.0, self.along_y)]

    def along_y(self):
        me = self.me
        self.done()
        self.vy[...] = self.vp[me.x] + self.vx[0] + self.vx[1] + self.vx[2]
        self.waits = [
            me.push(self.vy.at[wrap(me.y + d)], self.vq.at[k], me.at(0, d), self.vq.at[k])
            for k, d in enumerate((1, -1, 2))
        ]
        return [(2.0, self.along_z)]

    def along_z(self):
        me = self.me
        self.done()
        self.vz[...] = self.vy[me.y] + self.vq[0] + self.vq[1] + self.vq[2]
        self.waits = [
            me.push(self.vz, self.vr.at[k], me.at_z(d), self.vr.at[k]) for k, d in enumerate((1, -1, 2))
        ]

    def finish(self):
        self.done()
        self.out[...] = self.vz[...] + self.vr[0] + self.vr[1] + self.vr[2]


def back_kernel(
    dm, d_hidden, cols_t, active, att, cols_in, sums_in, tok, g_own, gain, n_all, g_all,
    d_tok, out_in, out_m, out_rows, out_vec,
    d_normed, cols_m, rws, sums, line, vec, turned, turned_r, buf, lhs, psend, acc, far, near,
    c_far, c_near, c_mine, c_total, c_a1, r_far, r_mid, vp, vx, vy, vq, vz, vr, send, recv, loc,
):
    me = Here(send, recv)
    me.greet(True, True, True)

    def operands(p, core):
        return d_hidden[2 * p + core], dm[p, core][:, 0:192]

    total = Total(me, operands, cols_t, d_normed, lhs, psend, acc, far, near)
    strips = [
        Columns(me, ref, out, c_far.at[i], c_near.at[i], c_mine.at[i], c_total.at[i], c_a1.at[i])
        for i, (ref, out) in enumerate(((cols_in, out_in), (cols_m, out_m)))
    ]
    rows = Rows(me, rws, out_rows, r_far, r_mid)
    vectors = Vectors(me, vec, out_vec, vp, vx, vy, vq, vz, vr)
    strips[0].start()
    sums[...] = jnp.zeros_like(sums)
    line[...] = jnp.zeros_like(line)
    vec[...] = jnp.zeros_like(vec)

    def put(r, v):
        flat = v.T.astype(BF)
        q = r.start // 128
        for k in (0, 1):
            cols_m[q + k, :, :, 0:192] = flat[128 * k : 128 * k + 128].reshape(4, 32, 192)
            cols_m[q + k, :, :, 192:256] = jnp.zeros((4, 32, 64), BF)

    def put_r(r, v):
        rws[:, r] = v.astype(BF)

    def left(p):
        return jnp.concatenate([two_blocks(active)(p), att[p].reshape(256, 128)[:, 0:64]], axis=1)

    def norm_back():
        def one(i, _):
            r = pl.ds(pl.multiple_of(i * 32, 32), 32)
            v, g, d = tok[r, :].astype(F32), g_own[r, :].astype(F32), d_normed[r, :]
            v = v - jnp.mean(v, axis=-1, keepdims=True)
            s = lax.rsqrt(jnp.mean(v * v, axis=-1, keepdims=True) + eps_norm)
            hat = v * s
            e = d * gain[...]
            e = e - jnp.mean(e, axis=-1, keepdims=True) - hat * jnp.mean(e * hat, axis=-1, keepdims=True)
            d_tok[r, :] = (g + s * e).astype(BF)
            line[0:1, :] += jnp.sum(d * hat, axis=0, keepdims=True)
            line[1:2, :] += jnp.sum(d, axis=0, keepdims=True)
            line[2:3, :] += jnp.sum(g, axis=0, keepdims=True)
            return 0

        lax.fori_loop(0, 4, one, 0)
        for j in range(32):
            q, base = vec.at[j // 8, (j // 2) % 4], 8 * (j % 2)
            ls = pl.ds(64 * j, 64)
            q[base : base + 1, 0:64] = line[0:1, ls]
            q[base : base + 1, 64:128] = line[1:2, ls]
            q[base + 1 : base + 2, 0:64] = line[2:3, ls]
        t = (me.x * 4 + me.y) * 2 + me.c
        for k in (0, 1):
            vec[me.x, me.y, pl.ds(8 * me.c + 3 + k, 1), :] = sums_in[0:1, 128 * k : 128 * k + 128]
        for m in range(3):
            f = t + 32 * m
            j = f // 3
            v = sums[0:1, 64 * m : 64 * m + 64]
            for i, (row, lane) in enumerate(((1, 64), (2, 0), (2, 64))):

                @pl.when(f % 3 == i)
                def _():
                    vec[j // 8, (j // 2) % 4, pl.ds(8 * (j % 2) + row, 1), lane : lane + 64] = v

        return [(0.0, vectors.start)]

    units = Outer(g_all, left, 320, put_r, turned_r, buf, loc).parts(4) + [rows.start]
    units += Outer(n_all, lambda p: dm[p].reshape(256, 256)[:, 0:192], 192, put, turned, buf, loc, sums).parts(4)
    units += [strips[1].start]
    for f in total.products():
        f()
    events = total.events() + [(14.0, strips[0].second), (52.5, norm_back)]
    weave(events, [(2.0, f) for f in units], 14.0)
    vectors.finish()
    for s in strips:
        s.finish()
    total.finish()
    me.finish()


def back(*operands):
    wide = [vmem(2, 2, 8, 32, 256), vmem(2, 2, 16, 32, 256), vmem(2, 2, 16, 32, 256)]
    return pl.pallas_call(
        back_kernel,
        out_shape=[
            arr(128, WIDTH), arr(2, 2, 4, 4, 32, 256), arr(2, 2, 4, 4, 32, 256), arr(320, WIDTH),
            arr(16, 128, t=F32),
        ],
        in_specs=[VM] * 10 + [ANY] * 2,
        out_specs=[VM] * 5,
        scratch_shapes=[
            vmem(128, WIDTH, t=F32), vmem(16, 4, 32, 256), vmem(320, WIDTH), vmem(8, 192, t=F32),
            vmem(8, WIDTH, t=F32), vmem(4, 4, 16, 128, t=F32), vmem(192, LENGTH), vmem(320, LENGTH),
            vmem(2, 32, 128, 256), vmem(512, 448), *SUM_SCRATCH,
            *wide, vmem(2, 4, 4, 32, 256), vmem(2, 4, 4, 32, 256), vmem(2, 160, WIDTH), vmem(2, 160, WIDTH),
            vmem(4, 4, 16, 128, t=F32), vmem(3, 4, 16, 128, t=F32), vmem(4, 16, 128, t=F32),
            vmem(3, 16, 128, t=F32), vmem(16, 128, t=F32), vmem(3, 16, 128, t=F32),
            DMA((110,)), DMA((110,)), DMA((2,)),
        ],
        compiler_params=pltpu.CompilerParams(
            collective_id=4, has_side_effects=True, vmem_limit_bytes=62 * 2**20
        ),
    )(*operands)


def finish_kernel(cols_in, cols_m, rws, g_qkv, g_in, g_out, g_back):
    g_back[...] = rws[0:256].astype(F32)
    g_out[...] = rws[256:320].astype(F32)

    def one(p, _):
        for h in (0, 1):
            r = pl.ds(32 * h, 32)
            g_in[r, pl.ds(pl.multiple_of(p * 512, 512), 256)] = cols_in[0, h, p].astype(F32)
            g_in[r, pl.ds(pl.multiple_of(p * 512 + 256, 256), 256)] = cols_in[1, h, p].astype(F32)
            a, b = cols_m[0, h, p].astype(F32), cols_m[1, h, p].astype(F32)
            for m in range(3):
                k = 64 * m
                both = jnp.concatenate([a[:, k : k + 64], b[:, k : k + 64]], axis=1)
                g_qkv[r, pl.ds(pl.multiple_of(m * WIDTH + p * 128, 128), 128)] = both
        return 0

    lax.fori_loop(0, 16, one, 0)


def finish(cols_in, cols_m, rws):
    return pl.pallas_call(
        finish_kernel,
        out_shape=[arr(64, 6144, t=F32), arr(64, 8192, t=F32), arr(64, WIDTH, t=F32), arr(256, WIDTH, t=F32)],
        in_specs=[VM] * 3,
        out_specs=[VM] * 4,
        compiler_params=pltpu.CompilerParams(vmem_limit_bytes=60 * 2**20),
    )(cols_in, cols_m, rws)


def body(
    tokens,
    span_order,
    ln_gain,
    ln_bias,
    qkv_weight,
    qkv_bias,
    out_weight,
    out_bias,
    fc1_weight,
    fc1_bias,
    fc2_weight,
    fc2_bias,
    cotangent,
):
    x, y, zh, zl, c = place()

    tok = tokens.reshape(128, WIDTH)
    g_own = cotangent.reshape(128, WIDTH)
    own = [ln_gain, ln_bias, out_bias, fc2_bias, qkv_bias, jnp.zeros((64,), BF), fc1_bias]
    own = [v.astype(F32) for v in own] + [span_order.reshape(32).astype(F32), jnp.zeros((224,), F32)]
    small = jnp.concatenate(own).reshape(8, 128)
    n_all, fields, active, slope, cols_t, rows_w, small_all, small_other = front(
        tok, small, qkv_weight, fc1_weight, out_weight, fc2_weight
    )
    small_all = small_all.reshape(32, 8, 128)
    gain = small_all[:, 0, :64].reshape(WIDTH)
    b_sum = (small_all[:, 1, :64] + small_all[:, 1, 64:]).reshape(WIDTH)
    order = jnp.where(c == zh, span_order.reshape(32), small_other[6, :32].astype(jnp.int32))

    blocks = jnp.arange(32, dtype=jnp.int32)
    inverse = jnp.sum(jnp.where(order[None, :] == blocks[:, None], blocks[None, :], 0), axis=1)
    freq = rope_base ** (-np.arange(16) * 2.0 / 32)
    angle = np.arange(LENGTH)[None, :] * freq[:, None]
    cos, sin = jnp.asarray(np.cos(angle), F32), jnp.asarray(np.sin(angle), F32)
    g_all, d_hidden, d_att, att, probs, q_n, v_n, k_t, o_t, scale = attend(
        order, inverse, fields.reshape(32, 128, 256), cos, sin, g_own, rows_w, slope
    )
    branch, dm, g_cols_in, sums_in = turn(
        order, inverse, d_att.reshape(32, 128, 128), att, active, rows_w, o_t, scale, q_n, v_n, k_t, cos, sin,
        d_hidden, probs, n_all,
    )
    d_tokens, cols_in, cols_m, rws, vec = back(
        dm, d_hidden, cols_t, active, att, g_cols_in.reshape(16, 4, 32, 256), sums_in, tok, g_own,
        gain.reshape(1, WIDTH), n_all, g_all,
    )
    d_tokens = d_tokens.reshape(1, 128, WIDTH)
    block_out = (tok.astype(F32) + branch + b_sum).astype(BF).reshape(1, 128, WIDTH)
    g_qkv, g_in, g_out, g_back = finish(
        cols_in.reshape(2, 2, 16, 32, 256), cols_m.reshape(2, 2, 16, 32, 256), rws
    )
    vec = lax.dynamic_index_in_dim(vec.reshape(2, 1024), zh, 0, keepdims=False)
    return (
        block_out,
        d_tokens,
        vec[:64],
        vec[64:128],
        g_qkv,
        vec[192:384],
        g_out,
        vec[128:192],
        g_in,
        vec[384:640],
        g_back,
        vec[128:192],
    )


def solution(mesh):
    act, rows, vec = P("rep", "shard", None), P("shard", None), P("shard")
    return jax.shard_map(
        body,
        mesh=mesh,
        in_specs=(act, P("rep", None), vec, vec, rows, vec, rows, vec, rows, vec, rows, vec, act),
        out_specs=(act, act, vec, vec, rows, vec, rows, vec, rows, vec, rows, vec),
        check_vma=False,
    )
```
